256 devices in a mesh: gx: 8 (over y, core), gy: 4 (over x), gz: 8 (over z).
Axes of the slice: x: 4, y: 4, z: 8, core: 2. Of those that a mesh axis runs over, the one named last changes fastest.
Arguments:
- right_side: float32 [128, 128, 512], P('gx', 'gz', 'gy'), may hold values from -8 to 8
- sigma: float32 [128, 128, 512], P('gx', 'gz', 'gy'), may hold values from 0.25 to 4
Outputs:
- solution_field: float32 [128, 128, 512], P('gx', 'gz', 'gy')
- residual: float32 [128, 128, 512], P('gx', 'gz', 'gy')
The draws below stay inside these ranges and needn't reach their ends.
All inputs are finite; a program needn't handle non-finite values.
Results may differ from the reference program's by a relative error of at most 0.0003.
Values sent between devices are 32-bit elements; how exact they have to be, the bound alone decides.
No kernel may reach another device: no remote copies, remote signals or barrier semaphores. Data moves between devices by JAX's collectives and lax.ppermute only.
A program may use at most 128 MiB of HBM per device.

```python
import math
import jax
import jax.numpy as jnp

NU = 2
BOTTOM = 8
NX = 128
NZ = 128
NY = 512


def draw_right_side(key, part):
    key = jax.random.fold_in(key, 11)
    shape = (NX, NZ, NY)
    return jnp.clip(jax.random.normal(key, shape, jnp.float32), -6.0, 6.0)


def steps_of(own_key, shape, pieces, low, largest):
    level, own = 1.0, jax.random.fold_in(own_key, 6)
    for position, blocks in pieces:
        draws = jnp.exp(jax.random.uniform(jax.random.fold_in(own, position), (blocks,), jnp.float32, low / len(pieces), largest / len(pieces)))
        level = level * jnp.repeat(draws, shape[position] // blocks).reshape([-1 if axis == position else 1 for axis in range(len(shape))])
    return level


def setup_inputs(seed: int = 0) -> dict:
    streams_of = jax.random.split(jax.random.key(seed), 3)
    return {
        "right_side": draw_right_side(jax.random.fold_in(streams_of[2], 71), 0),
        "sigma": jnp.clip(jnp.exp(math.log(4.0) - 2.7725887 * jax.random.uniform(streams_of[1], (NX, NZ, NY), jnp.float32) ** steps_of(streams_of[1], (NX, NZ, NY), ((0, 8), (1, 8), (2, 4)), -0.2, 0.2)), 0.25, 4.0),
    }


def six_sides(padded):
    return [padded[2:, 1:-1, 1:-1], padded[:-2, 1:-1, 1:-1],
            padded[1:-1, 2:, 1:-1], padded[1:-1, :-2, 1:-1],
            padded[1:-1, 1:-1, 2:], padded[1:-1, 1:-1, :-2]]


def couple(value_p, sigma_p):
    centre = sigma_p[1:-1, 1:-1, 1:-1]
    weight_sum = jnp.zeros(centre.shape, jnp.float32)
    pulled = jnp.zeros(centre.shape, jnp.float32)
    for near_sigma, near_value in zip(six_sides(sigma_p), six_sides(value_p)):
        beta = 0.5 * (centre + near_sigma)
        weight_sum = weight_sum + beta
        pulled = pulled + beta * near_value
    return weight_sum, pulled


def colouring(shape):
    first = jnp.arange(shape[0])[:, None, None]
    second = jnp.arange(shape[1])[None, :, None]
    third = jnp.arange(shape[2])[None, None, :]
    return (first + second + third) % 2 == 0


def smooth(phi, sigma_p, rhs, scale, sweeps):
    red = colouring(phi.shape)
    for sweep in range(sweeps):
        for colour in (red, jnp.logical_not(red)):
            weight_sum, pulled = couple(jnp.pad(phi, 1), sigma_p)
            phi = jnp.where(colour, (rhs * scale + pulled) / weight_sum, phi)
    return phi


def residual_of(phi, sigma_p, rhs, scale):
    weight_sum, pulled = couple(jnp.pad(phi, 1), sigma_p)
    return rhs - (weight_sum * phi - pulled) / scale


def restrict(field):
    a, b, c = field.shape
    return field.reshape(a // 2, 2, b // 2, 2, c // 2, 2).mean(axis=(1, 3, 5))


def prolong(field):
    return jnp.repeat(jnp.repeat(jnp.repeat(field, 2, axis=0), 2, axis=1), 2, axis=2)


def reference(right_side, sigma):
    sigmas = [sigma]
    for level in range(4):
        sigmas.append(restrict(sigmas[-1]))
    padded = [jnp.pad(s, 1) for s in sigmas]
    kept = []
    rhs_now = right_side
    for level in range(4):
        scale = 4.0 ** level
        phi = smooth(jnp.zeros_like(rhs_now), padded[level], rhs_now, scale, NU)
        kept.append((phi, rhs_now))
        rhs_now = restrict(residual_of(phi, padded[level], rhs_now, scale))
    correction = smooth(jnp.zeros_like(rhs_now), padded[4], rhs_now, 4.0 ** 4, BOTTOM)
    for level in (3, 2, 1, 0):
        phi, rhs_level = kept[level]
        correction = smooth(phi + prolong(correction), padded[level], rhs_level, 4.0 ** level, NU)
    residual = residual_of(correction, padded[0], right_side, 1.0)
    return correction, residual
```

```python
import functools

import jax
import jax.numpy as jnp
from jax import lax
from jax.experimental import pallas as pl
from jax.experimental.pallas import tpu as pltpu
from jax.sharding import PartitionSpec as P

NU = 2
BOTTOM = 8
F32 = jnp.float32
LANES = 128
STRIP = 8
PER = LANES // STRIP

H0, X0, Z0 = 5, 26, 32
H1, X1, Z1 = 7, 22, 24


def roll(v, shift, axis):
    return pltpu.roll(v, shift % v.shape[axis], axis)


def iota(shape, axis):
    return lax.broadcasted_iota(jnp.int32, shape, axis)


def exact_dot(a, b):
    return jnp.dot(a, b, precision=lax.Precision.HIGHEST, preferred_element_type=F32)


def halving(width):
    k, l = iota((width, LANES), 0), iota((width, LANES), 1)
    return jnp.where(k // 2 == l, 0.125, 0.0).astype(F32)


def doubling(width):
    k, l = iota((LANES, width), 0), iota((LANES, width), 1)
    return jnp.where(l // 2 == k, 1.0, 0.0).astype(F32)


def reds(shape, parity):
    return (iota(shape, 0) + iota(shape, 1)) % 2 == parity % 2


def couplings(s_ref, f_ref, c_ref, g_ref, w_ref, first, last, scale, so=0, fo=0, edges=False):
    shape = s_ref.shape[1:]
    if edges:
        z, y = iota(shape, 0), iota(shape, 1)
        walls = (None, None, z == shape[0] - 1, z == 0, y == shape[1] - 1, y == 0)

    def body(x, carry):
        centre = s_ref[x + so]
        near = [
            s_ref[x + so + 1],
            s_ref[x + so - 1],
            roll(centre, -1, 0),
            roll(centre, 1, 0),
            roll(centre, -1, 1),
            roll(centre, 1, 1),
        ]
        if edges:
            near = [v if wall is None else jnp.where(wall, 0.0, v) for v, wall in zip(near, walls)]
        betas = [0.5 * (centre + v) for v in near]
        total = ((betas[0] + betas[1]) + (betas[2] + betas[3])) + (betas[4] + betas[5])
        inverse = jnp.where(centre > 0.0, 1.0 / total, 0.0)
        for d in range(6):
            c = betas[d] * inverse
            if edges and walls[d] is not None:
                c = jnp.where(walls[d], 0.0, c)
            c_ref[d, x] = c
        g_ref[x] = f_ref[x + fo] * (inverse * scale)
        w_ref[x] = total * (1.0 / scale)
        return carry

    lax.fori_loop(first, last, body, 0)


def relaxed(u, c_ref, g_ref, x):
    low, centre, high = u
    a = c_ref[0, x] * high + c_ref[1, x] * low
    b = c_ref[2, x] * roll(centre, -1, 0) + c_ref[3, x] * roll(centre, 1, 0)
    d = c_ref[4, x] * roll(centre, -1, 1) + c_ref[5, x] * roll(centre, 1, 1)
    return g_ref[x] + ((a + b) + d)


def half_sweep(u_ref, c_ref, g_ref, first, last, parity, uo=0):
    shape = u_ref.shape[1:]

    def body(i, carry):
        x = first + 2 * i
        masks = (reds(shape, parity + first), reds(shape, parity + first + 1))
        u = [u_ref[x + uo + k] for k in (-1, 0, 1, 2)]
        u_ref[x + uo] = jnp.where(masks[0], relaxed(u[0:3], c_ref, g_ref, x), u[1])
        u_ref[x + uo + 1] = jnp.where(masks[1], relaxed(u[1:4], c_ref, g_ref, x + 1), u[2])
        return carry

    lax.fori_loop(0, (last - first) // 2, body, 0)


def first_half_sweep(u_ref, g_ref, first, last, parity, uo=0):
    shape = u_ref.shape[1:]

    def body(i, carry):
        x = first + 2 * i
        for k in range(2):
            u_ref[x + uo + k] = jnp.where(reds(shape, parity + first + k), g_ref[x + k], 0.0)
        return carry

    lax.fori_loop(0, (last - first) // 2, body, 0)


def residual_plane(u_ref, c_ref, g_ref, w_ref, x, uo=0):
    u = [u_ref[x + uo + k] for k in (-1, 0, 1)]
    return w_ref[x] * (relaxed(u, c_ref, g_ref, x) - u[1])


def pack_body(width, e_ref, lo_ref, hi_ref):
    planes, rows, _ = e_ref.shape
    group = iota((rows, LANES), 1) // STRIP
    for q in range(lo_ref.shape[0]):
        lo = hi = jnp.zeros((rows, LANES), F32)
        for k in range(min(PER, planes - q * PER)):
            v = e_ref[q * PER + k]
            lo = jnp.where(group == k, roll(v, STRIP * k, 1), lo)
            hi = jnp.where(group == k, roll(v, STRIP * (k + 1) - width, 1), hi)
        lo_ref[q] = lo
        hi_ref[q] = hi


def pack(width, *fields):
    shapes = [jax.ShapeDtypeStruct((-(-f.shape[0] // PER),) + f.shape[1:], F32) for f in fields]

    def kernel(*refs):
        n = len(fields)
        for i in range(n):
            pack_body(width[i], refs[i], refs[n + 2 * i], refs[n + 2 * i + 1])

    return call(kernel, [s for s in shapes for _ in range(2)], [])(*fields)


def unpacked(lo_ref, hi_ref, p, high_at):
    q, k = p // PER, p % PER
    lane = iota(lo_ref.shape[1:], 1)
    high = roll(hi_ref[q], high_at - STRIP * k, 1)
    low = roll(lo_ref[q], LANES - STRIP - STRIP * k, 1)
    inside = jnp.logical_and(lane >= high_at, lane < high_at + STRIP)
    return jnp.where(inside, high, jnp.where(lane >= LANES - STRIP, low, 0.0))


def fill_wide(out_ref, e_ref, lo_ref, hi_ref, base, planes):
    for x in range(planes):
        out_ref[x, :, :LANES] = e_ref[base + x]
        out_ref[x, :, LANES:] = unpacked(lo_ref, hi_ref, base + x, 0)


def fill_narrow(out_ref, e_ref, lo_ref, hi_ref, base, planes):
    half = LANES // 2
    lane = iota(e_ref.shape[1:], 1)
    for x in range(planes):
        out_ref[x] = jnp.where(lane < half, e_ref[base + x], unpacked(lo_ref, hi_ref, base + x, half))


def call(kernel, out_shape, scratch, smem=0):
    def run(*args):
        specs = [pl.BlockSpec(memory_space=pltpu.SMEM)] * smem
        specs += [pl.BlockSpec(memory_space=pltpu.VMEM)] * (len(args) - smem)
        return pl.pallas_call(
            kernel,
            out_shape=out_shape,
            in_specs=specs,
            out_specs=jax.tree.map(lambda _: pl.BlockSpec(memory_space=pltpu.VMEM), out_shape),
            scratch_shapes=scratch,
            compiler_params=pltpu.CompilerParams(vmem_limit_bytes=40 * 2**20),
        )(*args)

    return run


def vmem(*shape):
    return pltpu.VMEM(shape, F32)


def descend0(e_ref, lo_ref, hi_ref, u_out, next_out, s, f, c, g, w, u, q):
    fill_wide(f, e_ref, lo_ref, hi_ref, 0, X0)
    fill_wide(s, e_ref, lo_ref, hi_ref, X0, X0)
    couplings(s, f, c, g, w, 1, X0 - 1, 1.0)
    first_half_sweep(u, g, 1, X0 - 1, H0)
    half_sweep(u, c, g, 2, X0 - 2, H0 + 1)
    half_sweep(u, c, g, 3, X0 - 3, H0)
    half_sweep(u, c, g, 4, X0 - 4, H0 + 1)

    def body(i, carry):
        x = H0 + 2 * i
        r = residual_plane(u, c, g, w, x) + residual_plane(u, c, g, w, x + 1)
        q[0, i] = r[8:24, :LANES]
        q[1, i] = s[x, 8:24, :LANES] + s[x + 1, 8:24, :LANES]
        u_out[2 * i] = u[x, 8:24, :LANES]
        u_out[2 * i + 1] = u[x + 1, 8:24, :LANES]
        return carry

    lax.fori_loop(0, 8, body, 0)
    pairs = q[:, :, pl.ds(0, 8, stride=2), :] + q[:, :, pl.ds(1, 8, stride=2), :]
    next_out[...] = exact_dot(pairs.reshape(128, LANES), halving(LANES)).reshape(2, 8, 8, LANES)


def descend1(e_ref, lo_ref, hi_ref, u_out, tile_out, s, f, c, g, w, u, q, t):
    fill_narrow(f, e_ref, lo_ref, hi_ref, 0, X1)
    fill_narrow(s, e_ref, lo_ref, hi_ref, X1, X1)
    couplings(s, f, c, g, w, 3, X1 - 3, 4.0)
    first_half_sweep(u, g, 3, X1 - 3, H1)
    half_sweep(u, c, g, 4, X1 - 4, H1 + 1)
    half_sweep(u, c, g, 5, X1 - 5, H1)
    half_sweep(u, c, g, 6, X1 - 6, H1 + 1)
    k, l = iota((LANES, LANES), 0), iota((LANES, LANES), 1)
    total = jnp.zeros((8, LANES), F32)
    for i in range(4):
        x = H1 + 2 * i
        r = residual_plane(u, c, g, w, x) + residual_plane(u, c, g, w, x + 1)
        q[0] = r[8:16]
        q[1] = s[x, 8:16] + s[x + 1, 8:16]
        u_out[2 * i] = u[x, 8:16]
        u_out[2 * i + 1] = u[x + 1, 8:16]
        for b in range(2):
            t[4 * b : 4 * b + 4] = q[b, pl.ds(0, 4, stride=2), :] + q[b, pl.ds(1, 4, stride=2), :]
        place = jnp.where(jnp.logical_and(k < 64, l == 32 * i + k // 2), 0.125, 0.0).astype(F32)
        total = total + exact_dot(t[...], place)
    tile_out[...] = total


def coarse(where_ref, all_ref, out_ref, s2, f2, c2, g2, w2, u2, q2, d2, s3, f3, c3, g3, w3, u3, q3, d3, s4, f4, c4, g4, w4, u4):
    lane = iota((8, LANES), 1)
    row = iota((8, LANES), 0)
    zero2 = jnp.zeros((32, LANES), F32)

    def assemble(ix, carry):
        for zt in range(4):
            sides = []
            for iz in (2 * zt, 2 * zt + 1):
                tiles = [all_ref[(ix * 4 + iy) * 8 + iz] for iy in range(4)]
                merged = []
                for xl in range(4):
                    v = roll(tiles[0], -32 * xl, 1)
                    for iy in range(1, 4):
                        v = jnp.where(lane // 32 == iy, roll(tiles[iy], 32 * (iy - xl), 1), v)
                    merged.append(v)
                sides.append(merged)
            for xl in range(4):
                even, odd = sides[0][xl], sides[1][xl]
                f2[ix * 4 + xl, 8 * zt : 8 * zt + 8] = jnp.where(row < 4, even, roll(odd, 4, 0))
                s2[ix * 4 + xl + 1, 8 * zt : 8 * zt + 8] = jnp.where(row < 4, roll(even, 4, 0), odd)
        return carry

    lax.fori_loop(0, 8, assemble, 0)
    s2[0] = zero2
    s2[33] = zero2
    for x in (0, 1, 2, 3, 36, 37, 38, 39):
        u2[x] = zero2
    for x in (0, 17):
        s3[x] = zero2[:16]
        u3[x] = zero2[:16]
    for x in (0, 9):
        s4[x] = zero2[:8]
        u4[x] = zero2[:8]

    def down(s, f, c, g, w, u, uo, n, scale, q, s_next, f_next):
        couplings(s, f, c, g, w, 0, n, scale, so=1, edges=True)
        first_half_sweep(u, g, 0, n, 0, uo)
        half_sweep(u, c, g, 0, n, 1, uo)
        half_sweep(u, c, g, 0, n, 0, uo)
        half_sweep(u, c, g, 0, n, 1, uo)
        half = n // 2

        def body(i, carry):
            x = 2 * i
            q[0, i] = residual_plane(u, c, g, w, x, uo) + residual_plane(u, c, g, w, x + 1, uo)
            q[1, i] = s[x + 1] + s[x + 2]
            return carry

        lax.fori_loop(0, half, body, 0)
        pairs = q[:, :, pl.ds(0, half, stride=2), :] + q[:, :, pl.ds(1, half, stride=2), :]
        fine = exact_dot(pairs.reshape(2 * half * half, LANES), halving(LANES)).reshape(2, half, half, LANES)
        f_next[...] = fine[0]
        s_next[1 : half + 1] = fine[1]

    def up(c, g, u, uo, n, u_next, no, d):
        half = n // 2
        twice = exact_dot(u_next[no : no + half].reshape(half * half, LANES), doubling(LANES))
        twice = twice.reshape(half, half, LANES)
        d[:, pl.ds(0, half, stride=2), :] = twice
        d[:, pl.ds(1, half, stride=2), :] = twice

        def body(i, carry):
            for k in range(2):
                u[2 * i + k + uo] = u[2 * i + k + uo] + d[i]
            return carry

        lax.fori_loop(0, half, body, 0)
        for _ in range(NU):
            half_sweep(u, c, g, 0, n, 0, uo)
            half_sweep(u, c, g, 0, n, 1, uo)

    down(s2, f2, c2, g2, w2, u2, 4, 32, 16.0, q2, s3, f3)
    down(s3, f3, c3, g3, w3, u3, 1, 16, 64.0, q3, s4, f4)
    couplings(s4, f4, c4, g4, w4, 0, 8, 256.0, so=1, edges=True)
    first_half_sweep(u4, g4, 0, 8, 0, 1)
    half_sweep(u4, c4, g4, 0, 8, 1, 1)

    def more(i, carry):
        half_sweep(u4, c4, g4, 0, 8, 0, 1)
        half_sweep(u4, c4, g4, 0, 8, 1, 1)
        return carry

    lax.fori_loop(0, BOTTOM - 1, more, 0)
    up(c3, g3, u3, 1, 16, u4, 1, d3)
    up(c2, g2, u2, 4, 32, u3, 1, d2)
    ix, iy, iz = where_ref[0], where_ref[1], where_ref[2]
    down_z = lax.rem(36 - 4 * iz, 32)
    down_y = lax.rem(LANES - 32 * iy, LANES)
    for x in range(12):
        v = pltpu.roll(u2[ix * 4 + x], down_z, 0)
        out_ref[x] = pltpu.roll(v[:16], down_y, 1)


def ascend(e0, lo0, hi0, e1, lo1, hi1, v0, vlo0, vhi0, v1, vlo1, vhi1, win, u_out, r_out, s, f, c, g, w, u, t0, d0, sl, fl, cl, gl, wl, ul, t1, d1):
    fill_narrow(fl, e1, lo1, hi1, 0, X1)
    fill_narrow(sl, e1, lo1, hi1, X1, X1)
    fill_narrow(ul, v1, vlo1, vhi1, 0, X1)
    couplings(sl, fl, cl, gl, wl, 1, X1 - 1, 4.0)
    k, l = iota((LANES, LANES), 0), iota((LANES, LANES), 1)
    widen = jnp.where(k == jnp.where(l < 96, l // 2, 64 + l // 2), 1.0, 0.0).astype(F32)
    t1[...] = exact_dot(win[...].reshape(192, LANES), widen).reshape(12, 16, LANES)
    d1[:, pl.ds(0, 12, stride=2), :] = t1[:, :12]
    d1[:, pl.ds(1, 12, stride=2), :] = t1[:, :12]
    for x in range(X1):
        ul[x] = jnp.where(sl[x] > 0.0, ul[x] + d1[(x + 1) // 2], 0.0)
    half_sweep(ul, cl, gl, 1, X1 - 1, H1)
    half_sweep(ul, cl, gl, 2, X1 - 2, H1 + 1)
    half_sweep(ul, cl, gl, 3, X1 - 3, H1)
    half_sweep(ul, cl, gl, 4, X1 - 4, H1 + 1)
    fill_wide(f, e0, lo0, hi0, 0, X0)
    fill_wide(s, e0, lo0, hi0, X0, X0)
    fill_wide(u, v0, vlo0, vhi0, 0, X0)
    couplings(s, f, c, g, w, 1, X0 - 1, 1.0)
    t0[...] = exact_dot(ul[4:18].reshape(14 * Z1, LANES), doubling(2 * LANES)).reshape(14, Z1, 2 * LANES)
    for half in range(2):
        lanes = slice(half * LANES, half * LANES + LANES)
        d0[half, :, pl.ds(0, 16, stride=2), :] = t0[:, 4:20, lanes]
        d0[half, :, pl.ds(1, 16, stride=2), :] = t0[:, 4:20, lanes]
    for x in range(X0):
        for half in range(2):
            lanes = slice(half * LANES, half * LANES + LANES)
            u[x, :, lanes] = jnp.where(s[x, :, lanes] > 0.0, u[x, :, lanes] + d0[half, (x + 1) // 2], 0.0)
    half_sweep(u, c, g, 1, X0 - 1, H0)
    half_sweep(u, c, g, 2, X0 - 2, H0 + 1)
    half_sweep(u, c, g, 3, X0 - 3, H0)
    half_sweep(u, c, g, 4, X0 - 4, H0 + 1)

    def body(i, carry):
        x = H0 + i
        u_out[i] = u[x, 8:24, :LANES]
        r_out[i] = residual_plane(u, c, g, w, x)[8:24, :LANES]
        return carry

    lax.fori_loop(0, 16, body, 0)


def swap(low, high, axis):
    count = lax.axis_size(axis)
    even = lax.axis_index(axis) % 2 == 0
    first = [(i, i ^ 1) for i in range(count)]
    second = [(i, i + 1) for i in range(1, count - 1, 2)]
    second += [(j, i) for i, j in second]
    a = lax.ppermute(jnp.where(even, high, low), axis, first)
    b = lax.ppermute(jnp.where(even, low, high), axis, second)
    return jnp.where(even, b, a), jnp.where(even, a, b)


def join(pieces):
    return jnp.concatenate([p.reshape(-1, 8, LANES) for p in pieces], 0)


def split(joined, like):
    out, at = [], 0
    for p in like:
        n = p.size // (8 * LANES)
        out.append(joined[at : at + n].reshape(p.shape))
        at += n
    return out


def swap_many(lows, highs, axis):
    low, high = swap(join(lows), join(highs), axis)
    return split(low, lows), split(high, highs)


def extend(fields, rows, planes, widths):
    lows = [f[:, :, :8] for f in fields]
    highs = [f[:, :, -8:] for f in fields]
    lows, highs = swap_many(lows, highs, "gz")
    fields = [jnp.concatenate([a, f, b], 2) for a, f, b in zip(lows, fields, highs)]
    lows = [f[:, :h] for f, h in zip(fields, planes)]
    highs = [f[:, -h:] for f, h in zip(fields, planes)]
    lows, highs = swap_many(lows, highs, "gx")
    fields = [jnp.concatenate([a, f, b], 1) for a, f, b in zip(lows, fields, highs)]
    fields = [f.reshape((-1,) + f.shape[2:]) for f in fields]
    strips = pack(widths, *fields)
    lows, highs = swap_many(strips[0::2], strips[1::2], "gy")
    return [(f, a, b) for f, a, b in zip(fields, lows, highs)]


def level_scratch(planes, rows, lanes):
    p = (planes, rows, lanes)
    return [vmem(*p), vmem(*p), vmem(6, *p), vmem(*p), vmem(*p), vmem(*p)]


def full_scratch(n, uo):
    p = (n, LANES)
    return [vmem(n + 2, *p), vmem(n, *p), vmem(6, n, *p), vmem(n, *p), vmem(n, *p), vmem(n + 2 * uo, *p)]


def shape(*dims):
    return jax.ShapeDtypeStruct(dims, F32)


def on_device(right_side, sigma):
    ((e0, lo0, hi0),) = extend([jnp.stack([right_side, sigma])], None, [H0], [LANES])
    u0, next1 = call(descend0, [shape(16, 16, LANES), shape(2, 8, 8, LANES)], level_scratch(X0, Z0, 2 * LANES) + [vmem(2, 8, 16, LANES)])(e0, lo0, hi0)
    ((e1, lo1, hi1),) = extend([next1], None, [H1], [LANES // 2])
    u1, tile = call(descend1, [shape(8, 8, LANES), shape(8, LANES)], level_scratch(X1, Z1, LANES) + [vmem(2, 8, LANES), vmem(8, LANES)])(e1, lo1, hi1)
    (v0, vlo0, vhi0), (v1, vlo1, vhi1) = extend([u0[None], u1[None]], None, [H0, H1], [LANES, LANES // 2])
    every = lax.all_to_all(jnp.broadcast_to(tile[None], (256, 8, LANES)), ("gx", "gy", "gz"), 0, 0)
    place = jnp.stack([lax.axis_index("gx"), lax.axis_index("gy"), lax.axis_index("gz")]).astype(jnp.int32)
    window = call(
        coarse,
        shape(12, 16, LANES),
        full_scratch(32, 4)
        + [vmem(2, 16, 32, LANES), vmem(16, 32, LANES)]
        + full_scratch(16, 1)
        + [vmem(2, 8, 16, LANES), vmem(8, 16, LANES)]
        + full_scratch(8, 1),
        smem=1,
    )(place, every)
    return call(
        ascend,
        (shape(16, 16, LANES), shape(16, 16, LANES)),
        level_scratch(X0, Z0, 2 * LANES)
        + [vmem(14, Z1, 2 * LANES), vmem(2, 14, Z0, LANES)]
        + level_scratch(X1, Z1, LANES)
        + [vmem(12, 16, LANES), vmem(12, Z1, LANES)],
    )(e0, lo0, hi0, e1, lo1, hi1, v0, vlo0, vhi0, v1, vlo1, vhi1, window)


def solution(mesh):
    placed = (P("gx", "gz", "gy"), P("gx", "gz", "gy"))
    return jax.shard_map(
        on_device,
        mesh=mesh,
        in_specs=placed,
        out_specs=(P("gx", "gz", "gy"), P("gx", "gz", "gy")),
        check_vma=False,
    )
```

```python
import functools

import jax
import jax.numpy as jnp
from jax import lax
from jax.experimental import pallas as pl
from jax.experimental.pallas import tpu as pltpu
from jax.sharding import PartitionSpec as P

NU = 2
BOTTOM = 8
F32 = jnp.float32
LANES = 128
STRIP = 8
PER = LANES // STRIP

H0, X0, Z0 = 5, 26, 32
H1, X1, Z1 = 7, 22, 24


def roll(v, shift, axis):
    return pltpu.roll(v, shift % v.shape[axis], axis)


def iota(shape, axis):
    return lax.broadcasted_iota(jnp.int32, shape, axis)


def exact_dot(a, b):
    return jnp.dot(a, b, precision=lax.Precision.HIGHEST, preferred_element_type=F32)


def halving(width):
    k, l = iota((width, LANES), 0), iota((width, LANES), 1)
    return jnp.where(k // 2 == l, 0.125, 0.0).astype(F32)


def doubling(width):
    k, l = iota((LANES, width), 0), iota((LANES, width), 1)
    return jnp.where(l // 2 == k, 1.0, 0.0).astype(F32)


def reds(shape, parity):
    return (iota(shape, 0) + iota(shape, 1)) % 2 == parity % 2


def couplings(s_ref, f_ref, c_ref, g_ref, w_ref, first, last, scale, so=0, edges=False, step=1):
    shape = s_ref.shape[1:]
    if edges:
        z, y = iota(shape, 0), iota(shape, 1)
        walls = (None, None, z == shape[0] - 1, z == 0, y == shape[1] - 1, y == 0)

    def chunk(x, n):
        s = [s_ref[x + so + k] for k in range(-1, n + 1)]
        for k in range(n):
            centre = s[k + 1]
            near = [
                s[k + 2],
                s[k],
                roll(centre, -1, 0),
                roll(centre, 1, 0),
                roll(centre, -1, 1),
                roll(centre, 1, 1),
            ]
            if edges:
                near = [v if wall is None else jnp.where(wall, 0.0, v) for v, wall in zip(near, walls)]
            betas = [0.5 * (centre + v) for v in near]
            total = ((betas[0] + betas[1]) + (betas[2] + betas[3])) + (betas[4] + betas[5])
            inverse = jnp.where(centre > 0.0, 1.0 / total, 0.0)
            for d in range(6):
                c = betas[d] * inverse
                if edges and walls[d] is not None:
                    c = jnp.where(walls[d], 0.0, c)
                c_ref[d, x + k] = c
            g_ref[x + k] = f_ref[x + k] * (inverse * scale)
            w_ref[x + k] = total * (1.0 / scale)

    stepped(chunk, first, last, step)


def stepped(chunk, first, last, step):
    count, rest = divmod(last - first, step)
    if count == 1:
        chunk(first, step)
    elif count:

        def body(i, carry):
            chunk(first + i * step, step)
            return carry

        lax.fori_loop(0, count, body, 0)
    if rest:
        chunk(last - rest, rest)


def relaxed(u, c_ref, g_ref, x):
    low, centre, high = u
    a = c_ref[0, x] * high + c_ref[1, x] * low
    b = c_ref[2, x] * roll(centre, -1, 0) + c_ref[3, x] * roll(centre, 1, 0)
    d = c_ref[4, x] * roll(centre, -1, 1) + c_ref[5, x] * roll(centre, 1, 1)
    return g_ref[x] + ((a + b) + d)


def half_sweep(u_ref, c_ref, g_ref, first, last, parity, uo=0, step=4):
    shape = u_ref.shape[1:]
    masks = (reds(shape, parity + first), reds(shape, parity + first + 1))

    def chunk(x, n):
        u = [u_ref[x + uo + k] for k in range(-1, n + 1)]
        new = [jnp.where(masks[k % 2], relaxed(u[k : k + 3], c_ref, g_ref, x + k), u[k + 1]) for k in range(n)]
        for k in range(n):
            u_ref[x + uo + k] = new[k]

    stepped(chunk, first, last, step)


def first_half_sweep(u_ref, g_ref, first, last, parity, uo=0, step=4):
    shape = u_ref.shape[1:]
    masks = (reds(shape, parity + first), reds(shape, parity + first + 1))

    def chunk(x, n):
        for k in range(n):
            u_ref[x + uo + k] = jnp.where(masks[k % 2], g_ref[x + k], 0.0)

    stepped(chunk, first, last, step)


def residual_planes(u_ref, c_ref, g_ref, w_ref, x, n, uo=0):
    u = [u_ref[x + uo + k] for k in range(-1, n + 1)]
    return [w_ref[x + k] * (relaxed(u[k : k + 3], c_ref, g_ref, x + k) - u[k + 1]) for k in range(n)]


def packed(planes):
    rows = planes[0].shape[0]
    group = iota((rows, LANES), 1) // STRIP
    lo = hi = jnp.zeros((rows, LANES), F32)
    for k, v in enumerate(planes):
        lo = jnp.where(group == k, roll(v, STRIP * k, 1), lo)
        hi = jnp.where(group == k, roll(v, STRIP * (k + 1), 1), hi)
    return lo, hi


def unpacked(low, high, k):
    lane = iota(low.shape, 1)
    high = roll(high, -STRIP * k, 1)
    low = roll(low, LANES - STRIP - STRIP * k, 1)
    return jnp.where(lane < STRIP, high, jnp.where(lane >= LANES - STRIP, low, 0.0))


def fill_wide(out_ref, own, low, high, i):
    for part, at, count, k0 in ((low, 0, H0, 16 - H0), (own, H0, 16, 0), (high, H0 + 16, H0, 0)):
        planes_ref, below_ref, above_ref = part
        for k in range(count):
            out_ref[at + k, :, :LANES] = planes_ref[i, k]
            out_ref[at + k, :, LANES:] = unpacked(below_ref[i], above_ref[i], k0 + k)


def fill_narrow(out_ref, own, low, high, i):
    for part, at, count in ((low, 0, H1), (own, H1, 8), (high, H1 + 8, H1)):
        for k in range(count):
            out_ref[at + k] = part[i, k]


def call(kernel, out_shape, scratch, smem=0):
    def run(*args):
        specs = [pl.BlockSpec(memory_space=pltpu.SMEM)] * smem
        specs += [pl.BlockSpec(memory_space=pltpu.VMEM)] * (len(args) - smem)
        return pl.pallas_call(
            kernel,
            out_shape=out_shape,
            in_specs=specs,
            out_specs=jax.tree.map(lambda _: pl.BlockSpec(memory_space=pltpu.VMEM), out_shape),
            scratch_shapes=scratch,
            compiler_params=pltpu.CompilerParams(vmem_limit_bytes=40 * 2**20),
        )(*args)

    return run


def vmem(*shape):
    return pltpu.VMEM(shape, F32)


def packing(f_ref, s_ref, lo_ref, hi_ref):
    for i, ref in enumerate((f_ref, s_ref)):
        lo_ref[i], hi_ref[i] = packed([ref[k] for k in range(16)])


def descend0(e, el, eh, a, b, al, bl, ah, bh, u_out, ulo_out, uhi_out, next_out, s, f, c, g, w, u, q):
    fill_wide(f, (e, a, b), (el, al, bl), (eh, ah, bh), 0)
    fill_wide(s, (e, a, b), (el, al, bl), (eh, ah, bh), 1)
    couplings(s, f, c, g, w, 1, X0 - 1, 1.0, step=2)
    first_half_sweep(u, g, 1, X0 - 1, H0)
    half_sweep(u, c, g, 2, X0 - 2, H0 + 1)
    half_sweep(u, c, g, 3, X0 - 3, H0)
    half_sweep(u, c, g, 4, X0 - 4, H0 + 1)

    def body(i, carry):
        x = H0 + 4 * i
        r = residual_planes(u, c, g, w, x, 4)
        for k in range(2):
            q[0, 2 * i + k] = (r[2 * k] + r[2 * k + 1])[8:24, :LANES]
            q[1, 2 * i + k] = s[x + 2 * k, 8:24, :LANES] + s[x + 2 * k + 1, 8:24, :LANES]
        for k in range(4):
            u_out[4 * i + k] = u[x + k, 8:24, :LANES]
        return carry

    lax.fori_loop(0, 4, body, 0)
    ulo_out[...], uhi_out[...] = packed([u_out[k] for k in range(16)])
    pairs = q[:, :, pl.ds(0, 8, stride=2), :] + q[:, :, pl.ds(1, 8, stride=2), :]
    k, l = iota((LANES, LANES), 0), iota((LANES, LANES), 1)
    halve_twice = jnp.where(k // 2 == l % 64, 0.125, 0.0).astype(F32)
    next_out[...] = exact_dot(pairs.reshape(128, LANES), halve_twice).reshape(2, 8, 8, LANES)


def descend1(e, el, eh, u_out, tile_out, s, f, c, g, w, u, q, t):
    fill_narrow(f, e, el, eh, 0)
    fill_narrow(s, e, el, eh, 1)
    couplings(s, f, c, g, w, 3, X1 - 3, 4.0, step=4)
    first_half_sweep(u, g, 3, X1 - 3, H1, step=8)
    half_sweep(u, c, g, 4, X1 - 4, H1 + 1, step=8)
    half_sweep(u, c, g, 5, X1 - 5, H1, step=12)
    half_sweep(u, c, g, 6, X1 - 6, H1 + 1, step=10)
    k, l = iota((LANES, LANES), 0), iota((LANES, LANES), 1)
    total = jnp.zeros((8, LANES), F32)
    r = residual_planes(u, c, g, w, H1, 8)
    own = iota((8, LANES), 1) < 64
    for x in range(8):
        v = u[H1 + x, 8:16]
        u_out[x] = jnp.where(own, v, roll(v, 64, 1))
    for i in range(4):
        x = H1 + 2 * i
        q[i, 0] = (r[2 * i] + r[2 * i + 1])[8:16]
        q[i, 1] = s[x, 8:16] + s[x + 1, 8:16]
        for b in range(2):
            t[i, 4 * b : 4 * b + 4] = q[i, b, pl.ds(0, 4, stride=2), :] + q[i, b, pl.ds(1, 4, stride=2), :]
        place = jnp.where(jnp.logical_and(k < 64, l == 32 * i + k // 2), 0.125, 0.0).astype(F32)
        total = total + exact_dot(t[i], place)
    tile_out[...] = total


def coarse(where_ref, mine_ref, other_ref, out_ref, s2, f2, c2, g2, w2, u2, q2, d2, s3, f3, c3, g3, w3, u3, q3, d3, s4, f4, c4, g4, w4):
    lane = iota((8, LANES), 1)
    row = iota((8, LANES), 0)
    zero2 = jnp.zeros((32, LANES), F32)

    core = lax.rem(where_ref[0], 2)

    def assemble(xc, carry):
        for all_ref, ix in ((mine_ref, 2 * xc + core), (other_ref, 2 * xc + 1 - core)):
            for zt in range(4):
                sides = []
                for iz in (2 * zt, 2 * zt + 1):
                    tiles = [all_ref[(xc * 4 + iy) * 8 + iz] for iy in range(4)]
                    merged = []
                    for xl in range(4):
                        v = roll(tiles[0], -32 * xl, 1)
                        for iy in range(1, 4):
                            v = jnp.where(lane // 32 == iy, roll(tiles[iy], 32 * (iy - xl), 1), v)
                        merged.append(v)
                    sides.append(merged)
                for xl in range(4):
                    even, odd = sides[0][xl], sides[1][xl]
                    f2[ix * 4 + xl, 8 * zt : 8 * zt + 8] = jnp.where(row < 4, even, roll(odd, 4, 0))
                    s2[ix * 4 + xl + 1, 8 * zt : 8 * zt + 8] = jnp.where(row < 4, roll(even, 4, 0), odd)
        return carry

    lax.fori_loop(0, 4, assemble, 0)
    s2[0] = zero2
    s2[33] = zero2
    for x in (0, 1, 2, 3, 36, 37, 38, 39):
        u2[x] = zero2
    for x in (0, 17):
        s3[x] = zero2[:16]
        u3[x] = zero2[:16]
    for x in (0, 9):
        s4[x] = zero2[:8]

    def down(s, f, c, g, w, u, uo, n, scale, q, s_next, f_next, step):
        couplings(s, f, c, g, w, 0, n, scale, so=1, edges=True, step=step // 2)
        first_half_sweep(u, g, 0, n, 0, uo, step)
        half_sweep(u, c, g, 0, n, 1, uo, step)
        half_sweep(u, c, g, 0, n, 0, uo, step)
        half_sweep(u, c, g, 0, n, 1, uo, step)
        half = n // 2

        def chunk(x, m):
            r = residual_planes(u, c, g, w, 2 * x, 2 * m, uo)
            for k in range(m):
                q[0, x + k] = r[2 * k] + r[2 * k + 1]
                q[1, x + k] = s[2 * (x + k) + 1] + s[2 * (x + k) + 2]

        stepped(chunk, 0, half, step // 2)
        pairs = q[:, :, pl.ds(0, half, stride=2), :] + q[:, :, pl.ds(1, half, stride=2), :]
        fine = exact_dot(pairs.reshape(2 * half * half, LANES), halving(LANES)).reshape(2, half, half, LANES)
        f_next[...] = fine[0]
        s_next[1 : half + 1] = fine[1]

    def up(c, g, u, uo, n, coarser, d, step):
        half = n // 2
        twice = exact_dot(coarser.reshape(half * half, LANES), doubling(LANES)).reshape(half, half, LANES)
        d[:, pl.ds(0, half, stride=2), :] = twice
        d[:, pl.ds(1, half, stride=2), :] = twice

        def chunk(x, m):
            for k in range(m):
                v = d[x + k]
                for j in range(2):
                    at = 2 * (x + k) + j + uo
                    u[at] = u[at] + v

        stepped(chunk, 0, half, step // 2)
        for _ in range(NU):
            half_sweep(u, c, g, 0, n, 0, uo, step)
            half_sweep(u, c, g, 0, n, 1, uo, step)

    down(s2, f2, c2, g2, w2, u2, 4, 32, 16.0, q2, s3, f3, 8)
    down(s3, f3, c3, g3, w3, u3, 1, 16, 64.0, q3, s4, f4, 16)
    couplings(s4, f4, c4, g4, w4, 0, 8, 256.0, so=1, edges=True, step=8)
    masks = (reds((8, LANES), 0), reds((8, LANES), 1))
    nothing = jnp.zeros((8, LANES), F32)
    u4 = [jnp.where(masks[x % 2], g4[x], 0.0) for x in range(8)]
    for h in range(1, 2 * BOTTOM):
        around = [nothing] + u4 + [nothing]
        u4 = [jnp.where(masks[(x + h) % 2], relaxed(around[x : x + 3], c4, g4, x), u4[x]) for x in range(8)]
    up(c3, g3, u3, 1, 16, jnp.stack(u4), d3, 16)
    up(c2, g2, u2, 4, 32, u3[1:17], d2, 8)
    ix, iy, iz = where_ref[0], where_ref[1], where_ref[2]
    down_z = lax.rem(36 - 4 * iz, 32)
    down_y = lax.rem(LANES - 32 * iy, LANES)
    for x in range(12):
        v = pltpu.roll(u2[ix * 4 + x], down_z, 0)
        out_ref[x] = pltpu.roll(v[:16], down_y, 1)


def ascend(e, el, eh, a, b, al, bl, ah, bh, n, nl, nh, v, vl, vh, va, vb, val, vbl, vah, vbh, m, ml, mh, win, u_out, r_out, s, f, c, g, w, u, t0, d0, sl, fl, cl, gl, wl, ul, t1, d1):
    fill_narrow(fl, n, nl, nh, 0)
    fill_narrow(sl, n, nl, nh, 1)
    fill_narrow(ul, m, ml, mh, 0)
    couplings(sl, fl, cl, gl, wl, 1, X1 - 1, 4.0, step=4)
    k, l = iota((LANES, LANES), 0), iota((LANES, LANES), 1)
    widen = jnp.where(k == jnp.where(l < 96, l // 2, 64 + l // 2), 1.0, 0.0).astype(F32)
    t1[...] = exact_dot(win[...].reshape(192, LANES), widen).reshape(12, 16, LANES)
    d1[:, pl.ds(0, 12, stride=2), :] = t1[:, :12]
    d1[:, pl.ds(1, 12, stride=2), :] = t1[:, :12]
    for x in range(X1):
        ul[x] = jnp.where(sl[x] > 0.0, ul[x] + d1[(x + 1) // 2], 0.0)
    half_sweep(ul, cl, gl, 1, X1 - 1, H1, step=10)
    half_sweep(ul, cl, gl, 2, X1 - 2, H1 + 1, step=10)
    half_sweep(ul, cl, gl, 3, X1 - 3, H1, step=8)
    half_sweep(ul, cl, gl, 4, X1 - 4, H1 + 1, step=14)
    fill_wide(f, (e, a, b), (el, al, bl), (eh, ah, bh), 0)
    fill_wide(s, (e, a, b), (el, al, bl), (eh, ah, bh), 1)
    fill_wide(u, (v, va, vb), (vl, val, vbl), (vh, vah, vbh), 0)
    couplings(s, f, c, g, w, 1, X0 - 1, 1.0, step=2)
    t0[...] = exact_dot(ul[4:18].reshape(14 * Z1, LANES), doubling(2 * LANES)).reshape(14, Z1, 2 * LANES)
    for half in range(2):
        lanes = slice(half * LANES, half * LANES + LANES)
        d0[half, :, pl.ds(0, 16, stride=2), :] = t0[:, 4:20, lanes]
        d0[half, :, pl.ds(1, 16, stride=2), :] = t0[:, 4:20, lanes]
    for x in range(X0):
        for half in range(2):
            lanes = slice(half * LANES, half * LANES + LANES)
            u[x, :, lanes] = jnp.where(s[x, :, lanes] > 0.0, u[x, :, lanes] + d0[half, (x + 1) // 2], 0.0)
    half_sweep(u, c, g, 1, X0 - 1, H0)
    half_sweep(u, c, g, 2, X0 - 2, H0 + 1)
    half_sweep(u, c, g, 3, X0 - 3, H0)
    half_sweep(u, c, g, 4, X0 - 4, H0 + 1)

    def body(i, carry):
        r = residual_planes(u, c, g, w, H0 + 4 * i, 4)
        for j in range(4):
            u_out[4 * i + j] = u[H0 + 4 * i + j, 8:24, :LANES]
            r_out[4 * i + j] = r[j][8:24, :LANES]
        return carry

    lax.fori_loop(0, 4, body, 0)


def axis_of(name):
    return ("xc", "co") if name == "gx" else name


def swap(low, high, name):
    axis = axis_of(name)
    count = lax.axis_size(axis)
    even = lax.axis_index(axis) % 2 == 0
    first = [(i, i ^ 1) for i in range(count)]
    second = [(i, i + 1) for i in range(1, count - 1, 2)]
    second += [(j, i) for i, j in second]
    a = lax.ppermute(jnp.where(even, high, low), axis, first)
    b = lax.ppermute(jnp.where(even, low, high), axis, second)
    return jnp.where(even, b, a), jnp.where(even, a, b)


def join(pieces):
    return jnp.concatenate([p.reshape(-1, 8, LANES) for p in pieces], 0)


def split(joined, like):
    out, at = [], 0
    for p in like:
        n = p.size // (8 * LANES)
        out.append(joined[at : at + n].reshape(p.shape))
        at += n
    return out


def swap_many(lows, highs, axis):
    low, high = swap(join(lows), join(highs), axis)
    return split(low, lows), split(high, highs)


def extend_wide(field, lo, hi, rest=None):
    extra = [] if rest is None else [rest]
    (below, *r1), (above, *r2) = swap_many([lo] + extra, [hi] + extra, "gy")
    if extra:
        lane = lax.broadcasted_iota(jnp.int32, rest.shape, 3)
        extra = [jnp.where(lane < 64, rest, jnp.where(lane < 96, r2[0], r1[0]))]
    first = [field[:, :, :8], below[:, :8], above[:, :8]]
    last = [field[:, :, 8:], below[:, 8:], above[:, 8:]]
    lows, highs = swap_many(first + extra, last + extra, "gz")
    field = jnp.concatenate([lows[0], field, highs[0]], 2)
    below = jnp.concatenate([lows[1], below, highs[1]], 1)
    above = jnp.concatenate([lows[2], above, highs[2]], 1)
    extra = [jnp.concatenate([p, q, r], 2) for p, q, r in zip(lows[3:], extra, highs[3:])]
    first = [field[:, :H0], below, above] + [v[:, :H1] for v in extra]
    last = [field[:, -H0:], below, above] + [v[:, -H1:] for v in extra]
    lows, highs = swap_many(first, last, "gx")
    wide = [field, lows[0], highs[0], below, above, lows[1], lows[2], highs[1], highs[2]]
    return wide, (extra + lows[3:] + highs[3:])


def extend_narrow(field):
    below, above = swap(field, field, "gy")
    lane = lax.broadcasted_iota(jnp.int32, field.shape, 3)
    field = jnp.where(lane < 64, field, jnp.where(lane < 96, above, below))
    low, high = swap(field, field, "gz")
    field = jnp.concatenate([low, field, high], 2)
    low, high = swap(field[:, :H1], field[:, -H1:], "gx")
    return field, low, high


def gather(tile, sizes):
    def spread(x, axes):
        n = 1
        for a in axes:
            n *= sizes[a]
        every = lax.all_to_all(jnp.broadcast_to(x[None], (n,) + x.shape), axes, 0, 0)
        return every.reshape((-1,) + x.shape[1:])

    mine = spread(spread(tile[None], ("gz",)), ("xc", "gy"))
    return mine, lax.ppermute(mine, "co", [(0, 1), (1, 0)])


def level_scratch(planes, rows, lanes):
    p = (planes, rows, lanes)
    return [vmem(*p), vmem(*p), vmem(6, *p), vmem(*p), vmem(*p), vmem(*p)]


def full_scratch(n, uo):
    p = (n, LANES)
    return [vmem(n + 2, *p), vmem(n, *p), vmem(6, n, *p), vmem(n, *p), vmem(n, *p), vmem(n + 2 * uo, *p)]


def shape(*dims):
    return jax.ShapeDtypeStruct(dims, F32)


def on_device(sizes, right_side, sigma):
    lo, hi = call(packing, [shape(2, 16, LANES)] * 2, [])(right_side, sigma)
    wide, _ = extend_wide(jnp.stack([right_side, sigma]), lo, hi)
    u0, ulo, uhi, next1 = call(
        descend0,
        [shape(16, 16, LANES), shape(16, LANES), shape(16, LANES), shape(2, 8, 8, LANES)],
        level_scratch(X0, Z0, 2 * LANES) + [vmem(2, 8, 16, LANES)],
    )(*wide)
    uwide, narrow = extend_wide(u0[None], ulo[None], uhi[None], next1)
    u1, tile = call(
        descend1,
        [shape(8, 8, LANES), shape(8, LANES)],
        level_scratch(X1, Z1, LANES) + [vmem(4, 2, 8, LANES), vmem(4, 8, LANES)],
    )(*narrow)
    unarrow = extend_narrow(u1[None])
    mine, other = gather(tile, sizes)
    place = jnp.stack([lax.axis_index(axis_of("gx")), lax.axis_index("gy"), lax.axis_index("gz")]).astype(jnp.int32)
    window = call(
        coarse,
        shape(12, 16, LANES),
        full_scratch(32, 4)
        + [vmem(2, 16, 32, LANES), vmem(16, 32, LANES)]
        + full_scratch(16, 1)
        + [vmem(2, 8, 16, LANES), vmem(8, 16, LANES)]
        + full_scratch(8, 1)[:-1],
        smem=1,
    )(place, mine, other)
    return call(
        ascend,
        (shape(16, 16, LANES), shape(16, 16, LANES)),
        level_scratch(X0, Z0, 2 * LANES)
        + [vmem(14, Z1, 2 * LANES), vmem(2, 14, Z0, LANES)]
        + level_scratch(X1, Z1, LANES)
        + [vmem(12, 16, LANES), vmem(12, Z1, LANES)],
    )(*wide, *narrow, *uwide, *unarrow, window)


def solution(mesh):
    names, dims = list(mesh.axis_names), list(mesh.devices.shape)
    at = names.index("gx")
    fine = jax.sharding.Mesh(
        mesh.devices.reshape(dims[:at] + [dims[at] // 2, 2] + dims[at + 1 :]),
        names[:at] + ["xc", "co"] + names[at + 1 :],
    )
    placed = P(("xc", "co"), "gz", "gy")
    return jax.shard_map(
        functools.partial(on_device, dict(fine.shape)),
        mesh=fine,
        in_specs=(placed, placed),
        out_specs=(placed, placed),
        check_vma=False,
    )
```

```python
import functools

import jax
import jax.numpy as jnp
from jax import lax
from jax.experimental import pallas as pl
from jax.experimental.pallas import tpu as pltpu
from jax.sharding import PartitionSpec as P

NU = 2
BOTTOM = 8
F32 = jnp.float32
LANES = 128
STRIP = 8

HD, XD, ZD = 14, 44, 48
NEAR = 5
H0, X0, Z0 = 5, 26, 32
HALF = LANES // 2
H1, X1, Z1 = 7, 22, 24


def roll(v, shift, axis):
    return pltpu.roll(v, shift % v.shape[axis], axis)


def iota(shape, axis):
    return lax.broadcasted_iota(jnp.int32, shape, axis)


def exact_dot(a, b):
    return jnp.dot(a, b, precision=lax.Precision.HIGHEST, preferred_element_type=F32)


def halving(width):
    k, l = iota((width, LANES), 0), iota((width, LANES), 1)
    return jnp.where(k // 2 == l, 0.125, 0.0).astype(F32)


def doubling(width):
    k, l = iota((LANES, width), 0), iota((LANES, width), 1)
    return jnp.where(l // 2 == k, 1.0, 0.0).astype(F32)


def reds(shape, parity):
    return (iota(shape, 0) + iota(shape, 1)) % 2 == parity % 2


def couplings(s_ref, f_ref, c_ref, g_ref, w_ref, first, last, scale, so=0, edges=False, step=1):
    shape = s_ref.shape[1:]
    if edges:
        z, y = iota(shape, 0), iota(shape, 1)
        walls = (None, None, z == shape[0] - 1, z == 0, y == shape[1] - 1, y == 0)

    def chunk(x, n):
        s = [s_ref[x + so + k] for k in range(-1, n + 1)]
        for k in range(n):
            centre = s[k + 1]
            near = [
                s[k + 2],
                s[k],
                roll(centre, -1, 0),
                roll(centre, 1, 0),
                roll(centre, -1, 1),
                roll(centre, 1, 1),
            ]
            if edges:
                near = [v if wall is None else jnp.where(wall, 0.0, v) for v, wall in zip(near, walls)]
            betas = [0.5 * (centre + v) for v in near]
            total = ((betas[0] + betas[1]) + (betas[2] + betas[3])) + (betas[4] + betas[5])
            inverse = jnp.where(centre > 0.0, 1.0 / total, 0.0)
            for d in range(6):
                c = betas[d] * inverse
                if edges and walls[d] is not None:
                    c = jnp.where(walls[d], 0.0, c)
                c_ref[d, x + k] = c
            g_ref[x + k] = f_ref[x + k] * (inverse * scale)
            w_ref[x + k] = total * (1.0 / scale)

    stepped(chunk, first, last, step)


def stepped(chunk, first, last, step):
    count, rest = divmod(last - first, step)
    if count == 1:
        chunk(first, step)
    elif count:

        def body(i, carry):
            chunk(first + i * step, step)
            return carry

        lax.fori_loop(0, count, body, 0)
    if rest:
        chunk(last - rest, rest)


def relaxed(u, c_ref, g_ref, x):
    low, centre, high = u
    a = c_ref[0, x] * high + c_ref[1, x] * low
    b = c_ref[2, x] * roll(centre, -1, 0) + c_ref[3, x] * roll(centre, 1, 0)
    d = c_ref[4, x] * roll(centre, -1, 1) + c_ref[5, x] * roll(centre, 1, 1)
    return g_ref[x] + ((a + b) + d)


def half_sweep(u_ref, c_ref, g_ref, first, last, parity, uo=0, step=4):
    shape = u_ref.shape[1:]
    masks = (reds(shape, parity + first), reds(shape, parity + first + 1))

    def chunk(x, n):
        u = [u_ref[x + uo + k] for k in range(-1, n + 1)]
        new = [jnp.where(masks[k % 2], relaxed(u[k : k + 3], c_ref, g_ref, x + k), u[k + 1]) for k in range(n)]
        for k in range(n):
            u_ref[x + uo + k] = new[k]

    stepped(chunk, first, last, step)


def first_half_sweep(u_ref, g_ref, first, last, parity, uo=0, step=4):
    shape = u_ref.shape[1:]
    masks = (reds(shape, parity + first), reds(shape, parity + first + 1))

    def chunk(x, n):
        for k in range(n):
            u_ref[x + uo + k] = jnp.where(masks[k % 2], g_ref[x + k], 0.0)

    stepped(chunk, first, last, step)


def residual_planes(u_ref, c_ref, g_ref, w_ref, x, n, uo=0):
    u = [u_ref[x + uo + k] for k in range(-1, n + 1)]
    return [w_ref[x + k] * (relaxed(u[k : k + 3], c_ref, g_ref, x + k) - u[k + 1]) for k in range(n)]


def phases(shape, parity):
    return (iota(shape, 0) + parity) % 2 == 0


def beside(v, below):
    return jnp.where(below, roll(v, 1, 1), roll(v, -1, 1))


def couplings_rb(s, f, c, g, w, first, last, scale, parity, step):
    shape = s.shape[2:]
    masks = (phases(shape, parity), phases(shape, parity + 1))

    def chunk(x, n):
        for col in range(2):
            for k in range(n):
                centre, v = s[col, x + k], s[1 - col, x + k]
                near = [
                    s[1 - col, x + k + 1],
                    s[1 - col, x + k - 1],
                    roll(v, -1, 0),
                    roll(v, 1, 0),
                    v,
                    beside(v, masks[(first + k + col) % 2]),
                ]
                betas = [0.5 * (centre + v) for v in near]
                total = ((betas[0] + betas[1]) + (betas[2] + betas[3])) + (betas[4] + betas[5])
                inverse = jnp.where(centre > 0.0, 1.0 / total, 0.0)
                for d in range(6):
                    c[col, d, x + k] = betas[d] * inverse
                g[col, x + k] = f[col, x + k] * (inverse * scale)
                w[col, x + k] = total * (1.0 / scale)

    stepped(chunk, first, last, step)


def relaxed_rb(v, c, g, col, x, mask):
    low, centre, high = v
    a = c[col, 0, x] * high + c[col, 1, x] * low
    b = c[col, 2, x] * roll(centre, -1, 0) + c[col, 3, x] * roll(centre, 1, 0)
    d = c[col, 4, x] * centre + c[col, 5, x] * beside(centre, mask)
    return g[col, x] + ((a + b) + d)


def half_sweep_rb(u_ref, v_ref, c, g, col, first, last, parity, step):
    shape = v_ref.shape[1:]
    masks = (phases(shape, parity), phases(shape, parity + 1))

    def chunk(x, n):
        v = [v_ref[x + k] for k in range(-1, n + 1)]
        for k in range(n):
            u_ref[x + k] = relaxed_rb(v[k : k + 3], c, g, col, x + k, masks[(first + k + col) % 2])

    stepped(chunk, first, last, step)


def residuals_rb(u, c, g, w, first, x, n, parity):
    shape = u.shape[2:]
    masks = (phases(shape, parity), phases(shape, parity + 1))
    out = []
    for col in range(2):
        v = [u[1 - col, x + k] for k in range(-1, n + 1)]
        out.append(
            [
                w[col, x + k] * (relaxed_rb(v[k : k + 3], c, g, col, x + k, masks[(first + k + col) % 2]) - u[col, x + k])
                for k in range(n)
            ]
        )
    return out


def permuted(v, back):
    k, l = iota((LANES, LANES), 0), iota((LANES, LANES), 1)
    if back:
        k, l = l, k
    move = jnp.where(k == jnp.where(l < HALF, 2 * l, 2 * (l - HALF) + 1), 1.0, 0.0).astype(jnp.bfloat16)
    first = v.astype(jnp.bfloat16)
    rest = v - first.astype(F32)
    second = rest.astype(jnp.bfloat16)
    third = (rest - second.astype(F32)).astype(jnp.bfloat16)
    parts = [jnp.dot(x, move, preferred_element_type=F32) for x in (first, second, third)]
    return (parts[0] + parts[1]) + parts[2]


def swapped_rows(v, parity):
    return jnp.where(phases(v.shape, parity), v, roll(v, HALF, 1))


def packed(planes, at):
    rows = planes[0].shape[0]
    group = iota((rows, LANES), 1) // STRIP
    out = jnp.zeros((rows, LANES), F32)
    for k, v in enumerate(planes):
        out = jnp.where(group == k, roll(v, STRIP * k - at, 1), out)
    return out


def with_halo(v, low, high, k):
    lane = iota(v.shape, 1)
    high = roll(high, HALF - STRIP * k, 1)
    low = roll(low, LANES - STRIP - STRIP * k, 1)
    halo = jnp.where(lane < HALF + STRIP, high, jnp.where(lane >= LANES - STRIP, low, 0.0))
    return jnp.where(lane < HALF, v, halo)


def fill_rb(out, i, at, planes_ref, below, above, k0, count, rows=None):
    r = slice(0, ZD) if rows is None else rows
    for n in range(count):
        v = planes_ref[i, n]
        for col in range(2):
            own = v if col == 0 else roll(v, HALF, 1)
            out[col, at + n, r] = with_halo(own, below[2 * i + col, r], above[2 * i + col, r], k0 + n)
            if rows is not None:
                out[col, at + n, : r.start] = jnp.zeros((r.start, LANES), F32)
                out[col, at + n, r.stop :] = jnp.zeros((ZD - r.stop, LANES), F32)


def fill_narrow(out_ref, own, low, high, i):
    for part, at, count in ((low, 0, H1), (own, H1, 8), (high, H1 + 8, H1)):
        for k in range(count):
            out_ref[at + k] = part[i, k]


def call(kernel, out_shape, scratch, smem=0):
    def run(*args):
        specs = [pl.BlockSpec(memory_space=pltpu.SMEM)] * smem
        specs += [pl.BlockSpec(memory_space=pltpu.VMEM)] * (len(args) - smem)
        return pl.pallas_call(
            kernel,
            out_shape=out_shape,
            in_specs=specs,
            out_specs=jax.tree.map(lambda _: pl.BlockSpec(memory_space=pltpu.VMEM), out_shape),
            scratch_shapes=scratch,
            compiler_params=pltpu.CompilerParams(vmem_limit_bytes=40 * 2**20),
        )(*args)

    return run


def vmem(*shape):
    return pltpu.VMEM(shape, F32)


def packing(f_ref, s_ref, out_ref, lo_ref, hi_ref):
    for i, ref in enumerate((f_ref, s_ref)):
        out_ref[i] = permuted(ref[...].reshape(256, LANES), False).reshape(16, 16, LANES)
        planes = [swapped_rows(out_ref[i, x], x) for x in range(16)]
        for x in range(16):
            out_ref[i, x] = planes[x]
        for col in range(2):
            lo_ref[2 * i + col] = packed(planes, HALF * col)
            hi_ref[2 * i + col] = packed(planes, HALF * col + HALF - STRIP)


def descend(e, b, a, ln, lf, lb, la, hn, hf, hb, ha, top_out, s1_out, next_out, tile_out, s, f, c, g, w, u, q, fl, cl, gl, wl, ul, ql, t):
    far = slice(8, ZD - 8)
    for i, out in enumerate((f, s)):
        fill_rb(out, i, 0, lf, lb, la, 16 - HD, HD - NEAR, far)
        fill_rb(out, i, HD - NEAR, ln, lb, la, 16 - NEAR, NEAR)
        fill_rb(out, i, HD, e, b, a, 0, 16)
        fill_rb(out, i, HD + 16, hn, hb, ha, 0, NEAR)
        fill_rb(out, i, HD + 16 + NEAR, hf, hb, ha, NEAR, HD - NEAR, far)
    couplings_rb(s, f, c, g, w, 2, XD - 2, 1.0, 0, 2)
    red, black = u.at[0], u.at[1]
    half_sweep_rb(black, g.at[0], c, g, 1, 3, XD - 3, 0, 4)
    half_sweep_rb(red, black, c, g, 0, 4, XD - 4, 0, 4)
    half_sweep_rb(black, red, c, g, 1, 5, XD - 5, 0, 4)

    def residual_body(i, carry):
        r = residuals_rb(u, c, g, w, 6, 6 + 4 * i, 4, 0)
        for k in range(2):
            q[0, 2 * i + k + 3] = (r[0][2 * k] + r[0][2 * k + 1]) + (r[1][2 * k] + r[1][2 * k + 1])
        return carry

    lax.fori_loop(0, 8, residual_body, 0)
    nothing = jnp.zeros((ZD, LANES), F32)
    for i in (0, 1, 2, 19, 20, 21):
        q[0, i] = nothing

    def coefficient_body(i, carry):
        q[1, i] = (s[0, 2 * i] + s[0, 2 * i + 1]) + (s[1, 2 * i] + s[1, 2 * i + 1])
        return carry

    lax.fori_loop(0, X1, coefficient_body, 0)
    sl = s1_out
    for i, ref in enumerate((fl, sl)):
        ref[...] = 0.125 * (q[i, :, pl.ds(0, Z1, stride=2), :] + q[i, :, pl.ds(1, Z1, stride=2), :])

    def top_body(i, carry):
        for col in range(2):
            top_out[col, i] = s[col, HD - H0 + i, 8 : ZD - 8]
            top_out[2 + col, i] = f[col, HD - H0 + i, 8 : ZD - 8]
        top_out[4, i] = black[HD - H0 + i, 8 : ZD - 8]
        return carry

    lax.fori_loop(0, X0, top_body, 0)
    couplings(sl, fl, cl, gl, wl, 3, X1 - 3, 4.0, step=4)
    first_half_sweep(ul, gl, 3, X1 - 3, H1, step=8)
    half_sweep(ul, cl, gl, 4, X1 - 4, H1 + 1, step=14)
    half_sweep(ul, cl, gl, 5, X1 - 5, H1, step=12)
    half_sweep(ul, cl, gl, 6, X1 - 6, H1 + 1, step=10)
    k, l = iota((LANES, LANES), 0), iota((LANES, LANES), 1)
    total = jnp.zeros((8, LANES), F32)
    r = residual_planes(ul, cl, gl, wl, H1, 8)
    own = iota((8, LANES), 1) < HALF
    for x in range(8):
        for i, ref in enumerate((ul, fl)):
            v = ref[H1 + x, 8:16]
            next_out[i, x] = jnp.where(own, v, roll(v, HALF, 1))
    for i in range(4):
        x = H1 + 2 * i
        ql[i, 0] = (r[2 * i] + r[2 * i + 1])[8:16]
        ql[i, 1] = sl[x, 8:16] + sl[x + 1, 8:16]
        for b in range(2):
            t[i, 4 * b : 4 * b + 4] = ql[i, b, pl.ds(0, 4, stride=2), :] + ql[i, b, pl.ds(1, 4, stride=2), :]
        place = jnp.where(jnp.logical_and(k < HALF, l == 32 * i + k // 2), 0.125, 0.0).astype(F32)
        total = total + exact_dot(t[i], place)
    tile_out[...] = total


def coarse(where_ref, mine_ref, other_ref, out_ref, s2, f2, c2, g2, w2, u2, q2, d2, s3, f3, c3, g3, w3, u3, q3, d3, s4, f4, c4, g4, w4):
    lane = iota((8, LANES), 1)
    row = iota((8, LANES), 0)
    zero2 = jnp.zeros((32, LANES), F32)

    core = lax.rem(where_ref[0], 2)

    def assemble(xc, carry):
        for all_ref, ix in ((mine_ref, 2 * xc + core), (other_ref, 2 * xc + 1 - core)):
            for zt in range(4):
                sides = []
                for iz in (2 * zt, 2 * zt + 1):
                    tiles = [all_ref[(xc * 4 + iy) * 8 + iz] for iy in range(4)]
                    merged = []
                    for xl in range(4):
                        v = roll(tiles[0], -32 * xl, 1)
                        for iy in range(1, 4):
                            v = jnp.where(lane // 32 == iy, roll(tiles[iy], 32 * (iy - xl), 1), v)
                        merged.append(v)
                    sides.append(merged)
                for xl in range(4):
                    even, odd = sides[0][xl], sides[1][xl]
                    f2[ix * 4 + xl, 8 * zt : 8 * zt + 8] = jnp.where(row < 4, even, roll(odd, 4, 0))
                    s2[ix * 4 + xl + 1, 8 * zt : 8 * zt + 8] = jnp.where(row < 4, roll(even, 4, 0), odd)
        return carry

    lax.fori_loop(0, 4, assemble, 0)
    s2[0] = zero2
    s2[33] = zero2
    for x in (0, 1, 2, 3, 36, 37, 38, 39):
        u2[x] = zero2
    for x in (0, 17):
        s3[x] = zero2[:16]
        u3[x] = zero2[:16]
    for x in (0, 9):
        s4[x] = zero2[:8]

    def down(s, f, c, g, w, u, uo, n, scale, q, s_next, f_next, step):
        couplings(s, f, c, g, w, 0, n, scale, so=1, edges=True, step=step // 2)
        first_half_sweep(u, g, 0, n, 0, uo, step)
        half_sweep(u, c, g, 0, n, 1, uo, step)
        half_sweep(u, c, g, 0, n, 0, uo, step)
        half_sweep(u, c, g, 0, n, 1, uo, step)
        half = n // 2

        def chunk(x, m):
            r = residual_planes(u, c, g, w, 2 * x, 2 * m, uo)
            for k in range(m):
                q[0, x + k] = r[2 * k] + r[2 * k + 1]
                q[1, x + k] = s[2 * (x + k) + 1] + s[2 * (x + k) + 2]

        stepped(chunk, 0, half, step // 2)
        pairs = q[:, :, pl.ds(0, half, stride=2), :] + q[:, :, pl.ds(1, half, stride=2), :]
        fine = exact_dot(pairs.reshape(2 * half * half, LANES), halving(LANES)).reshape(2, half, half, LANES)
        f_next[...] = fine[0]
        s_next[1 : half + 1] = fine[1]

    def up(c, g, u, uo, n, coarser, d, step):
        half = n // 2
        twice = exact_dot(coarser.reshape(half * half, LANES), doubling(LANES)).reshape(half, half, LANES)
        d[:, pl.ds(0, half, stride=2), :] = twice
        d[:, pl.ds(1, half, stride=2), :] = twice

        def chunk(x, m):
            for k in range(m):
                v = d[x + k]
                for j in range(2):
                    at = 2 * (x + k) + j + uo
                    u[at] = u[at] + v

        stepped(chunk, 0, half, step // 2)
        for _ in range(NU):
            half_sweep(u, c, g, 0, n, 0, uo, step)
            half_sweep(u, c, g, 0, n, 1, uo, step)

    down(s2, f2, c2, g2, w2, u2, 4, 32, 16.0, q2, s3, f3, 8)
    down(s3, f3, c3, g3, w3, u3, 1, 16, 64.0, q3, s4, f4, 16)
    couplings(s4, f4, c4, g4, w4, 0, 8, 256.0, so=1, edges=True, step=8)
    masks = (reds((8, LANES), 0), reds((8, LANES), 1))
    nothing = jnp.zeros((8, LANES), F32)
    u4 = [jnp.where(masks[x % 2], g4[x], 0.0) for x in range(8)]
    for h in range(1, 2 * BOTTOM):
        around = [nothing] + u4 + [nothing]
        u4 = [jnp.where(masks[(x + h) % 2], relaxed(around[x : x + 3], c4, g4, x), u4[x]) for x in range(8)]
    up(c3, g3, u3, 1, 16, jnp.stack(u4), d3, 16)
    up(c2, g2, u2, 4, 32, u3[1:17], d2, 8)
    ix, iy, iz = where_ref[0], where_ref[1], where_ref[2]
    down_z = lax.rem(36 - 4 * iz, 32)
    down_y = lax.rem(LANES - 32 * iy, LANES)
    for x in range(12):
        v = pltpu.roll(u2[ix * 4 + x], down_z, 0)
        out_ref[x] = pltpu.roll(v[:16], down_y, 1)


def ascend(top, sl, m, ml, mh, win, u_out, r_out, c, g, w, u, d0, fl, cl, gl, wl, ul, t1, d1):
    fill_narrow(ul, m, ml, mh, 0)
    fill_narrow(fl, m, ml, mh, 1)
    couplings(sl, fl, cl, gl, wl, 1, X1 - 1, 4.0, step=4)
    k, l = iota((LANES, LANES), 0), iota((LANES, LANES), 1)
    widen = jnp.where(k == jnp.where(l < 96, l // 2, HALF + l // 2), 1.0, 0.0).astype(F32)
    t1[...] = exact_dot(win[...].reshape(192, LANES), widen).reshape(12, 16, LANES)
    d1[:, pl.ds(0, 12, stride=2), :] = t1[:, :12]
    d1[:, pl.ds(1, 12, stride=2), :] = t1[:, :12]
    for x in range(X1):
        ul[x] = jnp.where(sl[x] > 0.0, ul[x] + d1[(x + 1) // 2], 0.0)
    half_sweep(ul, cl, gl, 1, X1 - 1, H1, step=10)
    half_sweep(ul, cl, gl, 2, X1 - 2, H1 + 1, step=18)
    half_sweep(ul, cl, gl, 3, X1 - 3, H1, step=16)
    half_sweep(ul, cl, gl, 4, X1 - 4, H1 + 1, step=14)
    s, f, black, red = top.at[0:2], top.at[2:4], u.at[1], u.at[0]
    couplings_rb(s, f, c, g, w, 1, X0 - 1, 1.0, 1, 2)
    fine = ul[4:18, 4:20]
    d0[:, pl.ds(0, 16, stride=2), :] = fine
    d0[:, pl.ds(1, 16, stride=2), :] = fine
    for x in range(X0):
        black[x] = jnp.where(top[1, x] > 0.0, top[4, x] + d0[(x + 1) // 2], 0.0)
    half_sweep_rb(red, black, c, g, 0, 1, X0 - 1, 1, 6)
    half_sweep_rb(black, red, c, g, 1, 2, X0 - 2, 1, 6)
    half_sweep_rb(red, black, c, g, 0, 3, X0 - 3, 1, 6)
    half_sweep_rb(black, red, c, g, 1, 4, X0 - 4, 1, 6)

    lane = iota((16, LANES), 1)

    def body(i, carry):
        x = H0 + 4 * i
        r = residuals_rb(u, c, g, w, H0, x, 4, 1)
        for j in range(4):
            for out, a, b in ((u_out, u[0, x + j], u[1, x + j]), (r_out, r[0][j], r[1][j])):
                both = jnp.where(lane < HALF, a[8:24], roll(b[8:24], HALF, 1))
                out[4 * i + j] = swapped_rows(both, j)
        return carry

    lax.fori_loop(0, 4, body, 0)
    for out in (u_out, r_out):
        out[...] = permuted(out[...].reshape(256, LANES), True).reshape(16, 16, LANES)


def axis_of(name):
    return ("xc", "co") if name == "gx" else name


def swap(low, high, name):
    axis = axis_of(name)
    count = lax.axis_size(axis)
    even = lax.axis_index(axis) % 2 == 0
    first = [(i, i ^ 1) for i in range(count)]
    second = [(i, i + 1) for i in range(1, count - 1, 2)]
    second += [(j, i) for i, j in second]
    a = lax.ppermute(jnp.where(even, high, low), axis, first)
    b = lax.ppermute(jnp.where(even, low, high), axis, second)
    return jnp.where(even, b, a), jnp.where(even, a, b)


def join(pieces):
    return jnp.concatenate([p.reshape(-1, 8, LANES) for p in pieces], 0)


def split(joined, like):
    out, at = [], 0
    for p in like:
        n = p.size // (8 * LANES)
        out.append(joined[at : at + n].reshape(p.shape))
        at += n
    return out


def swap_many(lows, highs, axis):
    low, high = swap(join(lows), join(highs), axis)
    return split(low, lows), split(high, highs)


def extend_wide(field, lo, hi):
    below, above = swap(lo, hi, "gy")
    pieces = [field, below, above]
    lows, highs = swap_many(pieces, pieces, "gz")
    field, below, above = [jnp.concatenate(v, v[0].ndim - 2) for v in zip(lows, pieces, highs)]
    rows = slice(8, ZD - 8)
    first = [field[:, :NEAR], field[:, NEAR:HD, rows], below, above]
    last = [field[:, -NEAR:], field[:, -HD:-NEAR, rows], below, above]
    lows, highs = swap_many(first, last, "gx")
    return [field, below, above] + lows + highs


def extend_narrow(field):
    below, above = swap(field, field, "gy")
    lane = lax.broadcasted_iota(jnp.int32, field.shape, 3)
    field = jnp.where(lane < 64, field, jnp.where(lane < 96, above, below))
    low, high = swap(field, field, "gz")
    field = jnp.concatenate([low, field, high], 2)
    low, high = swap(field[:, :H1], field[:, -H1:], "gx")
    return field, low, high


def gather(tile, sizes):
    def spread(x, axes):
        n = 1
        for a in axes:
            n *= sizes[a]
        every = lax.all_to_all(jnp.broadcast_to(x[None], (n,) + x.shape), axes, 0, 0)
        return every.reshape((-1,) + x.shape[1:])

    mine = spread(spread(tile[None], ("gz",)), ("xc", "gy"))
    return mine, lax.ppermute(mine, "co", [(0, 1), (1, 0)])


def level_scratch(planes, rows):
    p = (planes, rows, LANES)
    return [vmem(*p), vmem(*p), vmem(6, *p), vmem(*p), vmem(*p), vmem(*p)]


def rb_scratch(planes, rows, count):
    p = (planes, rows, LANES)
    return ([vmem(2, *p)] * 6)[: count - 4] + [vmem(2, 6, *p)] + [vmem(2, *p)] * 3


def full_scratch(n, uo):
    p = (n, LANES)
    return [vmem(n + 2, *p), vmem(n, *p), vmem(6, n, *p), vmem(n, *p), vmem(n, *p), vmem(n + 2 * uo, *p)]


def shape(*dims):
    return jax.ShapeDtypeStruct(dims, F32)


def on_device(sizes, right_side, sigma):
    field, lo, hi = call(packing, [shape(2, 16, 16, LANES), shape(4, 16, LANES), shape(4, 16, LANES)], [])(right_side, sigma)
    top, s1, next1, tile = call(
        descend,
        [shape(5, X0, Z0, LANES), shape(X1, Z1, LANES), shape(2, 8, 8, LANES), shape(8, LANES)],
        rb_scratch(XD, ZD, 6)
        + [vmem(2, X1, ZD, LANES)]
        + level_scratch(X1, Z1)[1:]
        + [vmem(4, 2, 8, LANES), vmem(4, 8, LANES)],
    )(*extend_wide(field, lo, hi))
    narrow = extend_narrow(next1)
    mine, other = gather(tile, sizes)
    place = jnp.stack([lax.axis_index(axis_of("gx")), lax.axis_index("gy"), lax.axis_index("gz")]).astype(jnp.int32)
    window = call(
        coarse,
        shape(12, 16, LANES),
        full_scratch(32, 4)
        + [vmem(2, 16, 32, LANES), vmem(16, 32, LANES)]
        + full_scratch(16, 1)
        + [vmem(2, 8, 16, LANES), vmem(8, 16, LANES)]
        + full_scratch(8, 1)[:-1],
        smem=1,
    )(place, mine, other)
    return call(
        ascend,
        (shape(16, 16, LANES), shape(16, 16, LANES)),
        rb_scratch(X0, Z0, 4)
        + [vmem(14, Z0, LANES)]
        + level_scratch(X1, Z1)[1:]
        + [vmem(12, 16, LANES), vmem(12, Z1, LANES)],
    )(top, s1, *narrow, window)


def solution(mesh):
    names, dims = list(mesh.axis_names), list(mesh.devices.shape)
    at = names.index("gx")
    fine = jax.sharding.Mesh(
        mesh.devices.reshape(dims[:at] + [dims[at] // 2, 2] + dims[at + 1 :]),
        names[:at] + ["xc", "co"] + names[at + 1 :],
    )
    placed = P(("xc", "co"), "gz", "gy")
    return jax.shard_map(
        functools.partial(on_device, dict(fine.shape)),
        mesh=fine,
        in_specs=(placed, placed),
        out_specs=(placed, placed),
        check_vma=False,
    )
```

```python
import functools

import jax
import jax.numpy as jnp
from jax import lax
from jax.experimental import pallas as pl
from jax.experimental.pallas import tpu as pltpu
from jax.sharding import PartitionSpec as P

NU = 2
BOTTOM = 8
F32 = jnp.float32
LANES = 128
STRIP = 8

HD, XD, ZD = 14, 44, 48
NEAR = 5
H0, X0, Z0 = 5, 26, 32
HALF = LANES // 2
H1, X1, Z1 = 7, 22, 24


def roll(v, shift, axis):
    return pltpu.roll(v, shift % v.shape[axis], axis)


def iota(shape, axis):
    return lax.broadcasted_iota(jnp.int32, shape, axis)


def exact_dot(a, b):
    return jnp.dot(a, b, precision=lax.Precision.HIGHEST, preferred_element_type=F32)


def reds(shape, parity):
    return ((iota(shape, 0) + iota(shape, 1)) & 1) == parity % 2


def couplings(s_ref, f_ref, c_ref, g_ref, w_ref, first, last, scale, so=0, edges=False, step=1, lanes=1):
    shape = s_ref.shape[1:]
    if edges:
        z = iota(shape, 0)
        walls = (None, None, z == shape[0] - 1, z == 0, None, None)

    def chunk(x, n):
        s = [s_ref[x + so + k] for k in range(-1, n + 1)]
        for k in range(n):
            centre = s[k + 1]
            near = [
                s[k + 2],
                s[k],
                roll(centre, -1, 0),
                roll(centre, 1, 0),
                roll(centre, -lanes, 1),
                roll(centre, lanes, 1),
            ]
            if edges:
                near = [v if wall is None else jnp.where(wall, 0.0, v) for v, wall in zip(near, walls)]
            betas = [centre + v for v in near]
            total = ((betas[0] + betas[1]) + (betas[2] + betas[3])) + (betas[4] + betas[5])
            inverse = jnp.where(centre > 0.0, 1.0 / total, 0.0)
            for d in range(6):
                c = betas[d] * inverse
                if edges and walls[d] is not None:
                    c = jnp.where(walls[d], 0.0, c)
                c_ref[d, x + k] = c
            g_ref[x + k] = f_ref[x + k] * (inverse * (2.0 * scale))
            w_ref[x + k] = total * (0.5 / scale)

    stepped(chunk, first, last, step)


def stepped(chunk, first, last, step):
    count, rest = divmod(last - first, step)
    if count == 1:
        chunk(first, step)
    elif count:

        def body(i, carry):
            chunk(first + i * step, step)
            return carry

        lax.fori_loop(0, count, body, 0)
    if rest:
        chunk(last - rest, rest)


def relaxed(u, c_ref, g_ref, x, lanes=1):
    low, centre, high = u
    a = c_ref[0, x] * high + c_ref[1, x] * low
    b = c_ref[2, x] * roll(centre, -1, 0) + c_ref[3, x] * roll(centre, 1, 0)
    d = c_ref[4, x] * roll(centre, -lanes, 1) + c_ref[5, x] * roll(centre, lanes, 1)
    return g_ref[x] + ((a + b) + d)


def half_sweep(u_ref, c_ref, g_ref, first, last, parity, uo=0, step=4):
    shape = u_ref.shape[1:]
    masks = (reds(shape, parity + first), reds(shape, parity + first + 1))

    def chunk(x, n):
        u = [u_ref[x + uo + k] for k in range(-1, n + 1)]
        new = [jnp.where(masks[k % 2], relaxed(u[k : k + 3], c_ref, g_ref, x + k), u[k + 1]) for k in range(n)]
        for k in range(n):
            u_ref[x + uo + k] = new[k]

    stepped(chunk, first, last, step)


def first_half_sweep(u_ref, g_ref, first, last, parity, uo=0, step=4):
    shape = u_ref.shape[1:]
    masks = (reds(shape, parity + first), reds(shape, parity + first + 1))

    def chunk(x, n):
        for k in range(n):
            u_ref[x + uo + k] = jnp.where(masks[k % 2], g_ref[x + k], 0.0)

    stepped(chunk, first, last, step)


def residual_planes(u_ref, c_ref, g_ref, w_ref, x, n, uo=0):
    u = [u_ref[x + uo + k] for k in range(-1, n + 1)]
    return [w_ref[x + k] * (relaxed(u[k : k + 3], c_ref, g_ref, x + k) - u[k + 1]) for k in range(n)]


def phases(shape, parity):
    return (iota(shape, 0) & 1) == parity % 2


def beside(planes, below):
    out = []
    for a, b in zip(planes[0::2], planes[1::2]):
        lower = roll(jnp.where(below, a, b), 1, 1)
        upper = roll(jnp.where(below, b, a), -1, 1)
        out += [jnp.where(below, lower, upper), jnp.where(below, upper, lower)]
    return out


def couplings_rb(s, f, c, g, w, first, last, scale, parity, step, so=0, edges=False):
    shape = s.shape[2:]
    masks = (phases(shape, parity), phases(shape, parity + 1))
    z, j = iota(shape, 0), iota(shape, 1) & (HALF - 1)
    walls = [None] * 5
    if edges:
        walls = [None, None, z == shape[0] - 1, z == 0, None]
        ends = [j == jnp.where(m, 0, HALF - 1) for m in masks]

    def chunk(x, n):
        for col in range(2):
            others = [s[1 - col, x + k + so] for k in range(n)]
            others = list(zip(others, beside(others, masks[(first + col) % 2])))
            for k in range(n):
                m = (first + k + col) % 2
                centre = s[col, x + k + so]
                v, second = others[k]
                near = [
                    s[1 - col, x + k + so + 1],
                    s[1 - col, x + k + so - 1],
                    roll(v, -1, 0),
                    roll(v, 1, 0),
                    v,
                    second,
                ]
                wall = walls + [ends[m] if edges else None]
                near = [v if e is None else jnp.where(e, 0.0, v) for v, e in zip(near, wall)]
                betas = [centre + v for v in near]
                total = ((betas[0] + betas[1]) + (betas[2] + betas[3])) + (betas[4] + betas[5])
                inverse = jnp.where(centre > 0.0, 1.0 / total, 0.0)
                for d in range(6):
                    v = betas[d] * inverse
                    c[col, d, x + k] = v if wall[d] is None else jnp.where(wall[d], 0.0, v)
                g[col, x + k] = f[col, x + k] * (inverse * (2.0 * scale))
                w[col, x + k] = total * (0.5 / scale)

    stepped(chunk, first, last, step)


def relaxed_rb(v, second, c, g, col, x):
    low, centre, high = v
    a = c[col, 0, x] * high + c[col, 1, x] * low
    b = c[col, 2, x] * roll(centre, -1, 0) + c[col, 3, x] * roll(centre, 1, 0)
    d = c[col, 4, x] * centre + c[col, 5, x] * second
    return g[col, x] + ((a + b) + d)


def half_sweep_rb(u_ref, v_ref, c, g, col, first, last, parity, step, uo=0):
    mask = phases(v_ref.shape[1:], parity + first + col)

    def chunk(x, n):
        v = [v_ref[x + k + uo] for k in range(-1, n + 1)]
        seconds = beside(v[1:-1], mask)
        for k in range(n):
            u_ref[x + k + uo] = relaxed_rb(v[k : k + 3], seconds[k], c, g, col, x + k)

    stepped(chunk, first, last, step)


def residuals_rb(u, c, g, w, first, x, n, parity, uo=0):
    out = []
    for col in range(2):
        v = [u[1 - col, x + k + uo] for k in range(-1, n + 1)]
        seconds = beside(v[1:-1], phases(u.shape[2:], parity + first + col))
        new = [relaxed_rb(v[k : k + 3], seconds[k], c, g, col, x + k) for k in range(n)]
        out.append([w[col, x + k] * (new[k] - u[col, x + k + uo]) for k in range(n)])
    return out


def permuted(v, back):
    k, l = iota((LANES, LANES), 0), iota((LANES, LANES), 1)
    if back:
        k, l = l, k
    move = jnp.where(k == jnp.where(l < HALF, 2 * l, 2 * (l - HALF) + 1), 1.0, 0.0).astype(jnp.bfloat16)
    first = v.astype(jnp.bfloat16)
    rest = v - first.astype(F32)
    second = rest.astype(jnp.bfloat16)
    third = (rest - second.astype(F32)).astype(jnp.bfloat16)
    parts = [jnp.dot(x, move, preferred_element_type=F32) for x in (first, second, third)]
    return (parts[0] + parts[1]) + parts[2]


def swapped_rows(v, parity):
    return jnp.where(phases(v.shape, parity), v, roll(v, HALF, 1))


def packed(planes, at, group):
    rows = planes[0].shape[0]
    groups = iota((rows, LANES), 1) >> 3
    out = jnp.zeros((rows, LANES), F32)
    for k, v in enumerate(planes):
        out = jnp.where(groups == group(k), roll(v, STRIP * group(k) - at, 1), out)
    return out


def high_group(k):
    return 2 * k


def low_group(k):
    return (2 * k + 7) % 16


def fill_rb(out, i, at, planes_ref, strips, k0, count, rows, step=4):
    number = rows.stop - rows.start
    lane = iota((number, LANES), 1)
    own = lane < HALF
    halo = jnp.logical_or(lane < HALF + STRIP, lane >= LANES - STRIP)

    def chunk(n, many):
        for m in range(many):
            v = planes_ref[n + m]
            shift = lax.rem(HALF + LANES - 2 * STRIP * lax.rem(n + m + k0, 8), LANES)
            for col in range(2):
                h = jnp.where(halo, pltpu.roll(strips(2 * i + col), shift, 1), 0.0)
                out[col, at + n + m, rows.start : rows.stop] = jnp.where(own, roll(v, HALF, 1) if col else v, h)
                if number < ZD:
                    out[col, at + n + m, : rows.start] = jnp.zeros((rows.start, LANES), F32)
                    out[col, at + n + m, rows.stop :] = jnp.zeros((ZD - rows.stop, LANES), F32)

    def body(n, carry):
        chunk(n * step, step)
        return carry

    lax.fori_loop(0, count // step, body, 0)
    if count % step:
        chunk(jnp.int32(count - count % step), count % step)


def fill_narrow(u, f, own, low, high):
    lane = iota((Z1, LANES), 1)
    for part, at, count in ((low, 0, H1), (own, H1, 8), (high, H1 + 8, H1)):
        for k in range(count):
            v, h = part[0, k], part[1, k]
            u[at + k] = jnp.where(lane < HALF, v, roll(h, HALF, 1))
            f[at + k] = jnp.where(lane < HALF, roll(v, HALF, 1), h)


def call(kernel, out_shape, scratch, smem=0, cost=4):
    def run(*args):
        specs = [pl.BlockSpec(memory_space=pltpu.SMEM)] * smem
        specs += [pl.BlockSpec(memory_space=pltpu.VMEM)] * (len(args) - smem)
        return pl.pallas_call(
            kernel,
            out_shape=out_shape,
            in_specs=specs,
            out_specs=jax.tree.map(lambda _: pl.BlockSpec(memory_space=pltpu.VMEM), out_shape),
            scratch_shapes=scratch,
            compiler_params=pltpu.CompilerParams(vmem_limit_bytes=40 * 2**20),
            cost_estimate=pl.CostEstimate(flops=cost * 10**6, bytes_accessed=cost * 3 * 10**6, transcendentals=0),
        )(*args)

    return run


def vmem(*shape):
    return pltpu.VMEM(shape, F32)


def packing(f_ref, s_ref, out_ref, lo_ref, hi_ref):
    for i, ref in enumerate((f_ref, s_ref)):
        out_ref[i] = permuted(ref[...].reshape(256, LANES), False).reshape(16, 16, LANES)
        planes = [swapped_rows(out_ref[i, x], x) for x in range(16)]
        for x in range(16):
            out_ref[i, x] = planes[x]
        for col in range(2):
            for q in range(2):
                some = planes[8 * q : 8 * q + 8]
                lo_ref[2 * i + col, q] = packed(some, HALF * col, high_group)
                hi_ref[2 * i + col, q] = packed(some, HALF * col + HALF - STRIP, low_group)


def descend(e, b, lsn, lsf, lfn, lff, lb0, lb1, hsn, hsf, hfn, hff, hb0, hb1, top_out, s1_out, next_out, tile_out, s, f, c, g, w, u, q, fl, cl, gl, wl, ul, ql, t):
    every, some = slice(0, ZD), slice(8, ZD - 8)
    for i, out, ln, lf, hn, hf, near, deep in ((0, f, lfn, lff, hfn, hff, 3, 12), (1, s, lsn, lsf, hsn, hsf, NEAR, HD)):
        first = 16 - deep
        fill_rb(out, i, HD - deep, lf, lambda n: lb0[n], first, 8 - first, some)
        fill_rb(out, i, HD - 8, lf.at[8 - first :], lambda n: lb1[n, 8 : ZD - 8], 8, 8 - near, some)
        fill_rb(out, i, HD - near, ln, lambda n: lb1[n], 16 - near, near, every)
        for h in range(2):
            fill_rb(out, i, HD + 8 * h, e.at[i, 8 * h : 8 * h + 8], lambda n, h=h: b[n, h], 8 * h, 8, every)
        fill_rb(out, i, HD + 16, hn, lambda n: hb0[n], 0, near, every)
        fill_rb(out, i, HD + 16 + near, hf, lambda n: hb0[n, 8 : ZD - 8], near, 8 - near, some)
        fill_rb(out, i, HD + 24, hf.at[8 - near :], lambda n: hb1[n], 8, deep - 8, some)
    couplings_rb(s, f, c, g, w, 2, XD - 2, 1.0, 0, 4)
    red, black = u.at[0], u.at[1]
    half_sweep_rb(black, g.at[0], c, g, 1, 3, XD - 3, 0, 10)
    half_sweep_rb(red, black, c, g, 0, 4, XD - 4, 0, 12)
    half_sweep_rb(black, red, c, g, 1, 5, XD - 5, 0, 12)

    def residual_body(i, carry):
        r = residuals_rb(u, c, g, w, 6, 6 + 8 * i, 8, 0)
        for k in range(4):
            q[0, 4 * i + k + 3] = (r[0][2 * k] + r[0][2 * k + 1]) + (r[1][2 * k] + r[1][2 * k + 1])
        return carry

    lax.fori_loop(0, 4, residual_body, 0)
    nothing = jnp.zeros((ZD, LANES), F32)
    for i in (0, 1, 2, 19, 20, 21):
        q[0, i] = nothing

    def coefficient_body(i, carry):
        q[1, i] = (s[0, 2 * i] + s[0, 2 * i + 1]) + (s[1, 2 * i] + s[1, 2 * i + 1])
        return carry

    lax.fori_loop(0, X1, coefficient_body, 0)
    sl = s1_out
    for i, ref in enumerate((fl, sl)):
        ref[...] = 0.125 * (q[i, :, pl.ds(0, Z1, stride=2), :] + q[i, :, pl.ds(1, Z1, stride=2), :])

    def top_body(i, carry):
        for col in range(2):
            top_out[col, i] = s[col, HD - H0 + i, 8 : ZD - 8]
            top_out[2 + col, i] = f[col, HD - H0 + i, 8 : ZD - 8]
        top_out[4, i] = black[HD - H0 + i, 8 : ZD - 8]
        return carry

    lax.fori_loop(0, X0, top_body, 0)
    couplings(sl, fl, cl, gl, wl, 3, X1 - 3, 4.0, step=4)
    first_half_sweep(ul, gl, 3, X1 - 3, H1, step=8)
    half_sweep(ul, cl, gl, 4, X1 - 4, H1 + 1, step=14)
    half_sweep(ul, cl, gl, 5, X1 - 5, H1, step=12)
    half_sweep(ul, cl, gl, 6, X1 - 6, H1 + 1, step=10)
    k, l = iota((LANES, LANES), 0), iota((LANES, LANES), 1)
    total = jnp.zeros((8, LANES), F32)
    r = residual_planes(ul, cl, gl, wl, H1, 8)
    own = iota((8, LANES), 1) < HALF
    for x in range(8):
        next_out[x] = jnp.where(own, ul[H1 + x, 8:16], roll(fl[H1 + x, 8:16], HALF, 1))
    for i in range(4):
        x = H1 + 2 * i
        ql[i, 0] = (r[2 * i] + r[2 * i + 1])[8:16]
        ql[i, 1] = sl[x, 8:16] + sl[x + 1, 8:16]
        for b in range(2):
            t[i, 4 * b : 4 * b + 4] = ql[i, b, pl.ds(0, 4, stride=2), :] + ql[i, b, pl.ds(1, 4, stride=2), :]
        to = 32 * i + 16 * ((k // 2) % 2) + k // 4
        place = jnp.where(jnp.logical_and(k < HALF, l == to), 0.125, 0.0).astype(F32)
        total = total + exact_dot(t[i], place)
    group = iota((8, LANES), 1) // 16
    other = jnp.where(group % 2 == 0, roll(total, -16, 1), roll(total, 16, 1))
    tile_out[...] = jnp.where((group // 2 + iota((8, LANES), 0)) % 2 == 0, total, other)


def coarse(where_ref, mine_ref, other_ref, out_ref, s2, f2, c2, g2, w2, u2, q2, d2, s3, f3, c3, g3, w3, u3, q3, d3, s4, f4, c4, g4, w4):
    lane = iota((8, LANES), 1)
    wide = iota((32, LANES), 1)
    zero2 = jnp.zeros((32, LANES), F32)
    core = lax.rem(where_ref[0], 2)

    def transposed(groups):
        for s in (1, 2, 4):
            upper = (lane & (16 * s)) != 0
            for tiles in groups:
                for m in range(8):
                    if not m & s:
                        a, b = tiles[m], tiles[m + s]
                        tiles[m] = jnp.where(upper, roll(b, 16 * s, 1), a)
                        tiles[m + s] = jnp.where(upper, b, roll(a, -16 * s, 1))
        return groups

    def assemble(xcl, carry):
        for all_ref, c in ((mine_ref, core), (other_ref, 1 - core)):
            plane = 4 * (2 * xcl + c)
            groups = []
            for zi in range(8):
                at = [((2 * xh + xcl) * 4 + iy) * 8 + zi for xh in range(2) for iy in range(4)]
                groups.append([all_ref[i] for i in at])
            for zi, tiles in enumerate(transposed(groups)):
                rows = slice(8 * (zi // 2), 8 * (zi // 2) + 8)
                for g, v in enumerate(tiles):
                    if zi % 2 == 0:
                        f2[g % 2, plane + g // 2, rows] = v
                    else:
                        s2[g % 2, plane + g // 2 + 1, rows] = v
        return carry

    lax.fori_loop(0, 2, assemble, 0)

    def wrap(ref):
        ref[0] = jnp.where(wide < HALF, 0.0, roll(ref[16], HALF, 1))
        ref[17] = jnp.where(wide < HALF, roll(ref[1], HALF, 1), 0.0)

    for col in range(2):
        wrap(s2.at[col])
    for x in (0, 17):
        s3[x] = zero2[:16]
        u3[x] = zero2[:16]
    for x in (0, 9):
        s4[x] = zero2[:8]

    red, black = u2.at[0], u2.at[1]

    def sweep2(col):
        half_sweep_rb(u2.at[col], u2.at[1 - col], c2, g2, col, 0, 16, 0, 16, 1)
        wrap(u2.at[col])

    couplings_rb(s2, f2, c2, g2, w2, 0, 16, 16.0, 0, 4, 1, True)
    for x in range(16):
        red[x + 1] = g2[0, x]
    wrap(red)
    sweep2(1)
    sweep2(0)
    sweep2(1)

    def restrict2(i, carry):
        r = residuals_rb(u2, c2, g2, w2, 0, 8 * i, 8, 0, 1)
        for k in range(4):
            x = 8 * i + 2 * k + 1
            q2[0, 4 * i + k] = (r[0][2 * k] + r[0][2 * k + 1]) + (r[1][2 * k] + r[1][2 * k + 1])
            q2[1, 4 * i + k] = (s2[0, x] + s2[0, x + 1]) + (s2[1, x] + s2[1, x + 1])
        return carry

    lax.fori_loop(0, 2, restrict2, 0)
    narrow = iota((16, LANES), 1) < HALF
    for i, ref, at in ((0, f3, 0), (1, s3, 1)):
        for x in range(8):
            v = 0.125 * (q2[i, x, pl.ds(0, 16, stride=2), :] + q2[i, x, pl.ds(1, 16, stride=2), :])
            ref[x + at] = jnp.where(narrow, v, 0.0)
            ref[x + at + 8] = jnp.where(narrow, roll(v, HALF, 1), 0.0)
    couplings(s3, f3, c3, g3, w3, 0, 16, 64.0, so=1, edges=True, step=8)
    first_half_sweep(u3, g3, 0, 16, 0, 1, 16)
    for col in (1, 0, 1):
        half_sweep(u3, c3, g3, 0, 16, col, 1, 16)
    r = residual_planes(u3, c3, g3, w3, 0, 16, 1)
    for i in range(8):
        q3[0, i] = r[2 * i] + r[2 * i + 1]
        q3[1, i] = s3[2 * i + 1] + s3[2 * i + 2]
    lane4 = iota((8, LANES), 1)
    for i, ref, at in ((0, f4, 0), (1, s4, 1)):
        for x in range(8):
            v = 0.125 * (q3[i, x, pl.ds(0, 8, stride=2), :] + q3[i, x, pl.ds(1, 8, stride=2), :])
            ref[x + at] = jnp.where((lane4 & 1) == 0, v + roll(v, -1, 1), 0.0)
    couplings(s4, f4, c4, g4, w4, 0, 8, 256.0, so=1, edges=True, step=8, lanes=2)
    odd = (iota((8, LANES), 0) + (lane4 >> 1)) & 1
    masks = (odd == 0, odd == 1)
    nothing = jnp.zeros((8, LANES), F32)
    u4 = [jnp.where(masks[x % 2], g4[x], 0.0) for x in range(8)]
    for h in range(1, 2 * BOTTOM):
        around = [nothing] + u4 + [nothing]
        u4 = [jnp.where(masks[(x + h) % 2], relaxed(around[x : x + 3], c4, g4, x, 2), u4[x]) for x in range(8)]
    for x in range(8):
        v = u4[x] + roll(u4[x], 1, 1)
        d3[x, pl.ds(0, 8, stride=2), :] = v
        d3[x, pl.ds(1, 8, stride=2), :] = v
    for x in range(16):
        u3[x + 1] = u3[x + 1] + d3[x // 2]
    for col in (0, 1) * NU:
        half_sweep(u3, c3, g3, 0, 16, col, 1, 16)
    for x in range(8):
        v = jnp.where(narrow, u3[x + 1], roll(u3[x + 9], HALF, 1))
        d2[x, pl.ds(0, 16, stride=2), :] = v
        d2[x, pl.ds(1, 16, stride=2), :] = v
    for x in range(16):
        black[x + 1] = black[x + 1] + d2[x // 2]
    wrap(black)
    for _ in range(NU):
        sweep2(0)
        sweep2(1)
    ix, iy, iz = where_ref[0], where_ref[1], where_ref[2]
    down_z = lax.rem(36 - 4 * iz, 32)
    for n in range(12):
        x = 4 * ix + 12 + n
        at = lax.rem(x, 16) + 1
        shift = lax.rem(4 * LANES - HALF * (x // 16) - 16 * iy + HALF, LANES)
        for col in range(2):
            v = pltpu.roll(u2[col, at], down_z, 0)
            out_ref[col, n] = pltpu.roll(v[:16], shift, 1)


def ascend(top, sl, m, ml, mh, win, u_out, r_out, c, g, w, u, d0, fl, cl, gl, wl, ul, t1, d1):
    fill_narrow(ul, fl, m, ml, mh)
    couplings(sl, fl, cl, gl, wl, 1, X1 - 1, 4.0, step=4)
    k, l = iota((LANES, LANES), 0), iota((LANES, LANES), 1)
    from_lane = jnp.where(l < 96, l // 4, 96 + l // 4)
    parity = iota((1, 16, LANES), 1) + iota((12, 16, LANES), 0)
    v = [win[0], win[1]]
    both = [jnp.where(parity % 2 == 0, v[i], v[1 - i]).reshape(192, LANES) for i in range(2)]
    widen = [jnp.where(jnp.logical_and(k == from_lane, (l // 2) % 2 == i), 1.0, 0.0).astype(F32) for i in range(2)]
    t1[...] = (exact_dot(both[0], widen[0]) + exact_dot(both[1], widen[1])).reshape(12, 16, LANES)
    d1[:, pl.ds(0, 12, stride=2), :] = t1[:, :12]
    d1[:, pl.ds(1, 12, stride=2), :] = t1[:, :12]
    for x in range(X1):
        ul[x] = jnp.where(sl[x] > 0.0, ul[x] + d1[(x + 1) // 2], 0.0)
    half_sweep(ul, cl, gl, 1, X1 - 1, H1, step=10)
    half_sweep(ul, cl, gl, 2, X1 - 2, H1 + 1, step=18)
    half_sweep(ul, cl, gl, 3, X1 - 3, H1, step=16)
    half_sweep(ul, cl, gl, 4, X1 - 4, H1 + 1, step=14)
    s, f, black, red = top.at[0:2], top.at[2:4], u.at[1], u.at[0]
    couplings_rb(s, f, c, g, w, 1, X0 - 1, 1.0, 1, 6)
    fine = ul[4:18, 4:20]
    d0[:, pl.ds(0, 16, stride=2), :] = fine
    d0[:, pl.ds(1, 16, stride=2), :] = fine
    for x in range(X0):
        black[x] = jnp.where(top[1, x] > 0.0, top[4, x] + d0[(x + 1) // 2], 0.0)
    half_sweep_rb(red, black, c, g, 0, 1, X0 - 1, 1, 12)
    half_sweep_rb(black, red, c, g, 1, 2, X0 - 2, 1, 12)
    half_sweep_rb(red, black, c, g, 0, 3, X0 - 3, 1, 10)
    half_sweep_rb(black, red, c, g, 1, 4, X0 - 4, 1, 18)

    lane = iota((16, LANES), 1)

    def body(i, carry):
        x = H0 + 8 * i
        r = residuals_rb(u, c, g, w, H0, x, 8, 1)
        for j in range(8):
            for out, a, b in ((u_out, u[0, x + j], u[1, x + j]), (r_out, r[0][j], r[1][j])):
                both = jnp.where(lane < HALF, a[8:24], roll(b[8:24], HALF, 1))
                out[8 * i + j] = swapped_rows(both, j)
        return carry

    lax.fori_loop(0, 2, body, 0)
    for out in (u_out, r_out):
        out[...] = permuted(out[...].reshape(256, LANES), True).reshape(16, 16, LANES)


def axis_of(name):
    return ("xc", "co") if name == "gx" else name


def swap(low, high, name):
    axis = axis_of(name)
    count = lax.axis_size(axis)
    even = lax.axis_index(axis) % 2 == 0
    first = [(i, i ^ 1) for i in range(count)]
    second = [(i, i + 1) for i in range(1, count - 1, 2)]
    second += [(j, i) for i, j in second]
    a = lax.ppermute(jnp.where(even, high, low), axis, first)
    b = lax.ppermute(jnp.where(even, low, high), axis, second)
    return jnp.where(even, b, a), jnp.where(even, a, b)


def join(pieces):
    return jnp.concatenate([p.reshape(-1, 8, LANES) for p in pieces], 0)


def split(joined, like):
    out, at = [], 0
    for p in like:
        n = p.size // (8 * LANES)
        out.append(joined[at : at + n].reshape(p.shape))
        at += n
    return out


def swap_many(lows, highs, axis):
    low, high = swap(join(lows), join(highs), axis)
    return split(low, lows), split(high, highs)


def extend_wide(field, lo, hi):
    below, above = swap(lo, hi, "gy")
    group = lax.broadcasted_iota(jnp.int32, lo.shape, 3) // STRIP
    strips = jnp.where(group % 2 == 0, above, below)
    pieces = [field, strips]
    lows, highs = swap_many(pieces, pieces, "gz")
    field, strips = [jnp.concatenate(v, v[0].ndim - 2) for v in zip(lows, pieces, highs)]
    some = slice(8, ZD - 8)
    f, s = field[0], field[1]
    first = [s[:NEAR], s[NEAR:HD, some], f[:3], f[3:12, some], strips[:, 0], strips[:, 1, some]]
    last = [s[-NEAR:], s[-HD:-NEAR, some], f[-3:], f[-12:-3, some], strips[:, 0, some], strips[:, 1]]
    low, high = swap(join(first), join(last), "gx")
    return [field, strips] + split(low, last) + split(high, first)


def extend_narrow(own):
    below, above = swap(own, own, "gy")
    lane = lax.broadcasted_iota(jnp.int32, own.shape, 2)
    own = jnp.stack([own, jnp.where(lane % HALF < HALF // 2, above, below)])
    low, high = swap(own, own, "gz")
    own = jnp.concatenate([low, own, high], 2)
    low, high = swap(own[:, :H1], own[:, -H1:], "gx")
    return own, low, high


def spread(x, axes, sizes):
    n = 1
    for a in axes:
        n *= sizes[a]
    return lax.all_to_all(jnp.broadcast_to(x[None], (n,) + x.shape), axes, 0, 0)


def level_scratch(planes, rows):
    p = (planes, rows, LANES)
    return [vmem(*p), vmem(*p), vmem(6, *p), vmem(*p), vmem(*p), vmem(*p)]


def rb_scratch(planes, rows, count):
    p = (planes, rows, LANES)
    return ([vmem(2, *p)] * 6)[: count - 4] + [vmem(2, 6, *p)] + [vmem(2, *p)] * 3


def full_scratch(n, uo):
    p = (n, LANES)
    return [vmem(n + 2, *p), vmem(n, *p), vmem(6, n, *p), vmem(n, *p), vmem(n, *p), vmem(n + 2 * uo, *p)]


def shape(*dims):
    return jax.ShapeDtypeStruct(dims, F32)


def on_device(sizes, right_side, sigma):
    field, lo, hi = call(packing, [shape(2, 16, 16, LANES), shape(4, 2, 16, LANES), shape(4, 2, 16, LANES)], [])(right_side, sigma)
    top, s1, next1, tile = call(
        descend,
        [shape(5, X0, Z0, LANES), shape(X1, Z1, LANES), shape(8, 8, LANES), shape(8, LANES)],
        rb_scratch(XD, ZD, 6)
        + [vmem(2, X1, ZD, LANES)]
        + level_scratch(X1, Z1)[1:]
        + [vmem(4, 2, 8, LANES), vmem(4, 8, LANES)],
    )(*extend_wide(field, lo, hi))
    narrow = extend_narrow(next1)
    line = spread(tile, ("gz",), sizes)
    tiles = line.reshape(4, 2, 2, 4, LANES).transpose(0, 2, 1, 3, 4).reshape(8, 8, LANES)
    mine = spread(tiles, ("xc", "gy"), sizes).reshape(-1, 8, LANES)
    other = lax.ppermute(mine, "co", [(0, 1), (1, 0)])
    place = jnp.stack([lax.axis_index(axis_of("gx")), lax.axis_index("gy"), lax.axis_index("gz")]).astype(jnp.int32)
    window = call(
        coarse,
        shape(2, 12, 16, LANES),
        [vmem(2, 18, 32, LANES)]
        + rb_scratch(16, 32, 5)[:-1]
        + [vmem(2, 18, 32, LANES), vmem(2, 8, 32, LANES), vmem(8, 32, LANES)]
        + full_scratch(16, 1)
        + [vmem(2, 8, 16, LANES), vmem(8, 16, LANES)]
        + full_scratch(8, 1)[:-1],
        smem=1,
        cost=10,
    )(place, mine, other)
    return call(
        ascend,
        (shape(16, 16, LANES), shape(16, 16, LANES)),
        rb_scratch(X0, Z0, 4)
        + [vmem(14, Z0, LANES)]
        + level_scratch(X1, Z1)[1:]
        + [vmem(12, 16, LANES), vmem(12, Z1, LANES)],
    )(top, s1, *narrow, window)


def solution(mesh):
    names, dims = list(mesh.axis_names), list(mesh.devices.shape)
    at = names.index("gx")
    fine = jax.sharding.Mesh(
        mesh.devices.reshape(dims[:at] + [dims[at] // 2, 2] + dims[at + 1 :]),
        names[:at] + ["xc", "co"] + names[at + 1 :],
    )
    placed = P(("xc", "co"), "gz", "gy")
    return jax.shard_map(
        functools.partial(on_device, dict(fine.shape)),
        mesh=fine,
        in_specs=(placed, placed),
        out_specs=(placed, placed),
        check_vma=False,
    )
```

```python
import functools

import jax
import jax.numpy as jnp
from jax import lax
from jax.experimental import pallas as pl
from jax.experimental.pallas import tpu as pltpu
from jax.sharding import PartitionSpec as P

NU = 2
BOTTOM = 8
F32 = jnp.float32
LANES = 128
STRIP = 8

HD, XD, ZD = 14, 44, 48
NEAR = 5
H0, X0, Z0 = 5, 26, 32
HALF = LANES // 2
H1, X1, Z1 = 7, 22, 24


def roll(v, shift, axis):
    return pltpu.roll(v, shift % v.shape[axis], axis)


def iota(shape, axis):
    return lax.broadcasted_iota(jnp.int32, shape, axis)


def reds(shape, parity):
    return ((iota(shape, 0) + iota(shape, 1)) & 1) == parity % 2


def couplings(s_ref, f_ref, c_ref, g_ref, w_ref, first, last, scale, so=0, edges=False, step=1, lanes=1):
    shape = s_ref.shape[1:]
    if edges:
        z = iota(shape, 0)
        walls = (None, None, z == shape[0] - 1, z == 0, None, None)

    def chunk(x, n):
        s = [s_ref[x + so + k] for k in range(-1, n + 1)]
        for k in range(n):
            centre = s[k + 1]
            near = [
                s[k + 2],
                s[k],
                roll(centre, -1, 0),
                roll(centre, 1, 0),
                roll(centre, -lanes, 1),
                roll(centre, lanes, 1),
            ]
            if edges:
                near = [v if wall is None else jnp.where(wall, 0.0, v) for v, wall in zip(near, walls)]
            betas = [centre + v for v in near]
            total = ((betas[0] + betas[1]) + (betas[2] + betas[3])) + (betas[4] + betas[5])
            inverse = jnp.where(centre > 0.0, 1.0 / total, 0.0)
            for d in range(6):
                c = betas[d] * inverse
                if edges and walls[d] is not None:
                    c = jnp.where(walls[d], 0.0, c)
                c_ref[d, x + k] = c
            g_ref[x + k] = f_ref[x + k] * (inverse * (2.0 * scale))
            w_ref[x + k] = total * (0.5 / scale)

    stepped(chunk, first, last, step)


def stepped(chunk, first, last, step):
    count, rest = divmod(last - first, step)
    if count == 1:
        chunk(first, step)
    elif count:

        def body(i, carry):
            chunk(first + i * step, step)
            return carry

        lax.fori_loop(0, count, body, 0)
    if rest:
        chunk(last - rest, rest)


def relaxed(u, c_ref, g_ref, x, lanes=1):
    low, centre, high = u
    a = c_ref[0, x] * high + c_ref[1, x] * low
    b = c_ref[2, x] * roll(centre, -1, 0) + c_ref[3, x] * roll(centre, 1, 0)
    d = c_ref[4, x] * roll(centre, -lanes, 1) + c_ref[5, x] * roll(centre, lanes, 1)
    return g_ref[x] + ((a + b) + d)


def half_sweep(u_ref, c_ref, g_ref, first, last, parity, uo=0, step=4):
    shape = u_ref.shape[1:]
    masks = (reds(shape, parity + first), reds(shape, parity + first + 1))

    def chunk(x, n):
        u = [u_ref[x + uo + k] for k in range(-1, n + 1)]
        new = [jnp.where(masks[k % 2], relaxed(u[k : k + 3], c_ref, g_ref, x + k), u[k + 1]) for k in range(n)]
        for k in range(n):
            u_ref[x + uo + k] = new[k]

    stepped(chunk, first, last, step)


def first_half_sweep(u_ref, g_ref, first, last, parity, uo=0, step=4):
    shape = u_ref.shape[1:]
    masks = (reds(shape, parity + first), reds(shape, parity + first + 1))

    def chunk(x, n):
        for k in range(n):
            u_ref[x + uo + k] = jnp.where(masks[k % 2], g_ref[x + k], 0.0)

    stepped(chunk, first, last, step)


def residual_planes(u_ref, c_ref, g_ref, w_ref, x, n, uo=0):
    u = [u_ref[x + uo + k] for k in range(-1, n + 1)]
    return [w_ref[x + k] * (relaxed(u[k : k + 3], c_ref, g_ref, x + k) - u[k + 1]) for k in range(n)]


def phases(shape, parity):
    return (iota(shape, 0) & 1) == parity % 2


def beside(planes, below):
    out = []
    for a, b in zip(planes[0::2], planes[1::2]):
        lower = roll(jnp.where(below, a, b), 1, 1)
        upper = roll(jnp.where(below, b, a), -1, 1)
        out += [jnp.where(below, lower, upper), jnp.where(below, upper, lower)]
    return out


def couplings_rb(s, f, c, g, w, first, last, scale, parity, step, so=0, edges=False):
    shape = s.shape[2:]
    masks = (phases(shape, parity), phases(shape, parity + 1))
    z, j = iota(shape, 0), iota(shape, 1) & (HALF - 1)
    walls = [None] * 5
    if edges:
        walls = [None, None, z == shape[0] - 1, z == 0, None]
        ends = [j == jnp.where(m, 0, HALF - 1) for m in masks]

    def chunk(x, n):
        for col in range(2):
            others = [s[1 - col, x + k + so] for k in range(n)]
            others = list(zip(others, beside(others, masks[(first + col) % 2])))
            for k in range(n):
                m = (first + k + col) % 2
                centre = s[col, x + k + so]
                v, second = others[k]
                near = [
                    s[1 - col, x + k + so + 1],
                    s[1 - col, x + k + so - 1],
                    roll(v, -1, 0),
                    roll(v, 1, 0),
                    v,
                    second,
                ]
                wall = walls + [ends[m] if edges else None]
                near = [v if e is None else jnp.where(e, 0.0, v) for v, e in zip(near, wall)]
                betas = [centre + v for v in near]
                total = ((betas[0] + betas[1]) + (betas[2] + betas[3])) + (betas[4] + betas[5])
                inverse = jnp.where(centre > 0.0, 1.0 / total, 0.0)
                for d in range(6):
                    v = betas[d] * inverse
                    c[col, d, x + k] = v if wall[d] is None else jnp.where(wall[d], 0.0, v)
                g[col, x + k] = f[col, x + k] * (inverse * (2.0 * scale))
                w[col, x + k] = total * (0.5 / scale)

    stepped(chunk, first, last, step)


def relaxed_rb(v, second, c, g, col, x):
    low, centre, high = v
    a = c[col, 0, x] * high + c[col, 1, x] * low
    b = c[col, 2, x] * roll(centre, -1, 0) + c[col, 3, x] * roll(centre, 1, 0)
    d = c[col, 4, x] * centre + c[col, 5, x] * second
    return g[col, x] + ((a + b) + d)


def half_sweep_rb(u_ref, v_ref, c, g, col, first, last, parity, step, uo=0):
    mask = phases(v_ref.shape[1:], parity + first + col)

    def chunk(x, n):
        v = [v_ref[x + k + uo] for k in range(-1, n + 1)]
        seconds = beside(v[1:-1], mask)
        for k in range(n):
            u_ref[x + k + uo] = relaxed_rb(v[k : k + 3], seconds[k], c, g, col, x + k)

    stepped(chunk, first, last, step)


def residuals_rb(u, c, g, w, first, x, n, parity, uo=0):
    out = []
    for col in range(2):
        v = [u[1 - col, x + k + uo] for k in range(-1, n + 1)]
        seconds = beside(v[1:-1], phases(u.shape[2:], parity + first + col))
        new = [relaxed_rb(v[k : k + 3], seconds[k], c, g, col, x + k) for k in range(n)]
        out.append([w[col, x + k] * (new[k] - u[col, x + k + uo]) for k in range(n)])
    return out


def picked(v, matrix):
    matrix = matrix.astype(jnp.bfloat16)
    first = v.astype(jnp.bfloat16)
    rest = v - first.astype(F32)
    second = rest.astype(jnp.bfloat16)
    third = (rest - second.astype(F32)).astype(jnp.bfloat16)
    parts = [jnp.dot(x, matrix, preferred_element_type=F32) for x in (first, second, third)]
    return (parts[0] + parts[1]) + parts[2]


def permuted(v, back):
    k, l = iota((LANES, LANES), 0), iota((LANES, LANES), 1)
    if back:
        k, l = l, k
    return picked(v, jnp.where(k == jnp.where(l < HALF, 2 * l, 2 * (l - HALF) + 1), 1.0, 0.0))


def swapped_rows(v, parity):
    return jnp.where(phases(v.shape, parity), v, roll(v, HALF, 1))


def packed(planes, at, group):
    rows = planes[0].shape[0]
    groups = iota((rows, LANES), 1) >> 3
    out = jnp.zeros((rows, LANES), F32)
    for k, v in enumerate(planes):
        out = jnp.where(groups == group(k), roll(v, STRIP * group(k) - at, 1), out)
    return out


def high_group(k):
    return 2 * k


def low_group(k):
    return (2 * k + 7) % 16


def fill_rb(out, i, at, planes_ref, strips, k0, count, rows, step=4):
    number = rows.stop - rows.start
    lane = iota((number, LANES), 1)
    own = lane < HALF
    halo = jnp.logical_or(lane < HALF + STRIP, lane >= LANES - STRIP)

    def chunk(n, many):
        for m in range(many):
            v = planes_ref[n + m]
            shift = lax.rem(HALF + LANES - 2 * STRIP * lax.rem(n + m + k0, 8), LANES)
            for col in range(2):
                h = jnp.where(halo, pltpu.roll(strips(2 * i + col), shift, 1), 0.0)
                out[col, at + n + m, rows.start : rows.stop] = jnp.where(own, roll(v, HALF, 1) if col else v, h)
                if number < ZD:
                    out[col, at + n + m, : rows.start] = jnp.zeros((rows.start, LANES), F32)
                    out[col, at + n + m, rows.stop :] = jnp.zeros((ZD - rows.stop, LANES), F32)

    def body(n, carry):
        chunk(n * step, step)
        return carry

    lax.fori_loop(0, count // step, body, 0)
    if count % step:
        chunk(jnp.int32(count - count % step), count % step)


def fill_narrow(u, f, even, own, first, second):
    lane = iota((Z1, LANES), 1)
    for parts, at, count in (((second, first), 0, H1), ((own, own), H1, 8), ((first, second), H1 + 8, H1)):
        for k in range(count):
            v, h = [parts[0][i, k] if count == 8 else jnp.where(even, parts[0][i, k], parts[1][i, k]) for i in range(2)]
            u[at + k] = jnp.where(lane < HALF, v, roll(h, HALF, 1))
            f[at + k] = jnp.where(lane < HALF, roll(v, HALF, 1), h)


def call(kernel, out_shape, scratch, smem=0, cost=4):
    def run(*args):
        specs = [pl.BlockSpec(memory_space=pltpu.SMEM)] * smem
        specs += [pl.BlockSpec(memory_space=pltpu.VMEM)] * (len(args) - smem)
        return pl.pallas_call(
            kernel,
            out_shape=out_shape,
            in_specs=specs,
            out_specs=jax.tree.map(lambda _: pl.BlockSpec(memory_space=pltpu.VMEM), out_shape),
            scratch_shapes=scratch,
            compiler_params=pltpu.CompilerParams(vmem_limit_bytes=40 * 2**20),
            cost_estimate=pl.CostEstimate(flops=cost * 10**6, bytes_accessed=cost * 3 * 10**6, transcendentals=0),
        )(*args)

    return run


def vmem(*shape):
    return pltpu.VMEM(shape, F32)


def packing(in_ref, out_ref, lo_ref, hi_ref):
    for i in range(2):
        out_ref[i] = permuted(in_ref[i].reshape(256, LANES), False).reshape(16, 16, LANES)
        planes = [swapped_rows(out_ref[i, x], x) for x in range(16)]
        for x in range(16):
            out_ref[i, x] = planes[x]
        for col in range(2):
            for q in range(2):
                some = planes[8 * q : 8 * q + 8]
                lo_ref[2 * i + col, q] = packed(some, HALF * col, high_group)
                hi_ref[2 * i + col, q] = packed(some, HALF * col + HALF - STRIP, low_group)


def descend(e, b, lsn, lsf, lfn, lff, lb0, lb1, hsn, hsf, hfn, hff, hb0, hb1, top_out, s1_out, next_out, tile_out, s, f, c, g, w, u, q, fl, cl, gl, wl, ul, ql, t):
    every, some = slice(0, ZD), slice(8, ZD - 8)
    for i, out, ln, lf, hn, hf, near, deep in ((0, f, lfn, lff, hfn, hff, 3, 12), (1, s, lsn, lsf, hsn, hsf, NEAR, HD)):
        first = 16 - deep
        fill_rb(out, i, HD - deep, lf, lambda n: lb0[n], first, 8 - first, some)
        fill_rb(out, i, HD - 8, lf.at[8 - first :], lambda n: lb1[n, 8 : ZD - 8], 8, 8 - near, some)
        fill_rb(out, i, HD - near, ln, lambda n: lb1[n], 16 - near, near, every)
        for h in range(2):
            fill_rb(out, i, HD + 8 * h, e.at[i, 8 * h : 8 * h + 8], lambda n, h=h: b[n, h], 8 * h, 8, every)
        fill_rb(out, i, HD + 16, hn, lambda n: hb0[n], 0, near, every)
        fill_rb(out, i, HD + 16 + near, hf, lambda n: hb0[n, 8 : ZD - 8], near, 8 - near, some)
        fill_rb(out, i, HD + 24, hf.at[8 - near :], lambda n: hb1[n], 8, deep - 8, some)
    couplings_rb(s, f, c, g, w, 2, XD - 2, 1.0, 0, 4)
    red, black = u.at[0], u.at[1]
    half_sweep_rb(black, g.at[0], c, g, 1, 3, XD - 3, 0, 10)
    half_sweep_rb(red, black, c, g, 0, 4, XD - 4, 0, 12)
    half_sweep_rb(black, red, c, g, 1, 5, XD - 5, 0, 12)

    def residual_body(i, carry):
        r = residuals_rb(u, c, g, w, 6, 6 + 8 * i, 8, 0)
        for k in range(4):
            q[0, 4 * i + k + 3] = (r[0][2 * k] + r[0][2 * k + 1]) + (r[1][2 * k] + r[1][2 * k + 1])
        return carry

    lax.fori_loop(0, 4, residual_body, 0)
    nothing = jnp.zeros((ZD, LANES), F32)
    for i in (0, 1, 2, 19, 20, 21):
        q[0, i] = nothing

    def coefficient_body(i, carry):
        q[1, i] = (s[0, 2 * i] + s[0, 2 * i + 1]) + (s[1, 2 * i] + s[1, 2 * i + 1])
        return carry

    lax.fori_loop(0, X1, coefficient_body, 0)
    sl = s1_out
    for i, ref in enumerate((fl, sl)):
        ref[...] = 0.125 * (q[i, :, pl.ds(0, Z1, stride=2), :] + q[i, :, pl.ds(1, Z1, stride=2), :])

    def top_body(i, carry):
        for col in range(2):
            top_out[col, i] = s[col, HD - H0 + i, 8 : ZD - 8]
            top_out[2 + col, i] = f[col, HD - H0 + i, 8 : ZD - 8]
        top_out[4, i] = black[HD - H0 + i, 8 : ZD - 8]
        return carry

    lax.fori_loop(0, X0, top_body, 0)
    couplings(sl, fl, cl, gl, wl, 3, X1 - 3, 4.0, step=4)
    first_half_sweep(ul, gl, 3, X1 - 3, H1, step=8)
    half_sweep(ul, cl, gl, 4, X1 - 4, H1 + 1, step=14)
    half_sweep(ul, cl, gl, 5, X1 - 5, H1, step=12)
    half_sweep(ul, cl, gl, 6, X1 - 6, H1 + 1, step=10)
    r = residual_planes(ul, cl, gl, wl, H1, 8)
    own = iota((8, LANES), 1) < HALF
    for x in range(8):
        next_out[x] = jnp.where(own, ul[H1 + x, 8:16], roll(fl[H1 + x, 8:16], HALF, 1))
    for i in range(4):
        x = H1 + 2 * i
        ql[i, 0] = (r[2 * i] + r[2 * i + 1])[8:16]
        ql[i, 1] = sl[x, 8:16] + sl[x + 1, 8:16]
        for b in range(2):
            t[i, 4 * b : 4 * b + 4] = ql[i, b, pl.ds(0, 4, stride=2), :] + ql[i, b, pl.ds(1, 4, stride=2), :]
    k, l = iota((4 * LANES, LANES), 0), iota((4 * LANES, LANES), 1)
    cell = (k & (LANES - 1)) >> 1
    to = 32 * (k >> 7) + 16 * (cell & 1) + (cell >> 1)
    place = jnp.where(jnp.logical_and((k & HALF) == 0, l == to), 0.125, 0.0)
    total = picked(jnp.concatenate([t[i] for i in range(4)], 1), place)
    group = iota((8, LANES), 1) // 16
    other = jnp.where(group % 2 == 0, roll(total, -16, 1), roll(total, 16, 1))
    tile_out[...] = jnp.where((group // 2 + iota((8, LANES), 0)) % 2 == 0, total, other)


def coarse(where_ref, mine_ref, other_ref, out_ref, s2, f2, c2, g2, w2, u2, q2, d2, s3, f3, c3, g3, w3, u3, q3, d3, s4, f4, c4, g4, w4):
    lane = iota((8, LANES), 1)
    wide = iota((32, LANES), 1)
    zero2 = jnp.zeros((32, LANES), F32)
    core = lax.rem(where_ref[0], 2)

    def transposed(groups):
        for s in (1, 2, 4):
            upper = (lane & (16 * s)) != 0
            for tiles in groups:
                for m in range(8):
                    if not m & s:
                        a, b = tiles[m], tiles[m + s]
                        tiles[m] = jnp.where(upper, roll(b, 16 * s, 1), a)
                        tiles[m + s] = jnp.where(upper, b, roll(a, -16 * s, 1))
        return groups

    def assemble(xcl, carry):
        for all_ref, c in ((mine_ref, core), (other_ref, 1 - core)):
            plane = 4 * (2 * xcl + c)
            groups = []
            for zi in range(8):
                at = [((2 * xh + xcl) * 4 + iy) * 8 + zi for xh in range(2) for iy in range(4)]
                groups.append([all_ref[i] for i in at])
            for zi, tiles in enumerate(transposed(groups)):
                rows = slice(8 * (zi // 2), 8 * (zi // 2) + 8)
                for g, v in enumerate(tiles):
                    if zi % 2 == 0:
                        f2[g % 2, plane + g // 2, rows] = v
                    else:
                        s2[g % 2, plane + g // 2 + 1, rows] = v
        return carry

    lax.fori_loop(0, 2, assemble, 0)

    def wrap(ref):
        ref[0] = jnp.where(wide < HALF, 0.0, roll(ref[16], HALF, 1))
        ref[17] = jnp.where(wide < HALF, roll(ref[1], HALF, 1), 0.0)

    for col in range(2):
        wrap(s2.at[col])
    for x in (0, 17):
        s3[x] = zero2[:16]
        u3[x] = zero2[:16]
    for x in (0, 9):
        s4[x] = zero2[:8]

    red, black = u2.at[0], u2.at[1]

    def sweep2(col):
        half_sweep_rb(u2.at[col], u2.at[1 - col], c2, g2, col, 0, 16, 0, 16, 1)
        wrap(u2.at[col])

    couplings_rb(s2, f2, c2, g2, w2, 0, 16, 16.0, 0, 4, 1, True)
    for x in range(16):
        red[x + 1] = g2[0, x]
    wrap(red)
    sweep2(1)
    sweep2(0)
    sweep2(1)

    def restrict2(i, carry):
        r = residuals_rb(u2, c2, g2, w2, 0, 8 * i, 8, 0, 1)
        for k in range(4):
            x = 8 * i + 2 * k + 1
            q2[0, 4 * i + k] = (r[0][2 * k] + r[0][2 * k + 1]) + (r[1][2 * k] + r[1][2 * k + 1])
            q2[1, 4 * i + k] = (s2[0, x] + s2[0, x + 1]) + (s2[1, x] + s2[1, x + 1])
        return carry

    lax.fori_loop(0, 2, restrict2, 0)
    narrow = iota((16, LANES), 1) < HALF
    for i, ref, at in ((0, f3, 0), (1, s3, 1)):
        for x in range(8):
            v = 0.125 * (q2[i, x, pl.ds(0, 16, stride=2), :] + q2[i, x, pl.ds(1, 16, stride=2), :])
            ref[x + at] = jnp.where(narrow, v, 0.0)
            ref[x + at + 8] = jnp.where(narrow, roll(v, HALF, 1), 0.0)
    couplings(s3, f3, c3, g3, w3, 0, 16, 64.0, so=1, edges=True, step=8)
    first_half_sweep(u3, g3, 0, 16, 0, 1, 16)
    for col in (1, 0, 1):
        half_sweep(u3, c3, g3, 0, 16, col, 1, 16)
    r = residual_planes(u3, c3, g3, w3, 0, 16, 1)
    for i in range(8):
        q3[0, i] = r[2 * i] + r[2 * i + 1]
        q3[1, i] = s3[2 * i + 1] + s3[2 * i + 2]
    lane4 = iota((8, LANES), 1)
    for i, ref, at in ((0, f4, 0), (1, s4, 1)):
        for x in range(8):
            v = 0.125 * (q3[i, x, pl.ds(0, 8, stride=2), :] + q3[i, x, pl.ds(1, 8, stride=2), :])
            ref[x + at] = jnp.where((lane4 & 1) == 0, v + roll(v, -1, 1), 0.0)
    couplings(s4, f4, c4, g4, w4, 0, 8, 256.0, so=1, edges=True, step=8, lanes=2)
    odd = (iota((8, LANES), 0) + (lane4 >> 1)) & 1
    masks = (odd == 0, odd == 1)
    nothing = jnp.zeros((8, LANES), F32)
    u4 = [jnp.where(masks[x % 2], g4[x], 0.0) for x in range(8)]
    for h in range(1, 2 * BOTTOM):
        around = [nothing] + u4 + [nothing]
        u4 = [jnp.where(masks[(x + h) % 2], relaxed(around[x : x + 3], c4, g4, x, 2), u4[x]) for x in range(8)]
    for x in range(8):
        v = u4[x] + roll(u4[x], 1, 1)
        d3[x, pl.ds(0, 8, stride=2), :] = v
        d3[x, pl.ds(1, 8, stride=2), :] = v
    for x in range(16):
        u3[x + 1] = u3[x + 1] + d3[x // 2]
    for col in (0, 1) * NU:
        half_sweep(u3, c3, g3, 0, 16, col, 1, 16)
    for x in range(8):
        v = jnp.where(narrow, u3[x + 1], roll(u3[x + 9], HALF, 1))
        d2[x, pl.ds(0, 16, stride=2), :] = v
        d2[x, pl.ds(1, 16, stride=2), :] = v
    for x in range(16):
        black[x + 1] = black[x + 1] + d2[x // 2]
    wrap(black)
    for _ in range(NU):
        sweep2(0)
        sweep2(1)
    ix, iy, iz = where_ref[0], where_ref[1], where_ref[2]
    down_z = lax.rem(36 - 4 * iz, 32)
    for n in range(12):
        x = 4 * ix + 12 + n
        at = lax.rem(x, 16) + 1
        shift = lax.rem(4 * LANES - HALF * (x // 16) - 16 * iy + HALF, LANES)
        for col in range(2):
            v = pltpu.roll(u2[col, at], down_z, 0)
            out_ref[col, n] = pltpu.roll(v[:16], shift, 1)


def ascend(where_ref, top, sl, m, ma, mb, win, u_out, r_out, c, g, w, u, d0, fl, cl, gl, wl, ul, t1, d1):
    fill_narrow(ul, fl, lax.rem(where_ref[0], 2) == 0, m, ma, mb)
    couplings(sl, fl, cl, gl, wl, 1, X1 - 1, 4.0, step=4)
    k, l = iota((2 * LANES, LANES), 0), iota((2 * LANES, LANES), 1)
    from_lane = jnp.where(l < 96, l >> 2, 96 + (l >> 2))
    widen = jnp.where(k == from_lane + LANES * ((l >> 1) & 1), 1.0, 0.0)
    parity = iota((1, 16, LANES), 1) + iota((12, 16, LANES), 0)
    v = [win[0], win[1]]
    both = [jnp.where((parity & 1) == 0, v[i], v[1 - i]).reshape(192, LANES) for i in range(2)]
    t1[...] = picked(jnp.concatenate(both, 1), widen).reshape(12, 16, LANES)
    d1[:, pl.ds(0, 12, stride=2), :] = t1[:, :12]
    d1[:, pl.ds(1, 12, stride=2), :] = t1[:, :12]
    for x in range(X1):
        ul[x] = jnp.where(sl[x] > 0.0, ul[x] + d1[(x + 1) // 2], 0.0)
    half_sweep(ul, cl, gl, 1, X1 - 1, H1, step=10)
    half_sweep(ul, cl, gl, 2, X1 - 2, H1 + 1, step=18)
    half_sweep(ul, cl, gl, 3, X1 - 3, H1, step=16)
    half_sweep(ul, cl, gl, 4, X1 - 4, H1 + 1, step=14)
    s, f, black, red = top.at[0:2], top.at[2:4], u.at[1], u.at[0]
    couplings_rb(s, f, c, g, w, 1, X0 - 1, 1.0, 1, 6)
    fine = ul[4:18, 4:20]
    d0[:, pl.ds(0, 16, stride=2), :] = fine
    d0[:, pl.ds(1, 16, stride=2), :] = fine
    for x in range(X0):
        black[x] = jnp.where(top[1, x] > 0.0, top[4, x] + d0[(x + 1) // 2], 0.0)
    half_sweep_rb(red, black, c, g, 0, 1, X0 - 1, 1, 12)
    half_sweep_rb(black, red, c, g, 1, 2, X0 - 2, 1, 12)
    half_sweep_rb(red, black, c, g, 0, 3, X0 - 3, 1, 10)
    half_sweep_rb(black, red, c, g, 1, 4, X0 - 4, 1, 18)

    lane = iota((16, LANES), 1)

    def body(i, carry):
        x = H0 + 8 * i
        r = residuals_rb(u, c, g, w, H0, x, 8, 1)
        for j in range(8):
            for out, a, b in ((u_out, u[0, x + j], u[1, x + j]), (r_out, r[0][j], r[1][j])):
                both = jnp.where(lane < HALF, a[8:24], roll(b[8:24], HALF, 1))
                out[8 * i + j] = swapped_rows(both, j)
        return carry

    lax.fori_loop(0, 2, body, 0)
    for out in (u_out, r_out):
        out[...] = permuted(out[...].reshape(256, LANES), True).reshape(16, 16, LANES)


def axis_of(name):
    return ("xc", "co") if name == "gx" else name


def exchange(low, high, name):
    axis = axis_of(name)
    count = lax.axis_size(axis)
    even = lax.axis_index(axis) % 2 == 0
    first = [(i, i ^ 1) for i in range(count)]
    second = [(i, i + 1) for i in range(1, count - 1, 2)]
    second += [(j, i) for i, j in second]
    a = lax.ppermute(jnp.where(even, high, low), axis, first)
    b = lax.ppermute(jnp.where(even, low, high), axis, second)
    return a, b


def swap(low, high, name):
    even = lax.axis_index(axis_of(name)) % 2 == 0
    a, b = exchange(low, high, name)
    return jnp.where(even, b, a), jnp.where(even, a, b)


def join(pieces):
    return jnp.concatenate([p.reshape(-1, 8, LANES) for p in pieces], 0)


def split(joined, like):
    out, at = [], 0
    for p in like:
        n = p.size // (8 * LANES)
        out.append(joined[at : at + n].reshape(p.shape))
        at += n
    return out


def swap_many(lows, highs, axis):
    low, high = swap(join(lows), join(highs), axis)
    return split(low, lows), split(high, highs)


def extend_wide(field, lo, hi):
    below, above = swap(lo, hi, "gy")
    group = lax.broadcasted_iota(jnp.int32, lo.shape, 3) // STRIP
    strips = jnp.where(group % 2 == 0, above, below)
    pieces = [field, strips]
    lows, highs = swap_many(pieces, pieces, "gz")
    field, strips = [jnp.concatenate(v, v[0].ndim - 2) for v in zip(lows, pieces, highs)]
    some = slice(8, ZD - 8)
    f, s = field[0], field[1]
    first = [s[:NEAR], s[NEAR:HD, some], f[:3], f[3:12, some], strips[:, 0], strips[:, 1, some]]
    last = [s[-NEAR:], s[-HD:-NEAR, some], f[-3:], f[-12:-3, some], strips[:, 0, some], strips[:, 1]]
    low, high = swap(join(first), join(last), "gx")
    return [field, strips] + split(low, last) + split(high, first)


def extend_narrow(own):
    below, above = swap(own, own, "gy")
    lane = lax.broadcasted_iota(jnp.int32, own.shape, 2)
    own = jnp.stack([own, jnp.where(lane % HALF < HALF // 2, above, below)])
    low, high = swap(own, own, "gz")
    own = jnp.concatenate([low, own, high], 2)
    return (own,) + exchange(own[:, :H1], own[:, -H1:], "gx")


def spread(x, axes, sizes):
    n = 1
    for a in axes:
        n *= sizes[a]
    return lax.all_to_all(jnp.broadcast_to(x[None], (n,) + x.shape), axes, 0, 0)


def level_scratch(planes, rows):
    p = (planes, rows, LANES)
    return [vmem(*p), vmem(*p), vmem(6, *p), vmem(*p), vmem(*p), vmem(*p)]


def rb_scratch(planes, rows, count):
    p = (planes, rows, LANES)
    return ([vmem(2, *p)] * 6)[: count - 4] + [vmem(2, 6, *p)] + [vmem(2, *p)] * 3


def full_scratch(n, uo):
    p = (n, LANES)
    return [vmem(n + 2, *p), vmem(n, *p), vmem(6, n, *p), vmem(n, *p), vmem(n, *p), vmem(n + 2 * uo, *p)]


def shape(*dims):
    return jax.ShapeDtypeStruct(dims, F32)


def on_device(sizes, right_side, sigma):
    field, lo, hi = call(packing, [shape(2, 16, 16, LANES), shape(4, 2, 16, LANES), shape(4, 2, 16, LANES)], [])(jnp.stack([right_side, sigma]))
    top, s1, next1, tile = call(
        descend,
        [shape(5, X0, Z0, LANES), shape(X1, Z1, LANES), shape(8, 8, LANES), shape(8, LANES)],
        rb_scratch(XD, ZD, 6)
        + [vmem(2, X1, ZD, LANES)]
        + level_scratch(X1, Z1)[1:]
        + [vmem(4, 2, 8, LANES), vmem(4, 8, LANES)],
    )(*extend_wide(field, lo, hi))
    narrow = extend_narrow(next1)
    tiles = spread(tile, ("xc", "gy", "gz"), sizes)
    mine = tiles.reshape(-1, 4, 2, 2, 4, LANES).transpose(0, 1, 3, 2, 4, 5).reshape(-1, 8, LANES)
    other = lax.ppermute(mine, "co", [(0, 1), (1, 0)])
    place = jnp.stack([lax.axis_index(axis_of("gx")), lax.axis_index("gy"), lax.axis_index("gz")]).astype(jnp.int32)
    window = call(
        coarse,
        shape(2, 12, 16, LANES),
        [vmem(2, 18, 32, LANES)]
        + rb_scratch(16, 32, 5)[:-1]
        + [vmem(2, 18, 32, LANES), vmem(2, 8, 32, LANES), vmem(8, 32, LANES)]
        + full_scratch(16, 1)
        + [vmem(2, 8, 16, LANES), vmem(8, 16, LANES)]
        + full_scratch(8, 1)[:-1],
        smem=1,
        cost=10,
    )(place, mine, other)
    return call(
        ascend,
        (shape(16, 16, LANES), shape(16, 16, LANES)),
        rb_scratch(X0, Z0, 4)
        + [vmem(14, Z0, LANES)]
        + level_scratch(X1, Z1)[1:]
        + [vmem(12, 16, LANES), vmem(12, Z1, LANES)],
        smem=1,
    )(place, top, s1, *narrow, window)


def solution(mesh):
    names, dims = list(mesh.axis_names), list(mesh.devices.shape)
    at = names.index("gx")
    fine = jax.sharding.Mesh(
        mesh.devices.reshape(dims[:at] + [dims[at] // 2, 2] + dims[at + 1 :]),
        names[:at] + ["xc", "co"] + names[at + 1 :],
    )
    placed = P(("xc", "co"), "gz", "gy")
    return jax.shard_map(
        functools.partial(on_device, dict(fine.shape)),
        mesh=fine,
        in_specs=(placed, placed),
        out_specs=(placed, placed),
        check_vma=False,
    )
```

```python
import functools

import jax
import jax.numpy as jnp
from jax import lax
from jax.experimental import pallas as pl
from jax.experimental.pallas import tpu as pltpu
from jax.sharding import PartitionSpec as P

NU = 2
BOTTOM = 8
F32 = jnp.float32
LANES = 128
STRIP = 8

HD, XD, ZD = 14, 44, 48
NEAR = 5
H0, X0, Z0 = 5, 26, 32
HALF = LANES // 2
H1, X1, Z1 = 7, 22, 24


def roll(v, shift, axis):
    return pltpu.roll(v, shift % v.shape[axis], axis)


def iota(shape, axis):
    return lax.broadcasted_iota(jnp.int32, shape, axis)


def reds(shape, parity):
    return ((iota(shape, 0) + iota(shape, 1)) & 1) == parity % 2


def couplings(s_ref, f_ref, c_ref, g_ref, w_ref, first, last, scale, so=0, edges=False, step=1, lanes=1):
    shape = s_ref.shape[1:]
    if edges:
        z = iota(shape, 0)
        walls = (None, None, z == shape[0] - 1, z == 0, None, None)

    def chunk(x, n):
        s = [s_ref[x + so + k] for k in range(-1, n + 1)]
        for k in range(n):
            centre = s[k + 1]
            near = [
                s[k + 2],
                s[k],
                roll(centre, -1, 0),
                roll(centre, 1, 0),
                roll(centre, -lanes, 1),
                roll(centre, lanes, 1),
            ]
            if edges:
                near = [v if wall is None else jnp.where(wall, 0.0, v) for v, wall in zip(near, walls)]
            betas = [centre + v for v in near]
            total = ((betas[0] + betas[1]) + (betas[2] + betas[3])) + (betas[4] + betas[5])
            inverse = jnp.where(centre > 0.0, 1.0 / total, 0.0)
            for d in range(6):
                c = betas[d] * inverse
                if edges and walls[d] is not None:
                    c = jnp.where(walls[d], 0.0, c)
                c_ref[d, x + k] = c
            g_ref[x + k] = f_ref[x + k] * (inverse * (2.0 * scale))
            w_ref[x + k] = total * (0.5 / scale)

    stepped(chunk, first, last, step)


def stepped(chunk, first, last, step):
    count, rest = divmod(last - first, step)
    if count == 1:
        chunk(first, step)
    elif count:

        def body(i, carry):
            chunk(first + i * step, step)
            return carry

        lax.fori_loop(0, count, body, 0)
    if rest:
        chunk(last - rest, rest)


def relaxed(u, c_ref, g_ref, x, lanes=1):
    low, centre, high = u
    a = c_ref[0, x] * high + c_ref[1, x] * low
    b = c_ref[2, x] * roll(centre, -1, 0) + c_ref[3, x] * roll(centre, 1, 0)
    d = c_ref[4, x] * roll(centre, -lanes, 1) + c_ref[5, x] * roll(centre, lanes, 1)
    return g_ref[x] + ((a + b) + d)


def half_sweep(u_ref, c_ref, g_ref, first, last, parity, uo=0, step=4):
    shape = u_ref.shape[1:]
    masks = (reds(shape, parity + first), reds(shape, parity + first + 1))

    def chunk(x, n):
        u = [u_ref[x + uo + k] for k in range(-1, n + 1)]
        new = [jnp.where(masks[k % 2], relaxed(u[k : k + 3], c_ref, g_ref, x + k), u[k + 1]) for k in range(n)]
        for k in range(n):
            u_ref[x + uo + k] = new[k]

    stepped(chunk, first, last, step)


def first_half_sweep(u_ref, g_ref, first, last, parity, uo=0, step=4):
    shape = u_ref.shape[1:]
    masks = (reds(shape, parity + first), reds(shape, parity + first + 1))

    def chunk(x, n):
        for k in range(n):
            u_ref[x + uo + k] = jnp.where(masks[k % 2], g_ref[x + k], 0.0)

    stepped(chunk, first, last, step)


def residual_planes(u_ref, c_ref, g_ref, w_ref, x, n, uo=0):
    u = [u_ref[x + uo + k] for k in range(-1, n + 1)]
    return [w_ref[x + k] * (relaxed(u[k : k + 3], c_ref, g_ref, x + k) - u[k + 1]) for k in range(n)]


def phases(shape, parity):
    return (iota(shape, 0) & 1) == parity % 2


def beside(planes, below):
    out = []
    for a, b in zip(planes[0::2], planes[1::2]):
        lower = roll(jnp.where(below, a, b), 1, 1)
        upper = roll(jnp.where(below, b, a), -1, 1)
        out += [jnp.where(below, lower, upper), jnp.where(below, upper, lower)]
    return out


def couplings_rb(s, f, c, g, w, first, last, scale, parity, step, so=0, edges=False):
    shape = s.shape[2:]
    masks = (phases(shape, parity), phases(shape, parity + 1))
    z, j = iota(shape, 0), iota(shape, 1) & (HALF - 1)
    walls = [None] * 5
    if edges:
        walls = [None, None, z == shape[0] - 1, z == 0, None]
        ends = [j == jnp.where(m, 0, HALF - 1) for m in masks]

    def chunk(x, n):
        for col in range(2):
            others = [s[1 - col, x + k + so] for k in range(n)]
            others = list(zip(others, beside(others, masks[(first + col) % 2])))
            for k in range(n):
                m = (first + k + col) % 2
                centre = s[col, x + k + so]
                v, second = others[k]
                near = [
                    s[1 - col, x + k + so + 1],
                    s[1 - col, x + k + so - 1],
                    roll(v, -1, 0),
                    roll(v, 1, 0),
                    v,
                    second,
                ]
                wall = walls + [ends[m] if edges else None]
                near = [v if e is None else jnp.where(e, 0.0, v) for v, e in zip(near, wall)]
                betas = [centre + v for v in near]
                total = ((betas[0] + betas[1]) + (betas[2] + betas[3])) + (betas[4] + betas[5])
                inverse = jnp.where(centre > 0.0, 1.0 / total, 0.0)
                for d in range(6):
                    v = betas[d] * inverse
                    c[col, d, x + k] = v if wall[d] is None else jnp.where(wall[d], 0.0, v)
                g[col, x + k] = f[col, x + k] * (inverse * (2.0 * scale))
                w[col, x + k] = total * (0.5 / scale)

    stepped(chunk, first, last, step)


def relaxed_rb(v, second, c, g, col, x):
    low, centre, high = v
    a = c[col, 0, x] * high + c[col, 1, x] * low
    b = c[col, 2, x] * roll(centre, -1, 0) + c[col, 3, x] * roll(centre, 1, 0)
    d = c[col, 4, x] * centre + c[col, 5, x] * second
    return g[col, x] + ((a + b) + d)


def half_sweep_rb(u_ref, v_ref, c, g, col, first, last, parity, step, uo=0):
    mask = phases(v_ref.shape[1:], parity + first + col)

    def chunk(x, n):
        v = [v_ref[x + k + uo] for k in range(-1, n + 1)]
        seconds = beside(v[1:-1], mask)
        for k in range(n):
            u_ref[x + k + uo] = relaxed_rb(v[k : k + 3], seconds[k], c, g, col, x + k)

    stepped(chunk, first, last, step)


def residuals_rb(u, c, g, w, first, x, n, parity, uo=0):
    out = []
    for col in range(2):
        v = [u[1 - col, x + k + uo] for k in range(-1, n + 1)]
        seconds = beside(v[1:-1], phases(u.shape[2:], parity + first + col))
        new = [relaxed_rb(v[k : k + 3], seconds[k], c, g, col, x + k) for k in range(n)]
        out.append([w[col, x + k] * (new[k] - u[col, x + k + uo]) for k in range(n)])
    return out


def picked(v, matrix):
    matrix = matrix.astype(jnp.bfloat16)
    first = v.astype(jnp.bfloat16)
    rest = v - first.astype(F32)
    second = rest.astype(jnp.bfloat16)
    third = (rest - second.astype(F32)).astype(jnp.bfloat16)
    parts = [jnp.dot(x, matrix, preferred_element_type=F32) for x in (first, second, third)]
    return (parts[0] + parts[1]) + parts[2]


def permuted(v, back):
    k, l = iota((LANES, LANES), 0), iota((LANES, LANES), 1)
    if back:
        k, l = l, k
    return picked(v, jnp.where(k == jnp.where(l < HALF, 2 * l, 2 * (l - HALF) + 1), 1.0, 0.0))


def swapped_rows(v, parity):
    return jnp.where(phases(v.shape, parity), v, roll(v, HALF, 1))


def packed(planes, at, group):
    rows = planes[0].shape[0]
    groups = iota((rows, LANES), 1) >> 3
    out = jnp.zeros((rows, LANES), F32)
    for k, v in enumerate(planes):
        out = jnp.where(groups == group(k), roll(v, STRIP * group(k) - at, 1), out)
    return out


def high_group(k):
    return 2 * k


def low_group(k):
    return (2 * k + 7) % 16


def fill_rb(out, i, at, planes_ref, strips, k0, count, rows, step=8):
    number = rows.stop - rows.start
    lane = iota((number, LANES), 1)
    own = lane < HALF
    halo = jnp.logical_or(lane < HALF + STRIP, lane >= LANES - STRIP)

    def chunk(n, many):
        for m in range(many):
            v = planes_ref[n + m]
            shift = lax.rem(HALF + LANES - 2 * STRIP * lax.rem(n + m + k0, 8), LANES)
            for col in range(2):
                h = jnp.where(halo, pltpu.roll(strips(2 * i + col), shift, 1), 0.0)
                out[col, at + n + m, rows.start : rows.stop] = jnp.where(own, roll(v, HALF, 1) if col else v, h)
                if number < ZD:
                    out[col, at + n + m, : rows.start] = jnp.zeros((rows.start, LANES), F32)
                    out[col, at + n + m, rows.stop :] = jnp.zeros((ZD - rows.stop, LANES), F32)

    def body(n, carry):
        chunk(n * step, step)
        return carry

    lax.fori_loop(0, count // step, body, 0)
    if count % step:
        chunk(jnp.int32(count - count % step), count % step)


def fill_narrow(u, f, even, own, first, second):
    lane = iota((Z1, LANES), 1)
    for parts, at, count in (((second, first), 0, H1), ((own, own), H1, 8), ((first, second), H1 + 8, H1)):
        for k in range(count):
            v, h = [parts[0][i, k] if count == 8 else jnp.where(even, parts[0][i, k], parts[1][i, k]) for i in range(2)]
            u[at + k] = jnp.where(lane < HALF, v, roll(h, HALF, 1))
            f[at + k] = jnp.where(lane < HALF, roll(v, HALF, 1), h)


def call(kernel, out_shape, scratch, smem=0, cost=4):
    def run(*args):
        specs = [pl.BlockSpec(memory_space=pltpu.SMEM)] * smem
        specs += [pl.BlockSpec(memory_space=pltpu.VMEM)] * (len(args) - smem)
        return pl.pallas_call(
            kernel,
            out_shape=out_shape,
            in_specs=specs,
            out_specs=jax.tree.map(lambda _: pl.BlockSpec(memory_space=pltpu.VMEM), out_shape),
            scratch_shapes=scratch,
            compiler_params=pltpu.CompilerParams(vmem_limit_bytes=40 * 2**20),
            cost_estimate=pl.CostEstimate(flops=cost * 10**6, bytes_accessed=cost * 3 * 10**6, transcendentals=0),
        )(*args)

    return run


def vmem(*shape):
    return pltpu.VMEM(shape, F32)


def packing(in_ref, out_ref, lo_ref, hi_ref):
    for i in range(2):
        out_ref[i] = permuted(in_ref[i].reshape(256, LANES), False).reshape(16, 16, LANES)
        planes = [swapped_rows(out_ref[i, x], x) for x in range(16)]
        for x in range(16):
            out_ref[i, x] = planes[x]
        for col in range(2):
            for q in range(2):
                some = planes[8 * q : 8 * q + 8]
                lo_ref[2 * i + col, q] = packed(some, HALF * col, high_group)
                hi_ref[2 * i + col, q] = packed(some, HALF * col + HALF - STRIP, low_group)


def descend(e, b, lsn, lsf, lfn, lff, lb0, lb1, hsn, hsf, hfn, hff, hb0, hb1, top_out, s1_out, next_out, tile_out, s, f, c, g, w, u, q, fl, cl, gl, wl, ul, ql, t):
    every, some = slice(0, ZD), slice(8, ZD - 8)
    for i, out, ln, lf, hn, hf, near, deep in ((0, f, lfn, lff, hfn, hff, 3, 12), (1, s, lsn, lsf, hsn, hsf, NEAR, HD)):
        first = 16 - deep
        fill_rb(out, i, HD - deep, lf, lambda n: lb0[n], first, 8 - first, some)
        fill_rb(out, i, HD - 8, lf.at[8 - first :], lambda n: lb1[n, 8 : ZD - 8], 8, 8 - near, some)
        fill_rb(out, i, HD - near, ln, lambda n: lb1[n], 16 - near, near, every)
        for h in range(2):
            fill_rb(out, i, HD + 8 * h, e.at[i, 8 * h : 8 * h + 8], lambda n, h=h: b[n, h], 8 * h, 8, every)
        fill_rb(out, i, HD + 16, hn, lambda n: hb0[n], 0, near, every)
        fill_rb(out, i, HD + 16 + near, hf, lambda n: hb0[n, 8 : ZD - 8], near, 8 - near, some)
        fill_rb(out, i, HD + 24, hf.at[8 - near :], lambda n: hb1[n], 8, deep - 8, some)
    couplings_rb(s, f, c, g, w, 2, XD - 2, 1.0, 0, 4)
    red, black = u.at[0], u.at[1]
    half_sweep_rb(black, g.at[0], c, g, 1, 3, XD - 3, 0, 10)
    half_sweep_rb(red, black, c, g, 0, 4, XD - 4, 0, 12)
    half_sweep_rb(black, red, c, g, 1, 5, XD - 5, 0, 12)

    def residual_body(i, carry):
        r = residuals_rb(u, c, g, w, 6, 6 + 8 * i, 8, 0)
        for k in range(4):
            q[0, 4 * i + k + 3] = (r[0][2 * k] + r[0][2 * k + 1]) + (r[1][2 * k] + r[1][2 * k + 1])
        return carry

    lax.fori_loop(0, 4, residual_body, 0)
    nothing = jnp.zeros((ZD, LANES), F32)
    for i in (0, 1, 2, 19, 20, 21):
        q[0, i] = nothing

    def coefficient_body(i, carry):
        q[1, i] = (s[0, 2 * i] + s[0, 2 * i + 1]) + (s[1, 2 * i] + s[1, 2 * i + 1])
        return carry

    lax.fori_loop(0, X1, coefficient_body, 0)
    sl = s1_out
    for i, ref in enumerate((fl, sl)):
        ref[...] = 0.125 * (q[i, :, pl.ds(0, Z1, stride=2), :] + q[i, :, pl.ds(1, Z1, stride=2), :])

    def top_body(i, carry):
        for col in range(2):
            top_out[col, i] = s[col, HD - H0 + i, 8 : ZD - 8]
            top_out[2 + col, i] = f[col, HD - H0 + i, 8 : ZD - 8]
        top_out[4, i] = black[HD - H0 + i, 8 : ZD - 8]
        return carry

    lax.fori_loop(0, X0, top_body, 0)
    couplings(sl, fl, cl, gl, wl, 3, X1 - 3, 4.0, step=8)
    first_half_sweep(ul, gl, 3, X1 - 3, H1, step=8)
    half_sweep(ul, cl, gl, 4, X1 - 4, H1 + 1, step=8)
    half_sweep(ul, cl, gl, 5, X1 - 5, H1, step=12)
    half_sweep(ul, cl, gl, 6, X1 - 6, H1 + 1, step=10)
    r = residual_planes(ul, cl, gl, wl, H1, 8)
    own = iota((8, LANES), 1) < HALF
    for x in range(8):
        next_out[x] = jnp.where(own, ul[H1 + x, 8:16], roll(fl[H1 + x, 8:16], HALF, 1))
    for i in range(4):
        x = H1 + 2 * i
        ql[i, 0] = (r[2 * i] + r[2 * i + 1])[8:16]
        ql[i, 1] = sl[x, 8:16] + sl[x + 1, 8:16]
        for b in range(2):
            t[i, 4 * b : 4 * b + 4] = ql[i, b, pl.ds(0, 4, stride=2), :] + ql[i, b, pl.ds(1, 4, stride=2), :]
    k, l = iota((4 * LANES, LANES), 0), iota((4 * LANES, LANES), 1)
    cell = (k & (LANES - 1)) >> 1
    to = 32 * (k >> 7) + 16 * (cell & 1) + (cell >> 1)
    place = jnp.where(jnp.logical_and((k & HALF) == 0, l == to), 0.125, 0.0)
    total = picked(jnp.concatenate([t[i] for i in range(4)], 1), place)
    group = iota((8, LANES), 1) // 16
    other = jnp.where(group % 2 == 0, roll(total, -16, 1), roll(total, 16, 1))
    tile_out[...] = jnp.where((group // 2 + iota((8, LANES), 0)) % 2 == 0, total, other)


def coarse(where_ref, mine_ref, other_ref, out_ref, s2, f2, c2, g2, w2, u2, q2, d2, s3, f3, c3, g3, w3, u3, q3, d3, s4, f4, c4, g4, w4):
    lane = iota((8, LANES), 1)
    wide = iota((32, LANES), 1)
    zero2 = jnp.zeros((32, LANES), F32)
    core, chip = lax.rem(where_ref[0], 2), where_ref[0] // 2

    def transposed(groups):
        for s in (1, 2, 4):
            upper = (lane & (16 * s)) != 0
            for tiles in groups:
                for m in range(8):
                    if not m & s:
                        a, b = tiles[m], tiles[m + s]
                        tiles[m] = jnp.where(upper, roll(b, 16 * s, 1), a)
                        tiles[m + s] = jnp.where(upper, b, roll(a, -16 * s, 1))
        return groups

    def assemble(xcl, carry):
        for all_ref, c in ((mine_ref, core), (other_ref, 1 - core)):
            plane = 4 * (2 * xcl + c)
            groups = []
            for zi in range(8):
                at = [(lax.bitwise_xor(2 * xh + xcl, chip) * 4 + iy) * 8 + zi for xh in range(2) for iy in range(4)]
                groups.append([all_ref[i] for i in at])
            for zi, tiles in enumerate(transposed(groups)):
                rows = slice(8 * (zi // 2), 8 * (zi // 2) + 8)
                for g, v in enumerate(tiles):
                    if zi % 2 == 0:
                        f2[g % 2, plane + g // 2, rows] = v
                    else:
                        s2[g % 2, plane + g // 2 + 1, rows] = v
        return carry

    lax.fori_loop(0, 2, assemble, 0)

    def wrap(ref):
        ref[0] = jnp.where(wide < HALF, 0.0, roll(ref[16], HALF, 1))
        ref[17] = jnp.where(wide < HALF, roll(ref[1], HALF, 1), 0.0)

    for col in range(2):
        wrap(s2.at[col])
    for x in (0, 17):
        s3[x] = zero2[:16]
        u3[x] = zero2[:16]
    for x in (0, 9):
        s4[x] = zero2[:8]

    red, black = u2.at[0], u2.at[1]

    def sweep2(col):
        half_sweep_rb(u2.at[col], u2.at[1 - col], c2, g2, col, 0, 16, 0, 16, 1)
        wrap(u2.at[col])

    couplings_rb(s2, f2, c2, g2, w2, 0, 16, 16.0, 0, 4, 1, True)
    for x in range(16):
        red[x + 1] = g2[0, x]
    wrap(red)
    sweep2(1)
    sweep2(0)
    sweep2(1)

    def restrict2(i, carry):
        r = residuals_rb(u2, c2, g2, w2, 0, 8 * i, 8, 0, 1)
        for k in range(4):
            x = 8 * i + 2 * k + 1
            q2[0, 4 * i + k] = (r[0][2 * k] + r[0][2 * k + 1]) + (r[1][2 * k] + r[1][2 * k + 1])
            q2[1, 4 * i + k] = (s2[0, x] + s2[0, x + 1]) + (s2[1, x] + s2[1, x + 1])
        return carry

    lax.fori_loop(0, 2, restrict2, 0)
    narrow = iota((16, LANES), 1) < HALF
    for i, ref, at in ((0, f3, 0), (1, s3, 1)):
        for x in range(8):
            v = 0.125 * (q2[i, x, pl.ds(0, 16, stride=2), :] + q2[i, x, pl.ds(1, 16, stride=2), :])
            ref[x + at] = jnp.where(narrow, v, 0.0)
            ref[x + at + 8] = jnp.where(narrow, roll(v, HALF, 1), 0.0)
    couplings(s3, f3, c3, g3, w3, 0, 16, 64.0, so=1, edges=True, step=8)
    first_half_sweep(u3, g3, 0, 16, 0, 1, 16)
    for col in (1, 0, 1):
        half_sweep(u3, c3, g3, 0, 16, col, 1, 16)
    r = residual_planes(u3, c3, g3, w3, 0, 16, 1)
    for i in range(8):
        q3[0, i] = r[2 * i] + r[2 * i + 1]
        q3[1, i] = s3[2 * i + 1] + s3[2 * i + 2]
    lane4 = iota((8, LANES), 1)
    for i, ref, at in ((0, f4, 0), (1, s4, 1)):
        for x in range(8):
            v = 0.125 * (q3[i, x, pl.ds(0, 8, stride=2), :] + q3[i, x, pl.ds(1, 8, stride=2), :])
            ref[x + at] = jnp.where((lane4 & 1) == 0, v + roll(v, -1, 1), 0.0)
    couplings(s4, f4, c4, g4, w4, 0, 8, 256.0, so=1, edges=True, step=8, lanes=2)
    odd = (iota((8, LANES), 0) + (lane4 >> 1)) & 1
    masks = (odd == 0, odd == 1)
    nothing = jnp.zeros((8, LANES), F32)
    u4 = [jnp.where(masks[x % 2], g4[x], 0.0) for x in range(8)]
    for h in range(1, 2 * BOTTOM):
        around = [nothing] + u4 + [nothing]
        u4 = [jnp.where(masks[(x + h) % 2], relaxed(around[x : x + 3], c4, g4, x, 2), u4[x]) for x in range(8)]
    for x in range(8):
        v = u4[x] + roll(u4[x], 1, 1)
        d3[x, pl.ds(0, 8, stride=2), :] = v
        d3[x, pl.ds(1, 8, stride=2), :] = v
    for x in range(16):
        u3[x + 1] = u3[x + 1] + d3[x // 2]
    for col in (0, 1) * NU:
        half_sweep(u3, c3, g3, 0, 16, col, 1, 16)
    for x in range(8):
        v = jnp.where(narrow, u3[x + 1], roll(u3[x + 9], HALF, 1))
        d2[x, pl.ds(0, 16, stride=2), :] = v
        d2[x, pl.ds(1, 16, stride=2), :] = v
    for x in range(16):
        black[x + 1] = black[x + 1] + d2[x // 2]
    wrap(black)
    for _ in range(NU):
        sweep2(0)
        sweep2(1)
    ix, iy, iz = where_ref[0], where_ref[1], where_ref[2]
    down_z = lax.rem(36 - 4 * iz, 32)
    for n in range(12):
        x = 4 * ix + 12 + n
        at = lax.rem(x, 16) + 1
        shift = lax.rem(4 * LANES - HALF * (x // 16) - 16 * iy + HALF, LANES)
        for col in range(2):
            v = pltpu.roll(u2[col, at], down_z, 0)
            out_ref[col, n] = pltpu.roll(v[:16], shift, 1)


def ascend(where_ref, top, sl, m, ma, mb, win, u_out, r_out, c, g, w, u, d0, fl, cl, gl, wl, ul, t1, d1):
    fill_narrow(ul, fl, lax.rem(where_ref[0], 2) == 0, m, ma, mb)
    couplings(sl, fl, cl, gl, wl, 1, X1 - 1, 4.0, step=20)
    k, l = iota((2 * LANES, LANES), 0), iota((2 * LANES, LANES), 1)
    from_lane = jnp.where(l < 96, l >> 2, 96 + (l >> 2))
    widen = jnp.where(k == from_lane + LANES * ((l >> 1) & 1), 1.0, 0.0)
    parity = iota((1, 16, LANES), 1) + iota((12, 16, LANES), 0)
    v = [win[0], win[1]]
    both = [jnp.where((parity & 1) == 0, v[i], v[1 - i]).reshape(192, LANES) for i in range(2)]
    t1[...] = picked(jnp.concatenate(both, 1), widen).reshape(12, 16, LANES)
    d1[:, pl.ds(0, 12, stride=2), :] = t1[:, :12]
    d1[:, pl.ds(1, 12, stride=2), :] = t1[:, :12]
    for x in range(X1):
        ul[x] = jnp.where(sl[x] > 0.0, ul[x] + d1[(x + 1) // 2], 0.0)
    half_sweep(ul, cl, gl, 1, X1 - 1, H1, step=10)
    half_sweep(ul, cl, gl, 2, X1 - 2, H1 + 1, step=18)
    half_sweep(ul, cl, gl, 3, X1 - 3, H1, step=16)
    half_sweep(ul, cl, gl, 4, X1 - 4, H1 + 1, step=14)
    s, f, black, red = top.at[0:2], top.at[2:4], u.at[1], u.at[0]
    couplings_rb(s, f, c, g, w, 1, X0 - 1, 1.0, 1, 4)
    fine = ul[4:18, 4:20]
    d0[:, pl.ds(0, 16, stride=2), :] = fine
    d0[:, pl.ds(1, 16, stride=2), :] = fine
    for x in range(X0):
        black[x] = jnp.where(top[1, x] > 0.0, top[4, x] + d0[(x + 1) // 2], 0.0)
    half_sweep_rb(red, black, c, g, 0, 1, X0 - 1, 1, 12)
    half_sweep_rb(black, red, c, g, 1, 2, X0 - 2, 1, 12)
    half_sweep_rb(red, black, c, g, 0, 3, X0 - 3, 1, 10)
    half_sweep_rb(black, red, c, g, 1, 4, X0 - 4, 1, 18)

    lane = iota((16, LANES), 1)

    def body(i, carry):
        x = H0 + 8 * i
        r = residuals_rb(u, c, g, w, H0, x, 8, 1)
        for j in range(8):
            for out, a, b in ((u_out, u[0, x + j], u[1, x + j]), (r_out, r[0][j], r[1][j])):
                both = jnp.where(lane < HALF, a[8:24], roll(b[8:24], HALF, 1))
                out[8 * i + j] = swapped_rows(both, j)
        return carry

    lax.fori_loop(0, 2, body, 0)
    for out in (u_out, r_out):
        out[...] = permuted(out[...].reshape(256, LANES), True).reshape(16, 16, LANES)


def axis_of(name):
    return ("xc", "co") if name == "gx" else name


def exchange(low, high, name):
    axis = axis_of(name)
    count = lax.axis_size(axis)
    even = lax.axis_index(axis) % 2 == 0
    first = [(i, i ^ 1) for i in range(count)]
    second = [(i, i + 1) for i in range(1, count - 1, 2)]
    second += [(j, i) for i, j in second]
    b = lax.ppermute(jnp.where(even, low, high), axis, second)
    a = lax.ppermute(jnp.where(even, high, low), axis, first)
    return a, b


def swap(low, high, name):
    even = lax.axis_index(axis_of(name)) % 2 == 0
    a, b = exchange(low, high, name)
    return jnp.where(even, b, a), jnp.where(even, a, b)


def join(pieces):
    return jnp.concatenate([p.reshape(-1, 8, LANES) for p in pieces], 0)


def split(joined, like):
    out, at = [], 0
    for p in like:
        n = p.size // (8 * LANES)
        out.append(joined[at : at + n].reshape(p.shape))
        at += n
    return out


def swap_many(lows, highs, axis):
    low, high = swap(join(lows), join(highs), axis)
    return split(low, lows), split(high, highs)


def extend_wide(field, lo, hi):
    below, above = swap(lo, hi, "gy")
    group = lax.broadcasted_iota(jnp.int32, lo.shape, 3) // STRIP
    strips = jnp.where(group % 2 == 0, above, below)
    pieces = [field, strips]
    lows, highs = swap_many(pieces, pieces, "gz")
    field, strips = [jnp.concatenate(v, v[0].ndim - 2) for v in zip(lows, pieces, highs)]
    some = slice(8, ZD - 8)
    f, s = field[0], field[1]
    first = [s[:NEAR], s[NEAR:HD, some], f[:3], f[3:12, some], strips[:, 0], strips[:, 1, some]]
    last = [s[-NEAR:], s[-HD:-NEAR, some], f[-3:], f[-12:-3, some], strips[:, 0, some], strips[:, 1]]
    low, high = swap(join(first), join(last), "gx")
    return [field, strips] + split(low, last) + split(high, first)


def extend_narrow(own):
    below, above = swap(own, own, "gy")
    lane = lax.broadcasted_iota(jnp.int32, own.shape, 2)
    own = jnp.stack([own, jnp.where(lane % HALF < HALF // 2, above, below)])
    low, high = swap(own, own, "gz")
    own = jnp.concatenate([low, own, high], 2)
    return (own,) + exchange(own[:, :H1], own[:, -H1:], "gx")


def spread(x, axes, sizes):
    n = 1
    for a in axes:
        n *= sizes[a]
    return lax.all_to_all(jnp.broadcast_to(x[None], (n,) + x.shape), axes, 0, 0)


def level_scratch(planes, rows):
    p = (planes, rows, LANES)
    return [vmem(*p), vmem(*p), vmem(6, *p), vmem(*p), vmem(*p), vmem(*p)]


def rb_scratch(planes, rows, count):
    p = (planes, rows, LANES)
    return ([vmem(2, *p)] * 6)[: count - 4] + [vmem(2, 6, *p)] + [vmem(2, *p)] * 3


def full_scratch(n, uo):
    p = (n, LANES)
    return [vmem(n + 2, *p), vmem(n, *p), vmem(6, n, *p), vmem(n, *p), vmem(n, *p), vmem(n + 2 * uo, *p)]


def shape(*dims):
    return jax.ShapeDtypeStruct(dims, F32)


def on_device(sizes, right_side, sigma):
    field, lo, hi = call(packing, [shape(2, 16, 16, LANES), shape(4, 2, 16, LANES), shape(4, 2, 16, LANES)], [])(jnp.stack([right_side, sigma]))
    top, s1, next1, tile = call(
        descend,
        [shape(5, X0, Z0, LANES), shape(X1, Z1, LANES), shape(8, 8, LANES), shape(8, LANES)],
        rb_scratch(XD, ZD, 6)
        + [vmem(2, X1, ZD, LANES)]
        + level_scratch(X1, Z1)[1:]
        + [vmem(4, 2, 8, LANES), vmem(4, 8, LANES)],
    )(*extend_wide(field, lo, hi))
    narrow = extend_narrow(next1)
    line = spread(tile, ("gy", "gz"), sizes)
    line = line.reshape(-1, 4, 2, 2, 4, LANES).transpose(0, 1, 3, 2, 4, 5).reshape(-1, 8, LANES)
    chips = sizes["xc"]
    mine = [line] + [lax.ppermute(line, "xc", [(i, i ^ k) for i in range(chips)]) for k in range(1, chips)]
    mine = jnp.concatenate(mine)
    other = lax.ppermute(mine, "co", [(0, 1), (1, 0)])
    place = jnp.stack([lax.axis_index(axis_of("gx")), lax.axis_index("gy"), lax.axis_index("gz")]).astype(jnp.int32)
    window = call(
        coarse,
        shape(2, 12, 16, LANES),
        [vmem(2, 18, 32, LANES)]
        + rb_scratch(16, 32, 5)[:-1]
        + [vmem(2, 18, 32, LANES), vmem(2, 8, 32, LANES), vmem(8, 32, LANES)]
        + full_scratch(16, 1)
        + [vmem(2, 8, 16, LANES), vmem(8, 16, LANES)]
        + full_scratch(8, 1)[:-1],
        smem=1,
        cost=10,
    )(place, mine, other)
    return call(
        ascend,
        (shape(16, 16, LANES), shape(16, 16, LANES)),
        rb_scratch(X0, Z0, 4)
        + [vmem(14, Z0, LANES)]
        + level_scratch(X1, Z1)[1:]
        + [vmem(12, 16, LANES), vmem(12, Z1, LANES)],
        smem=1,
    )(place, top, s1, *narrow, window)


def solution(mesh):
    names, dims = list(mesh.axis_names), list(mesh.devices.shape)
    at = names.index("gx")
    fine = jax.sharding.Mesh(
        mesh.devices.reshape(dims[:at] + [dims[at] // 2, 2] + dims[at + 1 :]),
        names[:at] + ["xc", "co"] + names[at + 1 :],
    )
    placed = P(("xc", "co"), "gz", "gy")
    return jax.shard_map(
        functools.partial(on_device, dict(fine.shape)),
        mesh=fine,
        in_specs=(placed, placed),
        out_specs=(placed, placed),
        check_vma=False,
    )
```

```python
import functools

import jax
import jax.numpy as jnp
from jax import lax
from jax.experimental import pallas as pl
from jax.experimental.pallas import tpu as pltpu
from jax.sharding import PartitionSpec as P

NU = 2
BOTTOM = 8
F32 = jnp.float32
LANES = 128
STRIP = 8

HD, XD, ZD = 14, 44, 48
NEAR = 5
H0, X0, Z0 = 5, 26, 32
HALF = LANES // 2
H1, X1, Z1 = 7, 22, 24


def roll(v, shift, axis):
    return pltpu.roll(v, shift % v.shape[axis], axis)


def iota(shape, axis):
    return lax.broadcasted_iota(jnp.int32, shape, axis)


def reds(shape, parity):
    return ((iota(shape, 0) + iota(shape, 1)) & 1) == parity % 2


def couplings(s_ref, f_ref, c_ref, g_ref, w_ref, first, last, scale, so=0, edges=False, step=1, lanes=1):
    shape = s_ref.shape[1:]
    if edges:
        z = iota(shape, 0)
        walls = (None, None, z == shape[0] - 1, z == 0, None, None)

    def chunk(x, n):
        s = [s_ref[x + so + k] for k in range(-1, n + 1)]
        for k in range(n):
            centre = s[k + 1]
            near = [
                s[k + 2],
                s[k],
                roll(centre, -1, 0),
                roll(centre, 1, 0),
                roll(centre, -lanes, 1),
                roll(centre, lanes, 1),
            ]
            if edges:
                near = [v if wall is None else jnp.where(wall, 0.0, v) for v, wall in zip(near, walls)]
            betas = [centre + v for v in near]
            total = ((betas[0] + betas[1]) + (betas[2] + betas[3])) + (betas[4] + betas[5])
            inverse = jnp.where(centre > 0.0, 1.0 / total, 0.0)
            for d in range(6):
                c = betas[d] * inverse
                if edges and walls[d] is not None:
                    c = jnp.where(walls[d], 0.0, c)
                c_ref[d, x + k] = c
            g_ref[x + k] = f_ref[x + k] * (inverse * (2.0 * scale))
            w_ref[x + k] = total * (0.5 / scale)

    stepped(chunk, first, last, step)


def stepped(chunk, first, last, step):
    count, rest = divmod(last - first, step)
    if count == 1:
        chunk(first, step)
    elif count:

        def body(i, carry):
            chunk(first + i * step, step)
            return carry

        lax.fori_loop(0, count, body, 0)
    if rest:
        chunk(last - rest, rest)


def relaxed(u, c_ref, g_ref, x, lanes=1):
    low, centre, high = u
    a = c_ref[0, x] * high + c_ref[1, x] * low
    b = c_ref[2, x] * roll(centre, -1, 0) + c_ref[3, x] * roll(centre, 1, 0)
    d = c_ref[4, x] * roll(centre, -lanes, 1) + c_ref[5, x] * roll(centre, lanes, 1)
    return g_ref[x] + ((a + b) + d)


def half_sweep(u_ref, c_ref, g_ref, first, last, parity, uo=0, step=4):
    shape = u_ref.shape[1:]
    masks = (reds(shape, parity + first), reds(shape, parity + first + 1))

    def chunk(x, n):
        u = [u_ref[x + uo + k] for k in range(-1, n + 1)]
        new = [jnp.where(masks[k % 2], relaxed(u[k : k + 3], c_ref, g_ref, x + k), u[k + 1]) for k in range(n)]
        for k in range(n):
            u_ref[x + uo + k] = new[k]

    stepped(chunk, first, last, step)


def first_half_sweep(u_ref, g_ref, first, last, parity, uo=0, step=4):
    shape = u_ref.shape[1:]
    masks = (reds(shape, parity + first), reds(shape, parity + first + 1))

    def chunk(x, n):
        for k in range(n):
            u_ref[x + uo + k] = jnp.where(masks[k % 2], g_ref[x + k], 0.0)

    stepped(chunk, first, last, step)


def residual_planes(u_ref, c_ref, g_ref, w_ref, x, n, uo=0):
    u = [u_ref[x + uo + k] for k in range(-1, n + 1)]
    return [w_ref[x + k] * (relaxed(u[k : k + 3], c_ref, g_ref, x + k) - u[k + 1]) for k in range(n)]


def phases(shape, parity):
    return (iota(shape, 0) & 1) == parity % 2


def beside(planes, below):
    out = []
    for a, b in zip(planes[0::2], planes[1::2]):
        lower = roll(jnp.where(below, a, b), 1, 1)
        upper = roll(jnp.where(below, b, a), -1, 1)
        out += [jnp.where(below, lower, upper), jnp.where(below, upper, lower)]
    return out


def couplings_rb(s, f, c, g, w, first, last, scale, parity, step, so=0, edges=False):
    shape = s.shape[2:]
    masks = (phases(shape, parity), phases(shape, parity + 1))
    z, j = iota(shape, 0), iota(shape, 1) & (HALF - 1)
    walls = [None] * 5
    if edges:
        walls = [None, None, z == shape[0] - 1, z == 0, None]
        ends = [j == jnp.where(m, 0, HALF - 1) for m in masks]

    def chunk(x, n):
        for col in range(2):
            others = [s[1 - col, x + k + so] for k in range(n)]
            others = list(zip(others, beside(others, masks[(first + col) % 2])))
            for k in range(n):
                m = (first + k + col) % 2
                centre = s[col, x + k + so]
                v, second = others[k]
                near = [
                    s[1 - col, x + k + so + 1],
                    s[1 - col, x + k + so - 1],
                    roll(v, -1, 0),
                    roll(v, 1, 0),
                    v,
                    second,
                ]
                wall = walls + [ends[m] if edges else None]
                near = [v if e is None else jnp.where(e, 0.0, v) for v, e in zip(near, wall)]
                betas = [centre + v for v in near]
                total = ((betas[0] + betas[1]) + (betas[2] + betas[3])) + (betas[4] + betas[5])
                inverse = jnp.where(centre > 0.0, 1.0 / total, 0.0)
                for d in range(6):
                    v = betas[d] * inverse
                    c[col, d, x + k] = v if wall[d] is None else jnp.where(wall[d], 0.0, v)
                g[col, x + k] = f[col, x + k] * (inverse * (2.0 * scale))
                w[col, x + k] = total * (0.5 / scale)

    stepped(chunk, first, last, step)


def relaxed_rb(v, second, c, g, col, x):
    low, centre, high = v
    a = c[col, 0, x] * high + c[col, 1, x] * low
    b = c[col, 2, x] * roll(centre, -1, 0) + c[col, 3, x] * roll(centre, 1, 0)
    d = c[col, 4, x] * centre + c[col, 5, x] * second
    return g[col, x] + ((a + b) + d)


def half_sweep_rb(u_ref, v_ref, c, g, col, first, last, parity, step, uo=0):
    mask = phases(v_ref.shape[1:], parity + first + col)

    def chunk(x, n):
        v = [v_ref[x + k + uo] for k in range(-1, n + 1)]
        seconds = beside(v[1:-1], mask)
        for k in range(n):
            u_ref[x + k + uo] = relaxed_rb(v[k : k + 3], seconds[k], c, g, col, x + k)

    stepped(chunk, first, last, step)


def residuals_rb(u, c, g, w, first, x, n, parity, uo=0):
    out = []
    for col in range(2):
        v = [u[1 - col, x + k + uo] for k in range(-1, n + 1)]
        seconds = beside(v[1:-1], phases(u.shape[2:], parity + first + col))
        new = [relaxed_rb(v[k : k + 3], seconds[k], c, g, col, x + k) for k in range(n)]
        out.append([w[col, x + k] * (new[k] - u[col, x + k + uo]) for k in range(n)])
    return out


def picked(v, matrix):
    matrix = matrix.astype(jnp.bfloat16)
    first = v.astype(jnp.bfloat16)
    rest = v - first.astype(F32)
    second = rest.astype(jnp.bfloat16)
    third = (rest - second.astype(F32)).astype(jnp.bfloat16)
    parts = [jnp.dot(x, matrix, preferred_element_type=F32) for x in (first, second, third)]
    return (parts[0] + parts[1]) + parts[2]


def permuted(v, back):
    k, l = iota((LANES, LANES), 0), iota((LANES, LANES), 1)
    if back:
        k, l = l, k
    return picked(v, jnp.where(k == jnp.where(l < HALF, 2 * l, 2 * (l - HALF) + 1), 1.0, 0.0))


def swapped_rows(v, parity):
    return jnp.where(phases(v.shape, parity), v, roll(v, HALF, 1))


def packed(planes, at, group):
    rows = planes[0].shape[0]
    groups = iota((rows, LANES), 1) >> 3
    out = jnp.zeros((rows, LANES), F32)
    for k, v in enumerate(planes):
        out = jnp.where(groups == group(k), roll(v, STRIP * group(k) - at, 1), out)
    return out


def high_group(k):
    return 2 * k


def low_group(k):
    return (2 * k + 7) % 16


def fill_rb(out, i, at, planes_ref, strips, k0, count, rows, step=8):
    number = rows.stop - rows.start
    lane = iota((number, LANES), 1)
    own = lane < HALF
    halo = jnp.logical_or(lane < HALF + STRIP, lane >= LANES - STRIP)

    def chunk(n, many):
        for m in range(many):
            v = planes_ref[n + m]
            shift = lax.rem(HALF + LANES - 2 * STRIP * lax.rem(n + m + k0, 8), LANES)
            for col in range(2):
                h = jnp.where(halo, pltpu.roll(strips(2 * i + col), shift, 1), 0.0)
                out[col, at + n + m, rows.start : rows.stop] = jnp.where(own, roll(v, HALF, 1) if col else v, h)
                if number < ZD:
                    out[col, at + n + m, : rows.start] = jnp.zeros((rows.start, LANES), F32)
                    out[col, at + n + m, rows.stop :] = jnp.zeros((ZD - rows.stop, LANES), F32)

    def body(n, carry):
        chunk(n * step, step)
        return carry

    lax.fori_loop(0, count // step, body, 0)
    if count % step:
        chunk(jnp.int32(count - count % step), count % step)


def fill_narrow(u, f, even, own, first, second):
    lane = iota((Z1, LANES), 1)
    for parts, at, count in (((second, first), 0, H1), ((own, own), H1, 8), ((first, second), H1 + 8, H1)):
        for k in range(count):
            v, h = [parts[0][i, k] if count == 8 else jnp.where(even, parts[0][i, k], parts[1][i, k]) for i in range(2)]
            u[at + k] = jnp.where(lane < HALF, v, roll(h, HALF, 1))
            f[at + k] = jnp.where(lane < HALF, roll(v, HALF, 1), h)


def call(kernel, out_shape, scratch, smem=0, cost=4):
    def run(*args):
        specs = [pl.BlockSpec(memory_space=pltpu.SMEM)] * smem
        specs += [pl.BlockSpec(memory_space=pltpu.VMEM)] * (len(args) - smem)
        return pl.pallas_call(
            kernel,
            out_shape=out_shape,
            in_specs=specs,
            out_specs=jax.tree.map(lambda _: pl.BlockSpec(memory_space=pltpu.VMEM), out_shape),
            scratch_shapes=scratch,
            compiler_params=pltpu.CompilerParams(vmem_limit_bytes=40 * 2**20),
            cost_estimate=pl.CostEstimate(flops=cost * 10**6, bytes_accessed=cost * 3 * 10**6, transcendentals=0),
        )(*args)

    return run


def vmem(*shape):
    return pltpu.VMEM(shape, F32)


def packing(in_ref, out_ref, lo_ref, hi_ref):
    for i in range(2):
        out_ref[i] = permuted(in_ref[i].reshape(256, LANES), False).reshape(16, 16, LANES)
        planes = [swapped_rows(out_ref[i, x], x) for x in range(16)]
        for x in range(16):
            out_ref[i, x] = planes[x]
        for col in range(2):
            for q in range(2):
                some = planes[8 * q : 8 * q + 8]
                lo_ref[2 * i + col, q] = packed(some, HALF * col, high_group)
                hi_ref[2 * i + col, q] = packed(some, HALF * col + HALF - STRIP, low_group)


def descend(e, b, lsn, lsf, lfn, lff, lb0, lb1, hsn, hsf, hfn, hff, hb0, hb1, top_out, s1_out, next_out, tile_out, s, f, c, g, w, u, q, fl, cl, gl, wl, ul, ql, t):
    every, some = slice(0, ZD), slice(8, ZD - 8)
    for i, out, ln, lf, hn, hf, near, deep in ((0, f, lfn, lff, hfn, hff, 3, 12), (1, s, lsn, lsf, hsn, hsf, NEAR, HD)):
        first = 16 - deep
        fill_rb(out, i, HD - deep, lf, lambda n: lb0[n], first, 8 - first, some)
        fill_rb(out, i, HD - 8, lf.at[8 - first :], lambda n: lb1[n, 8 : ZD - 8], 8, 8 - near, some)
        fill_rb(out, i, HD - near, ln, lambda n: lb1[n], 16 - near, near, every)
        for h in range(2):
            fill_rb(out, i, HD + 8 * h, e.at[i, 8 * h : 8 * h + 8], lambda n, h=h: b[n, h], 8 * h, 8, every)
        fill_rb(out, i, HD + 16, hn, lambda n: hb0[n], 0, near, every)
        fill_rb(out, i, HD + 16 + near, hf, lambda n: hb0[n, 8 : ZD - 8], near, 8 - near, some)
        fill_rb(out, i, HD + 24, hf.at[8 - near :], lambda n: hb1[n], 8, deep - 8, some)
    couplings_rb(s, f, c, g, w, 2, XD - 2, 1.0, 0, 4)
    red, black = u.at[0], u.at[1]
    half_sweep_rb(black, g.at[0], c, g, 1, 3, XD - 3, 0, 10)
    half_sweep_rb(red, black, c, g, 0, 4, XD - 4, 0, 12)
    half_sweep_rb(black, red, c, g, 1, 5, XD - 5, 0, 12)

    def residual_body(i, carry):
        r = residuals_rb(u, c, g, w, 6, 6 + 16 * i, 16, 0)
        for k in range(8):
            both = (r[0][2 * k] + r[0][2 * k + 1]) + (r[1][2 * k] + r[1][2 * k + 1])
            q[0, 8 * i + k + 3, 8 : ZD - 8] = both[8 : ZD - 8]
            q[0, 8 * i + k + 3, :8] = q[0, 8 * i + k + 3, ZD - 8 :] = jnp.zeros((8, LANES), F32)
        return carry

    lax.fori_loop(0, 2, residual_body, 0)
    nothing = jnp.zeros((ZD, LANES), F32)
    for i in (0, 1, 2, 19, 20, 21):
        q[0, i] = nothing

    def coefficients(x, n):
        for i in range(n):
            a, b = 2 * (x + i), 2 * (x + i) + 1
            q[1, x + i] = (s[0, a] + s[0, b]) + (s[1, a] + s[1, b])

    stepped(coefficients, 0, X1, 11)
    sl = s1_out
    for i, ref in enumerate((fl, sl)):
        ref[...] = 0.125 * (q[i, :, pl.ds(0, Z1, stride=2), :] + q[i, :, pl.ds(1, Z1, stride=2), :])

    def keep(x, n):
        for i in range(n):
            for col in range(2):
                top_out[col, x + i] = s[col, HD - H0 + x + i, 8 : ZD - 8]
                top_out[2 + col, x + i] = f[col, HD - H0 + x + i, 8 : ZD - 8]
            top_out[4, x + i] = black[HD - H0 + x + i, 8 : ZD - 8]

    stepped(keep, 0, X0, 13)
    couplings(sl, fl, cl, gl, wl, 3, X1 - 3, 4.0, step=8)
    first_half_sweep(ul, gl, 3, X1 - 3, H1, step=8)
    half_sweep(ul, cl, gl, 4, X1 - 4, H1 + 1, step=8)
    half_sweep(ul, cl, gl, 5, X1 - 5, H1, step=12)
    half_sweep(ul, cl, gl, 6, X1 - 6, H1 + 1, step=10)
    r = residual_planes(ul, cl, gl, wl, H1, 8)
    own = iota((8, LANES), 1) < HALF
    for x in range(8):
        next_out[x] = jnp.where(own, ul[H1 + x, 8:16], roll(fl[H1 + x, 8:16], HALF, 1))
    for i in range(4):
        x = H1 + 2 * i
        ql[i, 0] = (r[2 * i] + r[2 * i + 1])[8:16]
        ql[i, 1] = sl[x, 8:16] + sl[x + 1, 8:16]
        for b in range(2):
            t[i, 4 * b : 4 * b + 4] = ql[i, b, pl.ds(0, 4, stride=2), :] + ql[i, b, pl.ds(1, 4, stride=2), :]
    k, l = iota((4 * LANES, LANES), 0), iota((4 * LANES, LANES), 1)
    cell = (k & (LANES - 1)) >> 1
    to = 32 * (k >> 7) + 16 * (cell & 1) + (cell >> 1)
    place = jnp.where(jnp.logical_and((k & HALF) == 0, l == to), 0.125, 0.0)
    total = picked(jnp.concatenate([t[i] for i in range(4)], 1), place)
    group = iota((8, LANES), 1) // 16
    other = jnp.where(group % 2 == 0, roll(total, -16, 1), roll(total, 16, 1))
    tile_out[...] = jnp.where((group // 2 + iota((8, LANES), 0)) % 2 == 0, total, other)


def coarse(where_ref, mine_ref, other_ref, out_ref, s2, f2, c2, g2, w2, u2, q2, d2, s3, f3, c3, g3, w3, u3, q3, d3, s4, f4, c4, g4, w4):
    lane = iota((8, LANES), 1)
    wide = iota((32, LANES), 1)
    zero2 = jnp.zeros((32, LANES), F32)
    core, chip = lax.rem(where_ref[0], 2), where_ref[0] // 2

    def transposed(groups):
        for s in (1, 2, 4):
            upper = (lane & (16 * s)) != 0
            for tiles in groups:
                for m in range(8):
                    if not m & s:
                        a, b = tiles[m], tiles[m + s]
                        tiles[m] = jnp.where(upper, roll(b, 16 * s, 1), a)
                        tiles[m + s] = jnp.where(upper, b, roll(a, -16 * s, 1))
        return groups

    def assemble(xcl, carry):
        for all_ref, c in ((mine_ref, core), (other_ref, 1 - core)):
            plane = 4 * (2 * xcl + c)
            groups = []
            for zi in range(8):
                at = [(lax.bitwise_xor(2 * xh + xcl, chip) * 4 + iy) * 8 + zi for xh in range(2) for iy in range(4)]
                groups.append([all_ref[i] for i in at])
            for zi, tiles in enumerate(transposed(groups)):
                rows = slice(8 * (zi // 2), 8 * (zi // 2) + 8)
                for g, v in enumerate(tiles):
                    if zi % 2 == 0:
                        f2[g % 2, plane + g // 2, rows] = v
                    else:
                        s2[g % 2, plane + g // 2 + 1, rows] = v
        return carry

    lax.fori_loop(0, 2, assemble, 0)

    def wrap(ref):
        ref[0] = jnp.where(wide < HALF, 0.0, roll(ref[16], HALF, 1))
        ref[17] = jnp.where(wide < HALF, roll(ref[1], HALF, 1), 0.0)

    for col in range(2):
        wrap(s2.at[col])
    for x in (0, 17):
        s3[x] = zero2[:16]
        u3[x] = zero2[:16]
    for x in (0, 9):
        s4[x] = zero2[:8]

    red, black = u2.at[0], u2.at[1]

    def sweep2(col):
        half_sweep_rb(u2.at[col], u2.at[1 - col], c2, g2, col, 0, 16, 0, 16, 1)
        wrap(u2.at[col])

    couplings_rb(s2, f2, c2, g2, w2, 0, 16, 16.0, 0, 4, 1, True)
    for x in range(16):
        red[x + 1] = g2[0, x]
    wrap(red)
    sweep2(1)
    sweep2(0)
    sweep2(1)

    def restrict2(i, carry):
        r = residuals_rb(u2, c2, g2, w2, 0, 8 * i, 8, 0, 1)
        for k in range(4):
            x = 8 * i + 2 * k + 1
            q2[0, 4 * i + k] = (r[0][2 * k] + r[0][2 * k + 1]) + (r[1][2 * k] + r[1][2 * k + 1])
            q2[1, 4 * i + k] = (s2[0, x] + s2[0, x + 1]) + (s2[1, x] + s2[1, x + 1])
        return carry

    lax.fori_loop(0, 2, restrict2, 0)
    narrow = iota((16, LANES), 1) < HALF
    for i, ref, at in ((0, f3, 0), (1, s3, 1)):
        for x in range(8):
            v = 0.125 * (q2[i, x, pl.ds(0, 16, stride=2), :] + q2[i, x, pl.ds(1, 16, stride=2), :])
            ref[x + at] = jnp.where(narrow, v, 0.0)
            ref[x + at + 8] = jnp.where(narrow, roll(v, HALF, 1), 0.0)
    couplings(s3, f3, c3, g3, w3, 0, 16, 64.0, so=1, edges=True, step=8)
    first_half_sweep(u3, g3, 0, 16, 0, 1, 16)
    for col in (1, 0, 1):
        half_sweep(u3, c3, g3, 0, 16, col, 1, 16)
    r = residual_planes(u3, c3, g3, w3, 0, 16, 1)
    for i in range(8):
        q3[0, i] = r[2 * i] + r[2 * i + 1]
        q3[1, i] = s3[2 * i + 1] + s3[2 * i + 2]
    lane4 = iota((8, LANES), 1)
    for i, ref, at in ((0, f4, 0), (1, s4, 1)):
        for x in range(8):
            v = 0.125 * (q3[i, x, pl.ds(0, 8, stride=2), :] + q3[i, x, pl.ds(1, 8, stride=2), :])
            ref[x + at] = jnp.where((lane4 & 1) == 0, v + roll(v, -1, 1), 0.0)
    couplings(s4, f4, c4, g4, w4, 0, 8, 256.0, so=1, edges=True, step=8, lanes=2)
    odd = (iota((8, LANES), 0) + (lane4 >> 1)) & 1
    masks = (odd == 0, odd == 1)
    nothing = jnp.zeros((8, LANES), F32)
    u4 = [jnp.where(masks[x % 2], g4[x], 0.0) for x in range(8)]
    for h in range(1, 2 * BOTTOM):
        around = [nothing] + u4 + [nothing]
        u4 = [jnp.where(masks[(x + h) % 2], relaxed(around[x : x + 3], c4, g4, x, 2), u4[x]) for x in range(8)]
    for x in range(8):
        v = u4[x] + roll(u4[x], 1, 1)
        d3[x, pl.ds(0, 8, stride=2), :] = v
        d3[x, pl.ds(1, 8, stride=2), :] = v
    for x in range(16):
        u3[x + 1] = u3[x + 1] + d3[x // 2]
    for col in (0, 1) * NU:
        half_sweep(u3, c3, g3, 0, 16, col, 1, 16)
    for x in range(8):
        v = jnp.where(narrow, u3[x + 1], roll(u3[x + 9], HALF, 1))
        d2[x, pl.ds(0, 16, stride=2), :] = v
        d2[x, pl.ds(1, 16, stride=2), :] = v
    for x in range(16):
        black[x + 1] = black[x + 1] + d2[x // 2]
    wrap(black)
    for _ in range(NU):
        sweep2(0)
        sweep2(1)
    ix, iy, iz = where_ref[0], where_ref[1], where_ref[2]
    down_z = lax.rem(36 - 4 * iz, 32)
    for n in range(12):
        x = 4 * ix + 12 + n
        at = lax.rem(x, 16) + 1
        shift = lax.rem(4 * LANES - HALF * (x // 16) - 16 * iy + HALF, LANES)
        for col in range(2):
            v = pltpu.roll(u2[col, at], down_z, 0)
            out_ref[col, n] = pltpu.roll(v[:16], shift, 1)


def ascend(where_ref, top, sl, m, ma, mb, win, u_out, r_out, c, g, w, u, d0, fl, cl, gl, wl, ul, t1, d1):
    fill_narrow(ul, fl, lax.rem(where_ref[0], 2) == 0, m, ma, mb)
    couplings(sl, fl, cl, gl, wl, 1, X1 - 1, 4.0, step=20)
    k, l = iota((2 * LANES, LANES), 0), iota((2 * LANES, LANES), 1)
    from_lane = jnp.where(l < 96, l >> 2, 96 + (l >> 2))
    widen = jnp.where(k == from_lane + LANES * ((l >> 1) & 1), 1.0, 0.0)
    parity = iota((1, 16, LANES), 1) + iota((12, 16, LANES), 0)
    v = [win[0], win[1]]
    both = [jnp.where((parity & 1) == 0, v[i], v[1 - i]).reshape(192, LANES) for i in range(2)]
    t1[...] = picked(jnp.concatenate(both, 1), widen).reshape(12, 16, LANES)
    d1[:, pl.ds(0, 12, stride=2), :] = t1[:, :12]
    d1[:, pl.ds(1, 12, stride=2), :] = t1[:, :12]
    for x in range(X1):
        ul[x] = jnp.where(sl[x] > 0.0, ul[x] + d1[(x + 1) // 2], 0.0)
    half_sweep(ul, cl, gl, 1, X1 - 1, H1, step=10)
    half_sweep(ul, cl, gl, 2, X1 - 2, H1 + 1, step=18)
    half_sweep(ul, cl, gl, 3, X1 - 3, H1, step=16)
    half_sweep(ul, cl, gl, 4, X1 - 4, H1 + 1, step=14)
    s, f, black, red = top.at[0:2], top.at[2:4], u.at[1], u.at[0]
    couplings_rb(s, f, c, g, w, 1, X0 - 1, 1.0, 1, 4)
    fine = ul[4:18, 4:20]
    d0[:, pl.ds(0, 16, stride=2), :] = fine
    d0[:, pl.ds(1, 16, stride=2), :] = fine
    for x in range(X0):
        black[x] = jnp.where(top[1, x] > 0.0, top[4, x] + d0[(x + 1) // 2], 0.0)
    half_sweep_rb(red, black, c, g, 0, 1, X0 - 1, 1, 12)
    half_sweep_rb(black, red, c, g, 1, 2, X0 - 2, 1, 12)
    half_sweep_rb(red, black, c, g, 0, 3, X0 - 3, 1, 10)
    half_sweep_rb(black, red, c, g, 1, 4, X0 - 4, 1, 18)

    lane = iota((16, LANES), 1)

    def body(i, carry):
        x = H0 + 8 * i
        r = residuals_rb(u, c, g, w, H0, x, 8, 1)
        for j in range(8):
            for out, a, b in ((u_out, u[0, x + j], u[1, x + j]), (r_out, r[0][j], r[1][j])):
                both = jnp.where(lane < HALF, a[8:24], roll(b[8:24], HALF, 1))
                out[8 * i + j] = swapped_rows(both, j)
        return carry

    lax.fori_loop(0, 2, body, 0)
    for out in (u_out, r_out):
        out[...] = permuted(out[...].reshape(256, LANES), True).reshape(16, 16, LANES)


def axis_of(name):
    return ("xc", "co") if name == "gx" else name


def exchange(low, high, name):
    axis = axis_of(name)
    count = lax.axis_size(axis)
    even = lax.axis_index(axis) % 2 == 0
    first = [(i, i ^ 1) for i in range(count)]
    second = [(i, i + 1) for i in range(1, count - 1, 2)]
    second += [(j, i) for i, j in second]
    b = lax.ppermute(jnp.where(even, low, high), axis, second)
    a = lax.ppermute(jnp.where(even, high, low), axis, first)
    return a, b


def swap(low, high, name):
    even = lax.axis_index(axis_of(name)) % 2 == 0
    a, b = exchange(low, high, name)
    return jnp.where(even, b, a), jnp.where(even, a, b)


def join(pieces):
    return jnp.concatenate([p.reshape(-1, 8, LANES) for p in pieces], 0)


def split(joined, like):
    out, at = [], 0
    for p in like:
        n = p.size // (8 * LANES)
        out.append(joined[at : at + n].reshape(p.shape))
        at += n
    return out


def swap_many(lows, highs, axis):
    low, high = swap(join(lows), join(highs), axis)
    return split(low, lows), split(high, highs)


def extend_wide(field, lo, hi):
    below, above = swap(lo, hi, "gy")
    group = lax.broadcasted_iota(jnp.int32, lo.shape, 3) // STRIP
    strips = jnp.where(group % 2 == 0, above, below)
    pieces = [field, strips]
    lows, highs = swap_many(pieces, pieces, "gz")
    field, strips = [jnp.concatenate(v, v[0].ndim - 2) for v in zip(lows, pieces, highs)]
    some = slice(8, ZD - 8)
    f, s = field[0], field[1]
    first = [s[:NEAR], s[NEAR:HD, some], f[:3], f[3:12, some], strips[:, 0], strips[:, 1, some]]
    last = [s[-NEAR:], s[-HD:-NEAR, some], f[-3:], f[-12:-3, some], strips[:, 0, some], strips[:, 1]]
    low, high = swap(join(first), join(last), "gx")
    return [field, strips] + split(low, last) + split(high, first)


def extend_narrow(own):
    below, above = swap(own, own, "gy")
    lane = lax.broadcasted_iota(jnp.int32, own.shape, 2)
    own = jnp.stack([own, jnp.where(lane % HALF < HALF // 2, above, below)])
    low, high = swap(own, own, "gz")
    own = jnp.concatenate([low, own, high], 2)
    return (own,) + exchange(own[:, :H1], own[:, -H1:], "gx")


def spread(x, axes, sizes):
    n = 1
    for a in axes:
        n *= sizes[a]
    return lax.all_to_all(jnp.broadcast_to(x[None], (n,) + x.shape), axes, 0, 0)


def level_scratch(planes, rows):
    p = (planes, rows, LANES)
    return [vmem(*p), vmem(*p), vmem(6, *p), vmem(*p), vmem(*p), vmem(*p)]


def rb_scratch(planes, rows, count):
    p = (planes, rows, LANES)
    return ([vmem(2, *p)] * 6)[: count - 4] + [vmem(2, 6, *p)] + [vmem(2, *p)] * 3


def full_scratch(n, uo):
    p = (n, LANES)
    return [vmem(n + 2, *p), vmem(n, *p), vmem(6, n, *p), vmem(n, *p), vmem(n, *p), vmem(n + 2 * uo, *p)]


def shape(*dims):
    return jax.ShapeDtypeStruct(dims, F32)


def on_device(sizes, right_side, sigma):
    field, lo, hi = call(packing, [shape(2, 16, 16, LANES), shape(4, 2, 16, LANES), shape(4, 2, 16, LANES)], [])(jnp.stack([right_side, sigma]))
    top, s1, next1, tile = call(
        descend,
        [shape(5, X0, Z0, LANES), shape(X1, Z1, LANES), shape(8, 8, LANES), shape(8, LANES)],
        rb_scratch(XD, ZD, 6)
        + [vmem(2, X1, ZD, LANES)]
        + level_scratch(X1, Z1)[1:]
        + [vmem(4, 2, 8, LANES), vmem(4, 8, LANES)],
    )(*extend_wide(field, lo, hi))
    narrow = extend_narrow(next1)
    line = spread(tile, ("gy", "gz"), sizes)
    line = line.reshape(-1, 4, 2, 2, 4, LANES).transpose(0, 1, 3, 2, 4, 5).reshape(-1, 8, LANES)
    chips = sizes["xc"]
    mine = [line] + [lax.ppermute(line, "xc", [(i, i ^ k) for i in range(chips)]) for k in range(1, chips)]
    mine = jnp.concatenate(mine)
    other = lax.ppermute(mine, "co", [(0, 1), (1, 0)])
    place = jnp.stack([lax.axis_index(axis_of("gx")), lax.axis_index("gy"), lax.axis_index("gz")]).astype(jnp.int32)
    window = call(
        coarse,
        shape(2, 12, 16, LANES),
        [vmem(2, 18, 32, LANES)]
        + rb_scratch(16, 32, 5)[:-1]
        + [vmem(2, 18, 32, LANES), vmem(2, 8, 32, LANES), vmem(8, 32, LANES)]
        + full_scratch(16, 1)
        + [vmem(2, 8, 16, LANES), vmem(8, 16, LANES)]
        + full_scratch(8, 1)[:-1],
        smem=1,
        cost=10,
    )(place, mine, other)
    return call(
        ascend,
        (shape(16, 16, LANES), shape(16, 16, LANES)),
        rb_scratch(X0, Z0, 4)
        + [vmem(14, Z0, LANES)]
        + level_scratch(X1, Z1)[1:]
        + [vmem(12, 16, LANES), vmem(12, Z1, LANES)],
        smem=1,
    )(place, top, s1, *narrow, window)


def solution(mesh):
    names, dims = list(mesh.axis_names), list(mesh.devices.shape)
    at = names.index("gx")
    fine = jax.sharding.Mesh(
        mesh.devices.reshape(dims[:at] + [dims[at] // 2, 2] + dims[at + 1 :]),
        names[:at] + ["xc", "co"] + names[at + 1 :],
    )
    placed = P(("xc", "co"), "gz", "gy")
    return jax.shard_map(
        functools.partial(on_device, dict(fine.shape)),
        mesh=fine,
        in_specs=(placed, placed),
        out_specs=(placed, placed),
        check_vma=False,
    )
```
